256 devices in a mesh: crop: 2 (over y_hi), dap: 128 (over y_lo, z, x, core).
Axes of the slice: x: 4, y: 4 (y_hi: 2, y_lo: 2; y = y_hi * 2 + y_lo), z: 8, core: 2. Of those that a mesh axis runs over, the one named last changes fastest.
Arguments:
- multiple_sequence_matrix: bfloat16 [128, 1024, 256], P('dap', 'crop'), parts along dimension 1, may hold values from -40 to 40
- layer_stretch: float32 [256], replicated, may hold values from 0.1 to 1.9
- layer_shift: float32 [256], replicated, may hold values from -3 to 3
- left_right_matrix: bfloat16 [256, 64], replicated, may hold values from -0.375 to 0.375
- mapping_offset: float32 [64], replicated, may hold values from -3 to 3
- final_projection_matrix: bfloat16 [1024, 128], replicated, may hold values from -2 to 2
- final_offset_vector: float32 [128], replicated, may hold values from -3 to 3
- couplet_adjoint: bfloat16 [512, 1024, 128], P('dap', 'crop'), parts along dimension 1, may hold values from -3 to 3
Outputs:
- pair_delta: bfloat16 [512, 1024, 128], P('dap', 'crop'), parts along dimension 1
- alignment_gradient: bfloat16 [128, 1024, 256], P('dap', 'crop'), parts along dimension 1
- proj_grad: float32 [512, 64], P('crop'), parts along dimension 0
- w_out_grad: float32 [2048, 128], P('crop'), parts along dimension 0
The draws below stay inside these ranges and needn't reach their ends.
There are 2 independent parts, one for each index of `crop`. The reference program is written for one: setup_inputs(seed, part) draws one part's arguments, and reference() takes and returns one part's arrays. A program takes and returns all parts, laid end to end along the dimension named above; an argument that names none is the same for every part. Nothing has to cross between parts.
All inputs are finite; a program needn't handle non-finite values.
Results may differ from the reference program's by a relative error of at most 0.0069.
Values may be sent and summed in bfloat16 or wider, within the bound.
A program may use at most 64 MiB of HBM per device.

```python
import math
import jax
import jax.numpy as jnp
from jax import lax

CM = 256
CH = 32
CZ = 128
SEQUENCE_ROWS = 128
RESIDUE_COUNT = 512


def draw_multiple_sequence_matrix(key, part):
    key = jax.random.fold_in(key, 11)
    first, second, third = jax.random.split(key, 3)
    array_shape = (SEQUENCE_ROWS, RESIDUE_COUNT, CM)
    base = jnp.clip(jax.random.normal(first, array_shape, jnp.float32), -4.0, 4.0)
    row_scale = jnp.exp(jax.random.uniform(second, (SEQUENCE_ROWS, RESIDUE_COUNT, 1), jnp.float32, math.log(0.3), math.log(3.0)))
    column_scale = jnp.exp(jax.random.uniform(third, (1, 1, CM), jnp.float32, math.log(0.5), math.log(2.0)))
    return (base * row_scale * column_scale).astype(jnp.bfloat16)


def block_levels(own_key, extent, cuts, low, largest):
    loudness, own = 1.0, jax.random.fold_in(own_key, 6)
    for axis_at, shards_of in cuts:
        steps = jnp.exp(jax.random.uniform(jax.random.fold_in(own, axis_at), (shards_of,), jnp.float32, low / len(cuts), largest / len(cuts)))
        loudness = loudness * jnp.repeat(steps, extent[axis_at] // shards_of).reshape([-1 if axis == axis_at else 1 for axis in range(len(extent))])
    return loudness


def bell_draw(key, extent, scale, bound, cuts=(), held_as=jnp.bfloat16):
    entries = jax.random.normal(key, extent, jnp.float32) * scale
    if len(cuts) > 0:
        entries = block_levels(key, extent, cuts, -0.22, 0.18) * entries
    return jnp.clip(entries, min=-bound, max=bound).astype(held_as)


def setup_inputs(seed: int = 0, part: int = 0) -> dict:
    streams_of = jax.random.split(jax.random.key(seed), 9)
    part_keys = jax.random.split(jax.random.fold_in(streams_of[8], part), 9)
    return {
        "multiple_sequence_matrix": draw_multiple_sequence_matrix(jax.random.fold_in(jax.random.fold_in(streams_of[8], part), 71), part),
        "layer_stretch": jnp.clip(1.0 + 0.18 * jax.random.normal(streams_of[1], (CM,), jnp.float32), 0.1, 1.9),
        "layer_shift": bell_draw(streams_of[2], (CM,), 0.5, 3.0, (), jnp.float32),
        "left_right_matrix": bell_draw(streams_of[3], (CM, 2 * CH), CM ** -0.5, 0.375),
        "mapping_offset": bell_draw(streams_of[4], (2 * CH,), 0.5, 3.0, (), jnp.float32),
        "final_projection_matrix": bell_draw(streams_of[5], (CH * CH, CZ), (CH * CH // SEQUENCE_ROWS) ** -0.5, 2.0),
        "final_offset_vector": bell_draw(streams_of[6], (CZ,), 0.5, 3.0, (), jnp.float32),
        "couplet_adjoint": bell_draw(part_keys[7], (RESIDUE_COUNT, RESIDUE_COUNT, CZ), 0.5, 3.0, ((0, 128),)),
    }


def reference(multiple_sequence_matrix, layer_stretch, layer_shift, left_right_matrix, mapping_offset, final_projection_matrix, final_offset_vector, couplet_adjoint):
    entry_label = multiple_sequence_matrix.astype(jnp.float32)
    average = lax.optimization_barrier(jnp.mean(entry_label, axis=-1, keepdims=True))
    centred = entry_label - average
    inverse_deviation = lax.rsqrt(lax.optimization_barrier(jnp.mean(centred * centred, axis=-1, keepdims=True)) + 1e-05)
    scaled_input = centred * inverse_deviation
    normed_input = (scaled_input * layer_stretch + layer_shift).astype(jnp.bfloat16)
    projected = jnp.dot(normed_input.reshape(-1, CM), left_right_matrix, preferred_element_type=jnp.float32) + mapping_offset
    projected = projected.astype(jnp.bfloat16).reshape(SEQUENCE_ROWS, RESIDUE_COUNT, 2 * CH)
    left_wide = projected[:, :, :CH].astype(jnp.float32)
    right_wide = projected[:, :, CH:].astype(jnp.float32)
    blocks = RESIDUE_COUNT // 8

    def one_block(carry, number):
        output_total, right_sum = carry
        first = (number * 8).astype(jnp.int32)
        left_block = lax.dynamic_slice_in_dim(left_wide, first, 8, 1)
        grad_block = lax.dynamic_slice_in_dim(couplet_adjoint, first, 8, 0).reshape(-1, CZ)
        outer = (jnp.einsum('sic,sjd->ijcd', left_block, right_wide) / SEQUENCE_ROWS).astype(jnp.bfloat16)
        outer = outer.reshape(-1, CH * CH)
        update = (jnp.dot(outer, final_projection_matrix, preferred_element_type=jnp.float32) + final_offset_vector).astype(jnp.bfloat16)
        outer_grad = jnp.dot(grad_block, final_projection_matrix.T, preferred_element_type=jnp.float32).astype(jnp.bfloat16)
        output_total = output_total + jnp.dot(outer.T, grad_block, preferred_element_type=jnp.float32)
        grad_wide = outer_grad.astype(jnp.float32).reshape(8, RESIDUE_COUNT, CH, CH)
        left_grad = jnp.einsum('ijcd,sjd->sic', grad_wide, right_wide) / SEQUENCE_ROWS
        right_sum = right_sum + jnp.einsum('ijcd,sic->sjd', grad_wide, left_block) / SEQUENCE_ROWS
        return ((output_total, right_sum), (update.reshape(8, RESIDUE_COUNT, CZ), left_grad))
    start = (jnp.zeros((CH * CH, CZ), jnp.float32), jnp.zeros((SEQUENCE_ROWS, RESIDUE_COUNT, CH), jnp.float32))
    (output_total, right_grad), (updates, left_parts) = lax.scan(one_block, start, jnp.arange(blocks, dtype=jnp.int32))
    pair_delta = updates.reshape(RESIDUE_COUNT, RESIDUE_COUNT, CZ)
    left_grad = jnp.transpose(left_parts, (1, 0, 2, 3)).reshape(SEQUENCE_ROWS, RESIDUE_COUNT, CH)
    projected_grad = jnp.concatenate([left_grad, right_grad], axis=-1).astype(jnp.bfloat16)
    flat_grad = projected_grad.reshape(-1, 2 * CH)
    projector_total = jnp.dot(normed_input.reshape(-1, CM).T, flat_grad, preferred_element_type=jnp.float32)
    normed_grad = jnp.dot(flat_grad, left_right_matrix.T, preferred_element_type=jnp.float32).reshape(SEQUENCE_ROWS, RESIDUE_COUNT, CM)
    hidden_width = normed_grad * layer_stretch
    alignment_gradient = inverse_deviation * (hidden_width - lax.optimization_barrier(jnp.mean(hidden_width, axis=-1, keepdims=True)) - scaled_input * lax.optimization_barrier(jnp.mean(hidden_width * scaled_input, axis=-1, keepdims=True)))
    return (pair_delta, alignment_gradient.astype(jnp.bfloat16), projector_total / RESIDUE_COUNT, output_total * (math.sqrt(SEQUENCE_ROWS) / RESIDUE_COUNT))
```

```python
import math

import jax
import jax.numpy as jnp
from jax import lax
from jax.experimental import pallas as pl
from jax.experimental.pallas import tpu as pltpu
from jax.sharding import PartitionSpec as P

EPSILON = 1e-05
MESH = pl.DeviceIdType.MESH
f32 = jnp.float32
bf16 = jnp.bfloat16

NX, NZ, NM = 4, 8, 16
CH = 32
ROWS = 128
RES = 512


def dot(a, b):
    return jnp.dot(a, b, preferred_element_type=f32)


def dot_nt(a, b):
    return lax.dot_general(a, b, (((1,), (1,)), ((), ())), preferred_element_type=f32)


def loop(low, high, body):
    def step(k, carry):
        body(k)
        return carry

    lax.fori_loop(low, high, step, 0)


def kernel(
    msa, stretch, shift, wlr, offs, wf, fbias, adj,
    pd_out, ag_out, pg_out, wo_out,
    scaled, inv, nf, nb, np_, wl4t, wrt, lrow, rt,
    sb, rb, rbf, ls, rs, lmat, lt, rmat, amat, wff, w2, w2t,
    gmat, xmat, rgs, rgr, rgo, rz, rzr, lacc, lgs, lzr, bsf, bs, br, ng,
    wpart, wsend, wrecv, wzs, wzr, wzg, wfin, pdb,
    psend, precv, pzs, pzr, pgs, pgr,
    s1s, s1r, cps, cpr, zls, zlr, zrs, zrr, crs, crr, rgss, rgrs, bzs, bzr, bls, blr, b1s, b1r,
    pds, pdr, w1s, w1r, wzss, wzrs, wgs, wgr, was, war, p1s, p1r, pzss, pzrs, pas, par,
):
    me = lax.axis_index("dap")
    core = lax.rem(me, 2)
    x = lax.rem(me // 2, NX)
    z = lax.rem(me // 8, NZ)
    y = me // 64
    m = y * 8 + x * 2 + core
    other = 1 - core

    def plane_dev(mm):
        return (mm // 8) * 64 + z * 8 + lax.rem(mm, 8)

    def z_dev(zz):
        return y * 64 + zz * 8 + x * 2 + core

    def x_dev(xx):
        return y * 64 + z * 8 + xx * 2 + core

    core_dev = y * 64 + z * 8 + x * 2 + other

    def rcopy(src, dst, ss, rs_, dev):
        return pltpu.make_async_remote_copy(
            src_ref=src, dst_ref=dst, send_sem=ss, recv_sem=rs_, device_id={"dap": dev}, device_id_type=MESH
        )

    def planes(body):
        loop(1, NM, lambda k: body(lax.rem(m + k, NM)))

    def zs(body):
        loop(1, NZ, lambda k: body(lax.rem(z + k, NZ)))

    def xs(body):
        loop(1, NX, lambda k: body(lax.rem(x + k, NX)))

    barrier = pltpu.get_barrier_semaphore()
    planes(lambda mm: pl.semaphore_signal(barrier, inc=1, device_id={"dap": plane_dev(mm)}, device_id_type=MESH))
    zs(lambda zz: pl.semaphore_signal(barrier, inc=1, device_id={"dap": z_dev(zz)}, device_id_type=MESH))

    def norm_rows(k):
        rows = pl.ds(pl.multiple_of(k * 64, 64), 64)
        v = msa[0, rows, :].astype(f32)
        c = v - jnp.mean(v, axis=-1, keepdims=True)
        iv = lax.rsqrt(jnp.mean(c * c, axis=-1, keepdims=True) + EPSILON)
        sc = c * iv
        scaled[rows, :] = sc
        inv[rows, :] = jnp.broadcast_to(iv, (64, 128))
        n = (sc * stretch[...] + shift[...]).astype(bf16)
        nb[rows, :] = n
        n = n.astype(f32)
        nf[0, rows, :] = n[:, :128]
        nf[1, rows, :] = n[:, 128:]

    loop(0, 8, norm_rows)
    for r in range(4):
        for yc in range(4):
            start = (yc // 2) * 256 + (yc % 2) * 4 + r
            for h in range(2):
                np_[pl.ds(r * 128 + yc * 32, 32), pl.ds(h * 128, 128)] = nf[
                    h, pl.ds(start, 32, stride=8), :
                ].astype(bf16)

    w_rows = wlr[...]
    wlrt = w_rows.astype(f32).T
    wrt[...] = wlrt[CH:, :].astype(bf16)
    spread = lax.broadcasted_iota(jnp.int32, (64, 128), 0) == (lax.broadcasted_iota(jnp.int32, (64, 128), 1) & 31)
    wl4 = dot(w_rows, spread.astype(f32).astype(bf16))
    wl4t[...] = wl4.T.astype(bf16)
    diag = lax.broadcasted_iota(jnp.int32, (64, 64), 0) == lax.broadcasted_iota(jnp.int32, (64, 64), 1)
    offs_col = jnp.sum(jnp.where(diag, jnp.broadcast_to(offs[...], (64, 64)), 0.0), axis=1, keepdims=True)
    offs4 = jnp.sum(jnp.where(spread, jnp.broadcast_to(offs_col, (64, 128)), 0.0), axis=0, keepdims=True)
    lane_r = lax.broadcasted_iota(jnp.int32, (256, 128), 1) >> 5
    left = jnp.zeros((128, 128), f32)
    for r in range(4):
        left = left + dot(np_[pl.ds(r * 128, 128), :], jnp.where(lane_r == r, wl4, 0.0).astype(bf16))
    lrow[...] = (left + offs4).astype(bf16)
    rt[...] = (dot_nt(wlrt[CH:, :].astype(bf16), nb[...]) + offs_col[CH:, :]).astype(bf16)
    for mm in range(NM):
        yc = (mm // 8) * 2 + mm % 2
        xx, cc = (mm % 8) // 2, mm % 2
        sb[mm, pl.ds(0, 32), :] = lrow[pl.ds(yc * 32, 32), :]
        sb[mm, pl.ds(32, 16), :] = rt[pl.ds(cc * 16, 16), pl.ds(xx * 128, 128)]

    pl.semaphore_wait(barrier, NM - 1 + NZ - 1)

    planes(lambda mm: rcopy(sb.at[mm], rb.at[m], s1s.at[mm], s1r.at[m], plane_dev(mm)).start())
    rb[m] = sb[m]

    def adj_part(xx):
        return adj.at[:, pl.ds(pl.multiple_of(xx * 128, 128), 128), :]

    def own_i(xx):
        return amat.at[pl.ds(xx * 4, 4)]

    xs(lambda xx: rcopy(adj_part(xx), own_i(x), cps.at[xx], cpr.at[x], x_dev(xx)).start())
    amat[pl.ds(x * 4, 4)] = adj[:, pl.ds(pl.multiple_of(x * 128, 128), 128), :]

    wff[...] = wf[...].astype(f32)
    for d in range(CH):
        w2[pl.ds(d * 32, 32), :] = wff[pl.ds(d, 32, stride=32), :].astype(bf16)
    for k in range(8):
        w2t[:, pl.ds(k * 128, 128)] = w2[pl.ds(k * 128, 128), :].astype(f32).T.astype(bf16)

    planes(lambda mm: rcopy(sb.at[mm], rb.at[mm], s1s.at[mm], s1r.at[mm], plane_dev(mm)).wait_recv())

    loop(0, NM, lambda k: rbf.__setitem__((pl.ds(pl.multiple_of(k * 48, 48), 48), slice(None)), rb[k].astype(f32)))
    for zz in range(NZ):
        for xx in range(NX):
            ls[zz, :, pl.ds(xx * 128, 128)] = rbf[pl.ds(zz * 4 + xx, 16, stride=48), :].astype(bf16)
    for d in range(16):
        rs[:, pl.ds(d * 128, 128)] = rbf[pl.ds(32 + d, 16, stride=48), :].astype(bf16)

    def zrows(zz):
        return pl.ds(pl.multiple_of(zz * 16, 16), 16)

    def half(cc):
        return pl.ds(pl.multiple_of(cc * 2048, 2048), 2048)

    zs(lambda zz: rcopy(ls.at[zz], lmat.at[zrows(z), :], zls.at[zz], zlr.at[z], z_dev(zz)).start())
    zs(lambda zz: rcopy(rs, rmat.at[zrows(z), half(core)], zrs.at[zz], zrr.at[z], z_dev(zz)).start())
    rcopy(rs, rmat.at[zrows(z), half(core)], crs.at[z], crr.at[z], core_dev).start()
    lmat[zrows(z), :] = ls[z]
    rmat[zrows(z), half(core)] = rs[...]

    def r_piece(zz, cc):
        return rmat.at[zrows(zz), half(cc)]

    xs(lambda xx: rcopy(adj_part(xx), own_i(xx), cps.at[xx], cpr.at[xx], x_dev(xx)).wait_recv())

    def grad_pair(t):
        a2 = amat[pl.ds(t * 2, 2)].reshape(256, 128)
        for q in range(4):
            g = dot_nt(w2[pl.ds(q * 256, 256), :], a2)
            for e in range(8):
                for u in range(2):
                    rows = pl.ds(pl.multiple_of((2 * t + u) * 32, 32), 32)
                    gmat[rows, pl.ds((q * 8 + e) * 128, 128)] = g[e * 32 : e * 32 + 32, u * 128 : u * 128 + 128].astype(
                        bf16
                    )

    loop(0, 8, grad_pair)

    def forward(zz):
        rcopy(rs, r_piece(zz, core), zrs.at[zz], zrr.at[zz], z_dev(zz)).wait_recv()
        rcopy(r_piece(zz, core), r_piece(zz, core), crs.at[zz], crr.at[zz], core_dev).start()

    zs(forward)

    zs(lambda zz: rcopy(ls.at[zz], lmat.at[zrows(zz), :], zls.at[zz], zlr.at[zz], z_dev(zz)).wait_recv())
    for k in range(4):
        lt[pl.ds(k * 128, 128), :] = lmat[:, pl.ds(k * 128, 128)].astype(f32).T.astype(bf16)

    def right_other(k):
        cols = pl.ds(pl.multiple_of(other * 2048 + k * 512, 512), 512)
        rgs[:, pl.ds(pl.multiple_of(k * 512, 512), 512)] = (dot(lmat[...], gmat[:, cols]) * (1.0 / ROWS)).astype(bf16)

    loop(0, 4, right_other)
    rg_copy = rcopy(rgs, rgr, rgss, rgrs, core_dev)
    rg_copy.start()

    def right_own(k):
        cols = pl.ds(pl.multiple_of(core * 2048 + k * 512, 512), 512)
        rgo[:, pl.ds(pl.multiple_of(k * 512, 512), 512)] = dot(lmat[...], gmat[:, cols]) * (1.0 / ROWS)

    loop(0, 4, right_own)
    rg_copy.wait_recv()

    def right_add(k):
        cols = pl.ds(pl.multiple_of(k * 512, 512), 512)
        rz[:, cols] = (rgo[:, cols] + rgr[:, cols].astype(f32)).astype(bf16)

    loop(0, 4, right_add)
    zs(lambda zz: rcopy(rz.at[zrows(zz), :], rzr.at[z], bzs.at[zz], bzr.at[z], z_dev(zz)).start())
    rzr[z] = rz[zrows(z), :]

    loop(0, NZ, lambda zz: rcopy(r_piece(zz, other), r_piece(zz, other), crs.at[zz], crr.at[zz], core_dev).wait_recv())
    lacc[...] = jnp.zeros((128, 512), f32)

    def left_part(k):
        cols = pl.ds(pl.multiple_of(k * 1024, 1024), 1024)
        lacc[...] += dot_nt(rmat[:, cols], gmat[:, cols])

    loop(0, 4, left_part)
    lgs[...] = (lacc[...] * (1.0 / ROWS)).astype(bf16)
    zs(lambda zz: rcopy(lgs.at[zrows(zz), :], lzr.at[z], bls.at[zz], blr.at[z], z_dev(zz)).start())
    lzr[z] = lgs[zrows(z), :]

    def outer_part(n):
        o = dot(lt[...], rmat[:, pl.ds(pl.multiple_of(n * 256, 256), 256)]) * (1.0 / ROWS)
        for i in range(16):
            for e in range(2):
                rows = pl.ds(pl.multiple_of((2 * n + e) * 32, 32), 32)
                xmat[rows, pl.ds(i * 128, 128)] = o[i * 32 : i * 32 + 32, e * 128 : e * 128 + 128].astype(bf16)

    loop(0, 16, outer_part)

    def delta_pair(t):
        p = dot(w2t[...], xmat[:, pl.ds(pl.multiple_of(t * 256, 256), 256)])
        pdb[pl.ds(t * 2, 2)] = (p.T + fbias[...]).astype(bf16).reshape(2, 128, 128)

    loop(0, 8, delta_pair)

    def out_part(xx):
        return pd_out.at[:, pl.ds(pl.multiple_of(xx * 128, 128), 128), :]

    xs(lambda xx: rcopy(pdb.at[pl.ds(xx * 4, 4)], out_part(x), pds.at[xx], pdr.at[x], x_dev(xx)).start())
    pd_out[:, pl.ds(pl.multiple_of(x * 128, 128), 128), :] = pdb[pl.ds(x * 4, 4)]

    def w_part(n):
        rows = pl.ds(pl.multiple_of(n * 256, 256), 256)
        wpart[rows, :] = dot(xmat[rows, :], amat[...].reshape(2048, 128))

    loop(0, 4, w_part)
    for c in range(CH):
        wsend[c // 2, pl.ds((c % 2) * 32, 32), :] = wpart[pl.ds(c, 32, stride=32), :].astype(bf16)
    planes(lambda mm: rcopy(wsend.at[mm], wrecv.at[m], w1s.at[mm], w1r.at[m], plane_dev(mm)).start())
    wrecv[m] = wsend[m]

    def back_wait(zz):
        rcopy(rz.at[zrows(zz), :], rzr.at[zz], bzs.at[zz], bzr.at[zz], z_dev(zz)).wait_recv()
        rcopy(lgs.at[zrows(zz), :], lzr.at[zz], bls.at[zz], blr.at[zz], z_dev(zz)).wait_recv()

    zs(back_wait)
    for d in range(16):
        t = rzr[0, :, pl.ds(d * 128, 128)].astype(f32)
        for zz in range(1, NZ):
            t = t + rzr[zz, :, pl.ds(d * 128, 128)].astype(f32)
        bsf[pl.ds(32 + d, 16, stride=48), :] = t
    for zz in range(NZ):
        for xx in range(NX):
            bsf[pl.ds(zz * 4 + xx, 16, stride=48), :] = lzr[zz, :, pl.ds(xx * 128, 128)].astype(f32)
    loop(0, NM, lambda k: bs.__setitem__(k, bsf[pl.ds(pl.multiple_of(k * 48, 48), 48), :].astype(bf16)))
    planes(lambda mm: rcopy(bs.at[mm], br.at[m], b1s.at[mm], b1r.at[m], plane_dev(mm)).start())
    br[m] = bs[m]

    planes(lambda mm: rcopy(wsend.at[mm], wrecv.at[mm], w1s.at[mm], w1r.at[mm], plane_dev(mm)).wait_recv())
    t = wrecv[0].astype(f32)
    for mm in range(1, NM):
        t = t + wrecv[mm].astype(f32)
    wzs[...] = t.reshape(NZ, 8, 128)
    zs(lambda zz: rcopy(wzs.at[zz], wzr.at[z], wzss.at[zz], wzrs.at[z], z_dev(zz)).start())
    wzr[z] = wzs[z]

    planes(lambda mm: rcopy(bs.at[mm], br.at[mm], b1s.at[mm], b1r.at[mm], plane_dev(mm)).wait_recv())
    lparts = []
    for yc in range(4):
        t = None
        for xx in range(NX):
            v = br[(yc // 2) * 8 + xx * 2 + yc % 2, pl.ds(0, 32), :].astype(f32)
            t = v if t is None else t + v
        lparts.append(t)
    lg = jnp.concatenate(lparts, axis=0)
    rparts = []
    for cc in range(2):
        row = []
        for xx in range(NX):
            row.append(br[xx * 2 + cc, pl.ds(32, 16), :].astype(f32) + br[8 + xx * 2 + cc, pl.ds(32, 16), :].astype(f32))
        rparts.append(jnp.concatenate(row, axis=1))
    rg = jnp.concatenate(rparts, axis=0)
    lgb = lg.astype(bf16)
    lgt = lgb.astype(f32).T
    lcat = jnp.concatenate([lgt[r * 32 : r * 32 + 32, :] for r in range(4)], axis=1).astype(bf16)
    rgb = rg.astype(bf16)
    pleft = dot(lcat, np_[...])
    pright = dot(rgb, nb[...])
    for h in range(2):
        cols = slice(h * 128, h * 128 + 128)
        for k in range(4):
            psend[h * 8 + k] = pleft[k * 8 : k * 8 + 8, cols]
            psend[h * 8 + 4 + k] = pright[k * 8 : k * 8 + 8, cols]
    planes(lambda mm: rcopy(psend.at[mm], precv.at[m], p1s.at[mm], p1r.at[m], plane_dev(mm)).start())
    precv[m] = psend[m]

    zs(lambda zz: rcopy(wzs.at[zz], wzr.at[zz], wzss.at[zz], wzrs.at[zz], z_dev(zz)).wait_recv())
    t = wzr[0]
    for zz in range(1, NZ):
        t = t + wzr[zz]
    wzg[z] = t * (math.sqrt(ROWS) / RES)
    zs(lambda zz: rcopy(wzg.at[z], wzg.at[z], wgs.at[zz], wgr.at[z], z_dev(zz)).start())

    row_r = lax.broadcasted_iota(jnp.int32, (128, 256), 0) >> 5
    for r in range(4):
        v = dot(lgb, jnp.where(row_r == r, wl4t[...].astype(f32), 0.0).astype(bf16))
        for yc in range(4):
            start = (yc // 2) * 256 + (yc % 2) * 4 + r
            for h in range(2):
                ng[h, pl.ds(start, 32, stride=8), :] = v[yc * 32 : yc * 32 + 32, h * 128 : h * 128 + 128]
    nr = dot(rgb.astype(f32).T.astype(bf16), wrt[...])
    ng[0] = ng[0] + nr[:, :128]
    ng[1] = ng[1] + nr[:, 128:]

    planes(lambda mm: rcopy(psend.at[mm], precv.at[mm], p1s.at[mm], p1r.at[mm], plane_dev(mm)).wait_recv())
    t = precv[0]
    for mm in range(1, NM):
        t = t + precv[mm]
    pzs[...] = t
    zs(lambda zz: rcopy(pzs, pzr.at[z], pzss.at[zz], pzrs.at[z], z_dev(zz)).start())
    pzr[z] = t

    zs(lambda zz: rcopy(wzg.at[zz], wzg.at[zz], wgs.at[zz], wgr.at[zz], z_dev(zz)).wait_recv())
    mrows = pl.ds(pl.multiple_of(m * 64, 64), 64)
    wfin[...] = wzg[...].reshape(64, 128)
    wo_out[mrows, :] = wfin[...]
    planes(lambda mm: rcopy(wfin, wo_out.at[mrows, :], was.at[mm], war.at[m], plane_dev(mm)).start())

    def back_rows(k):
        rows = pl.ds(pl.multiple_of(k * 64, 64), 64)
        hid = jnp.concatenate([ng[0, rows, :], ng[1, rows, :]], axis=1) * stretch[...]
        sc = scaled[rows, :]
        iv = inv[rows, :][:, :1]
        g = iv * (
            hid - jnp.mean(hid, axis=-1, keepdims=True) - sc * jnp.mean(hid * sc, axis=-1, keepdims=True)
        )
        ag_out[0, rows, :] = g.astype(bf16)

    loop(0, 8, back_rows)

    zs(lambda zz: rcopy(pzs, pzr.at[zz], pzss.at[zz], pzrs.at[zz], z_dev(zz)).wait_recv())
    t = pzr[0]
    for zz in range(1, NZ):
        t = t + pzr[zz]
    t = t * (1.0 / RES)
    pgs[...] = t
    planes(lambda mm: rcopy(pgs, pgr.at[m], pas.at[mm], par.at[m], plane_dev(mm)).start())
    pgr[m] = t
    planes(lambda mm: rcopy(pgs, pgr.at[mm], pas.at[mm], par.at[mm], plane_dev(mm)).wait_recv())
    pt = pgr[...].reshape(128, 128).T
    pg_out[pl.ds(0, 128), :] = pt[:, :64]
    pg_out[pl.ds(128, 128), :] = pt[:, 64:]

    xs(lambda xx: rcopy(pdb.at[pl.ds(xx * 4, 4)], out_part(xx), pds.at[xx], pdr.at[xx], x_dev(xx)).wait_recv())

    def rows_of(mm):
        return wo_out.at[pl.ds(pl.multiple_of(mm * 64, 64), 64), :]

    planes(lambda mm: rcopy(wfin, rows_of(mm), was.at[mm], war.at[mm], plane_dev(mm)).wait_recv())

    def sent_plane(mm):
        dev = plane_dev(mm)
        rcopy(sb.at[mm], rb.at[m], s1s.at[mm], s1r.at[m], dev).wait_send()
        rcopy(wsend.at[mm], wrecv.at[m], w1s.at[mm], w1r.at[m], dev).wait_send()
        rcopy(bs.at[mm], br.at[m], b1s.at[mm], b1r.at[m], dev).wait_send()
        rcopy(psend.at[mm], precv.at[m], p1s.at[mm], p1r.at[m], dev).wait_send()
        rcopy(wfin, wo_out.at[mrows, :], was.at[mm], war.at[m], dev).wait_send()
        rcopy(pgs, pgr.at[m], pas.at[mm], par.at[m], dev).wait_send()

    planes(sent_plane)

    def sent_z(zz):
        dev = z_dev(zz)
        rcopy(ls.at[zz], lmat.at[zrows(z), :], zls.at[zz], zlr.at[z], dev).wait_send()
        rcopy(rs, r_piece(z, core), zrs.at[zz], zrr.at[z], dev).wait_send()
        rcopy(rz.at[zrows(zz), :], rzr.at[z], bzs.at[zz], bzr.at[z], dev).wait_send()
        rcopy(lgs.at[zrows(zz), :], lzr.at[z], bls.at[zz], blr.at[z], dev).wait_send()
        rcopy(wzs.at[zz], wzr.at[z], wzss.at[zz], wzrs.at[z], dev).wait_send()
        rcopy(wzg.at[z], wzg.at[z], wgs.at[zz], wgr.at[z], dev).wait_send()
        rcopy(pzs, pzr.at[z], pzss.at[zz], pzrs.at[z], dev).wait_send()

    zs(sent_z)

    def sent_x(xx):
        dev = x_dev(xx)
        rcopy(adj_part(xx), own_i(x), cps.at[xx], cpr.at[x], dev).wait_send()
        rcopy(pdb.at[pl.ds(xx * 4, 4)], out_part(x), pds.at[xx], pdr.at[x], dev).wait_send()

    xs(sent_x)
    loop(0, NZ, lambda zz: rcopy(r_piece(zz, core), r_piece(zz, core), crs.at[zz], crr.at[zz], core_dev).wait_send())
    rg_copy.wait_send()


def shards(msa, stretch, shift, wlr, offs, wf, fbias, adj):
    def vm(shape, dtype):
        return pltpu.VMEM(shape, dtype)

    def sem(*n):
        return pltpu.SemaphoreType.DMA(n)

    scratch = [
        vm((512, 256), f32), vm((512, 128), f32), vm((2, 512, 128), f32), vm((512, 256), bf16), vm((512, 256), bf16),
        vm((128, 256), bf16), vm((32, 256), bf16), vm((128, 128), bf16), vm((32, 512), bf16),
        vm((16, 48, 128), bf16), vm((16, 48, 128), bf16), vm((768, 128), f32), vm((8, 16, 512), bf16),
        vm((16, 2048), bf16), vm((128, 512), bf16), vm((512, 128), bf16), vm((128, 4096), bf16),
        vm((16, 128, 128), bf16), vm((1024, 128), f32), vm((1024, 128), bf16), vm((128, 1024), bf16),
        vm((512, 4096), bf16), vm((1024, 2048), bf16), vm((128, 2048), bf16), vm((128, 2048), bf16),
        vm((128, 2048), f32), vm((128, 2048), bf16), vm((8, 16, 2048), bf16), vm((128, 512), f32),
        vm((128, 512), bf16), vm((8, 16, 512), bf16), vm((768, 128), f32), vm((16, 48, 128), bf16),
        vm((16, 48, 128), bf16), vm((2, 512, 128), f32),
        vm((1024, 128), f32), vm((16, 64, 128), bf16), vm((16, 64, 128), bf16), vm((8, 8, 128), f32),
        vm((8, 8, 128), f32), vm((8, 8, 128), f32), vm((64, 128), f32), vm((16, 128, 128), bf16),
        vm((16, 8, 128), f32), vm((16, 8, 128), f32), vm((8, 128), f32), vm((8, 8, 128), f32), vm((8, 128), f32),
        vm((16, 8, 128), f32),
        sem(16), sem(16), sem(4), sem(4), sem(8), sem(8), sem(8), sem(8), sem(8), sem(8),
        pltpu.SemaphoreType.DMA, pltpu.SemaphoreType.DMA,
        sem(8), sem(8), sem(8), sem(8), sem(16), sem(16),
        sem(4), sem(4), sem(16), sem(16), sem(8), sem(8), sem(8), sem(8), sem(16), sem(16), sem(16), sem(16),
        sem(8), sem(8), sem(16), sem(16),
    ]
    return pl.pallas_call(
        kernel,
        out_shape=(
            jax.ShapeDtypeStruct((4, 512, 128), bf16),
            jax.ShapeDtypeStruct((1, 512, 256), bf16),
            jax.ShapeDtypeStruct((256, 64), f32),
            jax.ShapeDtypeStruct((1024, 128), f32),
        ),
        in_specs=[pl.BlockSpec(memory_space=pltpu.VMEM)] * 8,
        out_specs=(pl.BlockSpec(memory_space=pltpu.VMEM),) * 4,
        scratch_shapes=scratch,
        compiler_params=pltpu.CompilerParams(
            collective_id=0, has_side_effects=True, vmem_limit_bytes=48 * 1024 * 1024
        ),
    )(
        msa,
        stretch.reshape(1, 256),
        shift.reshape(1, 256),
        wlr,
        offs.reshape(1, 64),
        wf,
        fbias.reshape(1, 128),
        adj,
    )


def solution(mesh):
    placed = (P("dap", "crop", None), P(), P(), P(), P(), P(), P(), P("dap", "crop", None))
    return jax.shard_map(
        shards,
        mesh=mesh,
        in_specs=placed,
        out_specs=(
            P("dap", "crop", None),
            P("dap", "crop", None),
            P("crop", None),
            P("crop", None),
        ),
        check_vma=False,
    )
```

```python
import math

import jax
import jax.numpy as jnp
from jax import lax
from jax.experimental import pallas as pl
from jax.experimental.pallas import tpu as pltpu
from jax.sharding import PartitionSpec as P

EPSILON = 1e-05
MESH = pl.DeviceIdType.MESH
f32 = jnp.float32
bf16 = jnp.bfloat16

NX, NZ, NM = 4, 8, 16
CH = 32
ROWS = 128
RES = 512


def dot(a, b):
    return jnp.dot(a, b, preferred_element_type=f32)


def dot_nt(a, b):
    return lax.dot_general(a, b, (((1,), (1,)), ((), ())), preferred_element_type=f32)


def loop(low, high, body):
    def step(k, carry):
        body(k)
        return carry

    lax.fori_loop(low, high, step, 0)


class Exchange:
    def __init__(self, each, device, mine, src, dst, whole, ssem, rsem, apart=False):
        self.each, self.device, self.mine, self.src, self.dst, self.whole = each, device, mine, src, dst, whole
        self.ssem, self.rsem, self.apart = ssem, rsem, apart
        self.waited = False

    def copy(self, p, slot):
        return pltpu.make_async_remote_copy(
            src_ref=self.src(p),
            dst_ref=self.dst(slot),
            send_sem=self.ssem.at[0],
            recv_sem=self.rsem.at[slot if self.apart else 0],
            device_id={"dap": self.device(p)},
            device_id_type=MESH,
        )

    def bulk(self):
        return pltpu.make_async_remote_copy(
            src_ref=self.whole,
            dst_ref=self.whole,
            send_sem=self.ssem.at[0],
            recv_sem=self.rsem.at[0],
            device_id={"dap": self.device(0)},
            device_id_type=MESH,
        )

    def start_one(self, p):
        self.copy(p, self.mine).start()

    def recv_one(self, p):
        self.copy(p, p).wait_recv()

    def start(self):
        self.each(self.start_one)

    def recv(self):
        self.waited = True
        if self.apart:
            self.each(self.recv_one)
        else:
            self.bulk().wait_recv()

    def sent(self):
        self.bulk().wait_send()


def kernel(
    msa_h, stretch_h, shift_h, wlrt_h, offs_h, wf_h, fbias_h, adj_h,
    pd_h, ag_h, pg_h, wo_h,
    pd_out, ag_out, pg_out, wo_out,
    msa, stretch, shift, wlrt_v, offs, wf, fbias, adj,
    scaled, inv, nf, nb, np_, wl4t, wrt, lrow, rt,
    sb, rb, rbf, ls, rs, lmat, lt, rmat, amat, wff, w2, w2t,
    gmat, xmat, rgs, rgr, rgo, ryq, ryr, rz, rzr, lacc, lgs, lzr, bsf, bs, br, ng,
    wpart, wsend, wrecv, wzs, wzr, wfin, wall_v, pdb,
    psend, precv, pzs, pzr, pgs, pgr,
    in_sem, adj_sem, ssems, rsems, adj_r, zr_r, yf_r, ry_r,
):
    me = lax.axis_index("dap")
    core = lax.rem(me, 2)
    x = lax.rem(me // 2, NX)
    z = lax.rem(me // 8, NZ)
    y = me // 64
    m = y * 8 + x * 2 + core
    other = 1 - core

    def plane_dev(mm):
        return (mm // 8) * 64 + z * 8 + lax.rem(mm, 8)

    def z_dev(zz):
        return y * 64 + zz * 8 + x * 2 + core

    def x_dev(xx):
        return y * 64 + z * 8 + xx * 2 + core

    def core_dev(_):
        return y * 64 + z * 8 + x * 2 + other

    def y_dev(_):
        return (1 - y) * 64 + z * 8 + x * 2 + core

    def planes(body):
        loop(1, NM, lambda k: body(lax.rem(m + k, NM)))

    def zs(body):
        for k in (4, 3, 5, 2, 6, 1, 7):
            body(lax.rem(z + k, NZ))

    def xs(body):
        for k in (1, 3, 2):
            body(lax.rem(x + k, NX))

    exchanges = []

    def exchange(each, device, mine, src, dst, whole, rsem=None):
        k = pl.ds(len(exchanges), 1)
        e = Exchange(
            each, device, mine, src, dst, whole, ssems.at[k], rsems.at[k] if rsem is None else rsem, rsem is not None
        )
        exchanges.append(e)
        return e

    def finish():
        for e in exchanges:
            if not e.waited:
                e.recv()
        for e in exchanges:
            e.sent()

    small = [
        pltpu.make_async_copy(src, dst, in_sem.at[k])
        for k, (src, dst) in enumerate(
            [
                (msa_h, msa), (stretch_h, stretch), (shift_h, shift), (wlrt_h, wlrt_v), (offs_h, offs),
                (wf_h, wf), (fbias_h, fbias), (adj_h, adj),
            ]
        )
    ]
    for c in small:
        c.start()

    def adj_part(xx):
        return adj.at[:, pl.ds(pl.multiple_of(xx * 128, 128), 128), :]

    def own_i(xx):
        return amat.at[pl.ds(xx * 4, 4)]


    barrier = pltpu.get_barrier_semaphore()
    planes(lambda mm: pl.semaphore_signal(barrier, inc=1, device_id={"dap": plane_dev(mm)}, device_id_type=MESH))
    zs(lambda zz: pl.semaphore_signal(barrier, inc=1, device_id={"dap": z_dev(zz)}, device_id_type=MESH))
    for c in small:
        c.wait()

    def norm_rows(k):
        rows = pl.ds(pl.multiple_of(k * 64, 64), 64)
        v = msa[0, rows, :].astype(f32)
        c = v - jnp.mean(v, axis=-1, keepdims=True)
        iv = lax.rsqrt(jnp.mean(c * c, axis=-1, keepdims=True) + EPSILON)
        sc = c * iv
        scaled[rows, :] = sc
        inv[rows, :] = jnp.broadcast_to(iv, (64, 128))
        n = (sc * stretch[...] + shift[...]).astype(bf16)
        nb[rows, :] = n
        n = n.astype(f32)
        nf[0, rows, :] = n[:, :128]
        nf[1, rows, :] = n[:, 128:]

    loop(0, 8, norm_rows)
    for r in range(4):
        for yc in range(4):
            start = (yc // 2) * 256 + (yc % 2) * 4 + r
            for h in range(2):
                np_[pl.ds(r * 128 + yc * 32, 32), pl.ds(h * 128, 128)] = nf[
                    h, pl.ds(start, 32, stride=8), :
                ].astype(bf16)

    wlrt = wlrt_v[...]
    w_rows = wlrt.astype(f32).T.astype(bf16)
    wrt[...] = wlrt[CH:, :]
    spread = lax.broadcasted_iota(jnp.int32, (64, 128), 0) == (lax.broadcasted_iota(jnp.int32, (64, 128), 1) & 31)
    wl4 = dot(w_rows, spread.astype(f32).astype(bf16))
    wl4t[...] = wl4.T.astype(bf16)
    diag = lax.broadcasted_iota(jnp.int32, (64, 64), 0) == lax.broadcasted_iota(jnp.int32, (64, 64), 1)
    offs_col = jnp.sum(jnp.where(diag, jnp.broadcast_to(offs[...], (64, 64)), 0.0), axis=1, keepdims=True)
    offs4 = jnp.sum(jnp.where(spread, jnp.broadcast_to(offs_col, (64, 128)), 0.0), axis=0, keepdims=True)
    lane_r = lax.broadcasted_iota(jnp.int32, (256, 128), 1) >> 5
    left = jnp.zeros((128, 128), f32)
    for r in range(4):
        left = left + dot(np_[pl.ds(r * 128, 128), :], jnp.where(lane_r == r, wl4, 0.0).astype(bf16))
    lrow[...] = (left + offs4).astype(bf16)
    rt[...] = (dot_nt(wlrt[CH:, :], nb[...]) + offs_col[CH:, :]).astype(bf16)
    for mm in range(NM):
        yc = (mm // 8) * 2 + mm % 2
        xx, cc = (mm % 8) // 2, mm % 2
        sb[mm, pl.ds(0, 32), :] = lrow[pl.ds(yc * 32, 32), :]
        sb[mm, pl.ds(32, 16), :] = rt[pl.ds(cc * 16, 16), pl.ds(xx * 128, 128)]

    pl.semaphore_wait(barrier, NM - 1 + NZ - 1)

    first = exchange(planes, plane_dev, m, lambda mm: sb.at[mm], lambda mm: rb.at[mm], rb.at[pl.ds(0, NM - 1)])
    first.start()
    rb[m] = sb[m]
    adjoint = exchange(xs, x_dev, x, adj_part, own_i, amat.at[pl.ds(0, 12)], adj_r)
    adjoint.start()
    own_adj = pltpu.make_async_copy(adj_part(x), own_i(x), adj_sem)
    own_adj.start()

    wff[...] = wf[...].astype(f32)
    for d in range(CH):
        w2[pl.ds(d * 32, 32), :] = wff[pl.ds(d, 32, stride=32), :].astype(bf16)
    for k in range(8):
        w2t[:, pl.ds(k * 128, 128)] = w2[pl.ds(k * 128, 128), :].astype(f32).T.astype(bf16)

    first.recv()

    loop(0, NM, lambda k: rbf.__setitem__((pl.ds(pl.multiple_of(k * 48, 48), 48), slice(None)), rb[k].astype(f32)))
    for zz in range(NZ):
        for xx in range(NX):
            ls[zz, :, pl.ds(xx * 128, 128)] = (rbf[pl.ds(zz * 4 + xx, 16, stride=48), :] * (1.0 / ROWS)).astype(bf16)
    for d in range(16):
        rs[:, pl.ds(d * 128, 128)] = rbf[pl.ds(32 + d, 16, stride=48), :].astype(bf16)

    def zrows(zz):
        return pl.ds(pl.multiple_of(zz * 16, 16), 16)

    def half(cc):
        return pl.ds(pl.multiple_of(cc * 2048, 2048), 2048)

    def quarter(cc, yy):
        return pl.ds(pl.multiple_of(cc * 2048 + yy * 1024, 1024), 1024)

    def r_piece(zz, yy):
        return rmat.at[zrows(zz), quarter(core, yy)]

    zleft = exchange(
        zs, z_dev, z, lambda zz: ls.at[zz], lambda zz: lmat.at[zrows(zz), :], lmat.at[pl.ds(0, 112), :]
    )
    zleft.start()
    rs_own = rs.at[:, pl.ds(pl.multiple_of(y * 1024, 1024), 1024)]
    zright = exchange(
        zs, z_dev, z, lambda zz: rs_own, lambda zz: r_piece(zz, y), rmat.at[pl.ds(0, 112), quarter(core, y)], zr_r
    )
    zright.start()
    lmat[zrows(z), :] = ls[z]
    rmat[zrows(z), half(core)] = rs[...]

    yswap = exchange(
        zs, y_dev, None, lambda zz: r_piece(zz, y), None, rmat.at[pl.ds(0, 112), quarter(core, y)], yf_r
    )
    swap = exchange(None, core_dev, None, None, None, rmat.at[:, half(other)])

    def to_core(piece):
        pltpu.make_async_remote_copy(
            src_ref=piece,
            dst_ref=piece,
            send_sem=swap.ssem.at[0],
            recv_sem=swap.rsem.at[0],
            device_id={"dap": core_dev(0)},
            device_id_type=MESH,
        ).start()

    def y_copy(zz, yy):
        return pltpu.make_async_remote_copy(
            src_ref=r_piece(zz, yy),
            dst_ref=r_piece(zz, yy),
            send_sem=yswap.ssem.at[0],
            recv_sem=yf_r.at[zz],
            device_id={"dap": y_dev(0)},
            device_id_type=MESH,
        )

    yswap.recv_one = lambda zz: y_copy(zz, 1 - y).wait_recv()

    def forward(k):
        zz = lax.rem(z + k, NZ)
        zright.recv_one(zz)
        y_copy(zz, y).start()
        to_core(r_piece(zz, y))

    def forward_y(k):
        zz = lax.rem(z + k, NZ)
        yswap.recv_one(zz)
        to_core(r_piece(zz, 1 - y))

    to_core(rmat.at[zrows(z), half(core)])
    zright.waited = True
    yswap.waited = True

    def grad_pair(t):
        a2 = amat[pl.ds(t * 2, 2)].reshape(256, 128)
        for q in range(4):
            g = dot_nt(w2[pl.ds(q * 256, 256), :], a2)
            for e in range(8):
                for u in range(2):
                    rows = pl.ds(pl.multiple_of((2 * t + u) * 32, 32), 32)
                    gmat[rows, pl.ds((q * 8 + e) * 128, 128)] = g[e * 32 : e * 32 + 32, u * 128 : u * 128 + 128].astype(
                        bf16
                    )

    own_adj.wait()
    loop(x * 2, x * 2 + 2, grad_pair)
    adjoint.waited = True
    for k in (1, 3, 2):
        xx = lax.rem(x + k, NX)
        adjoint.recv_one(xx)
        loop(xx * 2, xx * 2 + 2, grad_pair)

    zleft.recv()
    for k in range(4):
        lt[pl.ds(k * 128, 128), :] = lmat[:, pl.ds(k * 128, 128)].astype(f32).T.astype(bf16)

    def right_other(yy):
        def part(k):
            cols = pl.ds(pl.multiple_of(other * 2048 + yy * 1024 + k * 512, 512), 512)
            rgs[:, pl.ds(pl.multiple_of(yy * 1024 + k * 512, 512), 512)] = dot(lmat[...], gmat[:, cols]).astype(bf16)

        loop(0, 2, part)

    def columns(ref, yy):
        return ref.at[:, pl.ds(pl.multiple_of(yy * 1024, 1024), 1024)]

    add = [
        exchange(lambda body: body(0), core_dev, 0, lambda _: columns(rgs, 1 - y), lambda _: columns(rgr, 1 - y), columns(rgr, 1 - y)),
        exchange(lambda body: body(0), core_dev, 0, lambda _: columns(rgs, y), lambda _: columns(rgr, y), columns(rgr, y)),
    ]
    right_other(1 - y)
    add[0].start()
    right_other(y)
    add[1].start()

    def right_own(k):
        cols = pl.ds(pl.multiple_of(core * 2048 + k * 512, 512), 512)
        rgo[:, pl.ds(pl.multiple_of(k * 512, 512), 512)] = dot(lmat[...], gmat[:, cols])

    loop(0, 4, right_own)
    for k in (4, 3, 5, 2):
        forward(k)
    add[0].recv()

    def right_add(k):
        cols = pl.ds(pl.multiple_of((1 - y) * 1024 + k * 512, 512), 512)
        ryq[:, pl.ds(pl.multiple_of(k * 512, 512), 512)] = (rgo[:, cols] + rgr[:, cols].astype(f32)).astype(bf16)

    loop(0, 2, right_add)

    def all_z(body):
        for k in (4, 3, 5, 2, 6, 1, 7, 0):
            body(lax.rem(z + k, NZ))

    ry = exchange(all_z, y_dev, None, lambda zz: ryq.at[zrows(zz), :], None, ryr, ry_r)
    ry.copy = lambda zz, _: pltpu.make_async_remote_copy(
        src_ref=ryq.at[zrows(zz), :],
        dst_ref=ryr.at[zrows(zz), :],
        send_sem=ry.ssem.at[0],
        recv_sem=ry_r.at[zz],
        device_id={"dap": y_dev(0)},
        device_id_type=MESH,
    )
    ry.start()
    for k in (6, 1, 7):
        forward(k)
    add[1].recv()

    for k in (4, 3, 5, 2, 6, 1, 7):
        forward_y(k)
    swap.recv()

    bright = exchange(
        zs, z_dev, z, lambda zz: rz.at[zrows(zz), :], lambda zz: rzr.at[zz], rzr.at[pl.ds(0, NZ - 1)]
    )
    mine = pl.ds(pl.multiple_of(y * 1024, 1024), 1024)
    ry.waited = True

    def right_rows(k):
        zz = lax.rem(z + k, NZ)
        ry.recv_one(zz)
        t = rgo[zrows(zz), mine] + rgr[zrows(zz), mine].astype(f32) + ryr[zrows(zz), :].astype(f32)
        if k == 0:
            rzr[z] = t.astype(bf16)
        else:
            rz[zrows(zz), :] = t.astype(bf16)
            bright.start_one(zz)

    lacc[...] = jnp.zeros((128, 512), f32)
    for n, ks in enumerate([(4, 3), (5, 2), (6, 1), (7, 0)]):
        lacc[...] += dot_nt(rmat[:, pl.ds(n * 1024, 1024)], gmat[:, pl.ds(n * 1024, 1024)])
        for k in ks:
            right_rows(k)
    lgs[...] = (lacc[...] * (1.0 / ROWS)).astype(bf16)
    bleft = exchange(
        zs, z_dev, z, lambda zz: lgs.at[zrows(zz), :], lambda zz: lzr.at[zz], lzr.at[pl.ds(0, NZ - 1)]
    )
    bleft.start()
    lzr[z] = lgs[zrows(z), :]

    def outer_part(n):
        o = dot(lt[...], rmat[:, pl.ds(pl.multiple_of(n * 256, 256), 256)])
        for i in range(16):
            for e in range(2):
                rows = pl.ds(pl.multiple_of((2 * n + e) * 32, 32), 32)
                xmat[rows, pl.ds(i * 128, 128)] = o[i * 32 : i * 32 + 32, e * 128 : e * 128 + 128].astype(bf16)

    loop(0, 16, outer_part)

    def delta_pair(t):
        p = dot(w2t[...], xmat[:, pl.ds(pl.multiple_of(t * 256, 256), 256)])
        pdb[pl.ds(t * 2, 2)] = (p.T + fbias[...]).astype(bf16).reshape(2, 128, 128)

    loop(0, 8, delta_pair)

    def out_part(xx):
        return pd_out.at[:, pl.ds(pl.multiple_of(xx * 128, 128), 128), :]

    delta = exchange(xs, x_dev, x, lambda xx: pdb.at[pl.ds(xx * 4, 4)], out_part, pd_out.at[:, pl.ds(0, 384), :])
    delta.start()
    pd_out[:, pl.ds(pl.multiple_of(x * 128, 128), 128), :] = pdb[pl.ds(x * 4, 4)]

    def w_part(n):
        rows = pl.ds(pl.multiple_of(n * 256, 256), 256)
        wpart[rows, :] = dot(xmat[rows, :], amat[...].reshape(2048, 128))

    loop(0, 4, w_part)
    for c in range(CH):
        wsend[c // 2, pl.ds((c % 2) * 32, 32), :] = wpart[pl.ds(c, 32, stride=32), :].astype(bf16)
    wplane = exchange(planes, plane_dev, m, lambda mm: wsend.at[mm], lambda mm: wrecv.at[mm], wrecv.at[pl.ds(0, NM - 1)])
    wplane.start()
    wrecv[m] = wsend[m]

    bright.recv()
    bleft.recv()
    bsf[...] = jnp.zeros((768, 128), f32)
    for d in range(8):
        t = rzr[0, :, pl.ds(d * 128, 128)].astype(f32)
        for zz in range(1, NZ):
            t = t + rzr[zz, :, pl.ds(d * 128, 128)].astype(f32)
        bsf[pl.ds(32 + d, 16, stride=48), :] = t
    for zz in range(NZ):
        for xx in range(NX):
            bsf[pl.ds(zz * 4 + xx, 16, stride=48), :] = lzr[zz, :, pl.ds(xx * 128, 128)].astype(f32)
    loop(0, NM, lambda k: bs.__setitem__(k, bsf[pl.ds(pl.multiple_of(k * 48, 48), 48), :].astype(bf16)))
    back = exchange(planes, plane_dev, m, lambda mm: bs.at[mm], lambda mm: br.at[mm], br.at[pl.ds(0, NM - 1)])
    back.start()
    br[m] = bs[m]

    back.recv()
    lparts = []
    for yc in range(4):
        t = None
        for xx in range(NX):
            v = br[(yc // 2) * 8 + xx * 2 + yc % 2, pl.ds(0, 32), :].astype(f32)
            t = v if t is None else t + v
        lparts.append(t)
    lg = jnp.concatenate(lparts, axis=0)
    rparts = []
    for cc in range(2):
        for yy in range(2):
            row = [br[yy * 8 + xx * 2 + cc, pl.ds(32, 16), :].astype(f32)[:8] for xx in range(NX)]
            rparts.append(jnp.concatenate(row, axis=1))
    rg = jnp.concatenate(rparts, axis=0)
    lgb = lg.astype(bf16)
    lgt = lgb.astype(f32).T
    lcat = jnp.concatenate([lgt[r * 32 : r * 32 + 32, :] for r in range(4)], axis=1).astype(bf16)
    rgb = rg.astype(bf16)
    pleft = dot(lcat, np_[...])
    pright = dot(rgb, nb[...])
    for h in range(2):
        cols = slice(h * 128, h * 128 + 128)
        for k in range(4):
            psend[h * 8 + k] = pleft[k * 8 : k * 8 + 8, cols]
            psend[h * 8 + 4 + k] = pright[k * 8 : k * 8 + 8, cols]
    pplane = exchange(planes, plane_dev, m, lambda mm: psend.at[mm], lambda mm: precv.at[mm], precv.at[pl.ds(0, NM - 1)])
    pplane.start()
    precv[m] = psend[m]

    wplane.recv()
    t = wrecv[0].astype(f32)
    for mm in range(1, NM):
        t = t + wrecv[mm].astype(f32)
    wzs[...] = t.astype(bf16)
    wz = exchange(zs, z_dev, z, lambda zz: wzs, lambda zz: wzr.at[zz], wzr.at[pl.ds(0, NZ - 1)])
    wz.start()
    wzr[z] = wzs[...]

    row_r = lax.broadcasted_iota(jnp.int32, (128, 256), 0) >> 5
    for r in range(4):
        v = dot(lgb, jnp.where(row_r == r, wl4t[...].astype(f32), 0.0).astype(bf16))
        for yc in range(4):
            start = (yc // 2) * 256 + (yc % 2) * 4 + r
            for h in range(2):
                ng[h, pl.ds(start, 32, stride=8), :] = v[yc * 32 : yc * 32 + 32, h * 128 : h * 128 + 128]
    nr = dot(rgb.astype(f32).T.astype(bf16), wrt[...])
    ng[0] = ng[0] + nr[:, :128]
    ng[1] = ng[1] + nr[:, 128:]

    pplane.recv()
    t = precv[0]
    for mm in range(1, NM):
        t = t + precv[mm]
    pzs[...] = t
    pz = exchange(zs, z_dev, z, lambda zz: pzs, lambda zz: pzr.at[zz], pzr.at[pl.ds(0, NZ - 1)])
    pz.start()
    pzr[z] = t
    def back_rows(k):
        rows = pl.ds(pl.multiple_of(k * 64, 64), 64)
        hid = jnp.concatenate([ng[0, rows, :], ng[1, rows, :]], axis=1) * stretch[...]
        sc = scaled[rows, :]
        iv = inv[rows, :][:, :1]
        g = iv * (
            hid - jnp.mean(hid, axis=-1, keepdims=True) - sc * jnp.mean(hid * sc, axis=-1, keepdims=True)
        )
        ag_out[0, rows, :] = g.astype(bf16)

    loop(0, 8, back_rows)
    ag_copy = pltpu.make_async_copy(ag_out, ag_h, in_sem.at[0])
    ag_copy.start()

    wz.recv()
    t = wzr[0].astype(f32)
    for zz in range(1, NZ):
        t = t + wzr[zz].astype(f32)
    wfin[...] = (t * (math.sqrt(ROWS) / RES)).astype(bf16)
    wall = exchange(
        planes, plane_dev, m, lambda mm: wfin, lambda mm: wall_v.at[mm], wall_v.at[pl.ds(0, NM - 1)]
    )
    wall.start()
    wall_v[m] = wfin[...]

    pz.recv()
    t = pzr[0]
    for zz in range(1, NZ):
        t = t + pzr[zz]
    t = t * (1.0 / RES)
    pgs[...] = t
    pall = exchange(planes, plane_dev, m, lambda mm: pgs, lambda mm: pgr.at[mm], pgr.at[pl.ds(0, NM - 1)])
    pall.start()
    pgr[m] = t

    delta.recv()
    pd_copy = pltpu.make_async_copy(pd_out, pd_h, in_sem.at[1])
    pd_copy.start()
    wall.recv()
    wo_out[...] = wall_v[...].reshape(1024, 128).astype(f32)
    wo_copy = pltpu.make_async_copy(wo_out, wo_h, in_sem.at[2])
    wo_copy.start()
    pall.recv()
    pt = pgr[...].reshape(2, 64, 128)
    pg_out[:, pl.ds(0, 128)] = pt[0]
    pg_out[:, pl.ds(128, 128)] = pt[1]
    pg_copy = pltpu.make_async_copy(pg_out, pg_h, in_sem.at[3])
    pg_copy.start()
    finish()
    for c in (ag_copy, pd_copy, wo_copy, pg_copy):
        c.wait()


def emit(pd, ag, pg, wo, pd_o, ag_o, pg_o, wo_o, pd_v, ag_v, pg_v, wo_v, sems):
    parts = [(pd.at[k], pd_v.at[k], pd_o.at[k]) for k in range(4)]
    parts += [(ag, ag_v, ag_o), (pg, pg_v, pg_o), (wo, wo_v, wo_o)]
    for k, (src, mid, _) in enumerate(parts):
        pltpu.make_async_copy(src, mid, sems.at[k]).start()
    for k, (src, mid, dst) in enumerate(parts):
        pltpu.make_async_copy(src, mid, sems.at[k]).wait()
        pltpu.make_async_copy(mid, dst, sems.at[k]).start()
    for k, (_, mid, dst) in enumerate(parts):
        pltpu.make_async_copy(mid, dst, sems.at[k]).wait()


def shards(msa, stretch, shift, wlr, offs, wf, fbias, adj):
    def vm(shape, dtype):
        return pltpu.VMEM(shape, dtype)

    def sem(*n):
        return pltpu.SemaphoreType.DMA(n)

    scratch = [
        vm((4, 512, 128), bf16), vm((1, 512, 256), bf16), vm((64, 256), f32), vm((1024, 128), f32),
        vm((1, 512, 256), bf16), vm((1, 256), f32), vm((1, 256), f32), vm((64, 256), bf16), vm((1, 64), f32),
        vm((1024, 128), bf16), vm((1, 128), f32), vm((4, 512, 128), bf16),
        vm((512, 256), f32), vm((512, 128), f32), vm((2, 512, 128), f32), vm((512, 256), bf16), vm((512, 256), bf16),
        vm((128, 256), bf16), vm((32, 256), bf16), vm((128, 128), bf16), vm((32, 512), bf16),
        vm((16, 48, 128), bf16), vm((16, 48, 128), bf16), vm((768, 128), f32), vm((8, 16, 512), bf16),
        vm((16, 2048), bf16), vm((128, 512), bf16), vm((512, 128), bf16), vm((128, 4096), bf16),
        vm((16, 128, 128), bf16), vm((1024, 128), f32), vm((1024, 128), bf16), vm((128, 1024), bf16),
        vm((512, 4096), bf16), vm((1024, 2048), bf16), vm((128, 2048), bf16), vm((128, 2048), bf16),
        vm((128, 2048), f32), vm((128, 1024), bf16), vm((128, 1024), bf16), vm((128, 1024), bf16),
        vm((8, 16, 1024), bf16), vm((128, 512), f32),
        vm((128, 512), bf16), vm((8, 16, 512), bf16), vm((768, 128), f32), vm((16, 48, 128), bf16),
        vm((16, 48, 128), bf16), vm((2, 512, 128), f32),
        vm((1024, 128), f32), vm((16, 64, 128), bf16), vm((16, 64, 128), bf16), vm((64, 128), bf16),
        vm((8, 64, 128), bf16), vm((64, 128), bf16), vm((16, 64, 128), bf16), vm((16, 128, 128), bf16),
        vm((16, 8, 128), f32), vm((16, 8, 128), f32), vm((8, 128), f32), vm((8, 8, 128), f32), vm((8, 128), f32),
        vm((16, 8, 128), f32),
        sem(8), pltpu.SemaphoreType.DMA, sem(20), sem(20), sem(4), sem(8), sem(8), sem(8),
    ]
    pd, ag, pg, wo = pl.pallas_call(
        kernel,
        out_shape=(
            jax.ShapeDtypeStruct((4, 512, 128), bf16),
            jax.ShapeDtypeStruct((1, 512, 256), bf16),
            jax.ShapeDtypeStruct((64, 256), f32),
            jax.ShapeDtypeStruct((1024, 128), f32),
        ),
        in_specs=[pl.BlockSpec(memory_space=pltpu.HBM)] * 8,
        out_specs=(pl.BlockSpec(memory_space=pltpu.HBM),) * 4,
        scratch_shapes=scratch,
        compiler_params=pltpu.CompilerParams(
            collective_id=0, has_side_effects=True, vmem_limit_bytes=60 * 1024 * 1024
        ),
    )(
        msa,
        stretch.reshape(1, 256),
        shift.reshape(1, 256),
        wlr.T,
        offs.reshape(1, 64),
        wf,
        fbias.reshape(1, 128),
        adj,
    )
    pd, ag, pg, wo = pl.pallas_call(
        emit,
        out_shape=tuple(jax.ShapeDtypeStruct(v.shape, v.dtype) for v in (pd, ag, pg, wo)),
        in_specs=[pl.BlockSpec(memory_space=pltpu.HBM)] * 4,
        out_specs=(pl.BlockSpec(memory_space=pltpu.HBM),) * 4,
        scratch_shapes=[vm((4, 512, 128), bf16), vm((1, 512, 256), bf16), vm((64, 256), f32), vm((1024, 128), f32), sem(7)],
        compiler_params=pltpu.CompilerParams(vmem_limit_bytes=60 * 1024 * 1024),
    )(pd, ag, pg, wo)
    return pd, ag, pg.T, wo


def solution(mesh):
    placed = (P("dap", "crop", None), P(), P(), P(), P(), P(), P(), P("dap", "crop", None))
    return jax.shard_map(
        shards,
        mesh=mesh,
        in_specs=placed,
        out_specs=(
            P("dap", "crop", None),
            P("dap", "crop", None),
            P("crop", None),
            P("crop", None),
        ),
        check_vma=False,
    )
```

```python
import math

import jax
import jax.numpy as jnp
from jax import lax
from jax.experimental import pallas as pl
from jax.experimental.pallas import tpu as pltpu
from jax.sharding import PartitionSpec as P

EPSILON = 1e-05
MESH = pl.DeviceIdType.MESH
f32 = jnp.float32
bf16 = jnp.bfloat16

NX, NZ, NM = 4, 8, 16
CH = 32
ROWS = 128
RES = 512
FAR = (4, 3, 5)
NEAR = (2, 6, 1, 7)


def dot(a, b):
    return jnp.dot(a, b, preferred_element_type=f32)


def dot_nt(a, b):
    return lax.dot_general(a, b, (((1,), (1,)), ((), ())), preferred_element_type=f32)


def loop(low, high, body):
    def step(k, carry):
        body(k)
        return carry

    lax.fori_loop(low, high, step, 0)


class Exchange:
    def __init__(self, each, device, mine, src, dst, whole, ssem, rsem, apart=False):
        self.each, self.device, self.mine, self.src, self.dst, self.whole = each, device, mine, src, dst, whole
        self.ssem, self.rsem, self.apart = ssem, rsem, apart
        self.waited = False

    def copy(self, p, slot):
        return pltpu.make_async_remote_copy(
            src_ref=self.src(p),
            dst_ref=self.dst(slot),
            send_sem=self.ssem.at[0],
            recv_sem=self.rsem.at[slot if self.apart else 0],
            device_id={"dap": self.device(p)},
            device_id_type=MESH,
        )

    def bulk(self):
        return pltpu.make_async_remote_copy(
            src_ref=self.whole,
            dst_ref=self.whole,
            send_sem=self.ssem.at[0],
            recv_sem=self.rsem.at[0],
            device_id={"dap": self.device(0)},
            device_id_type=MESH,
        )

    def start_one(self, p):
        self.copy(p, self.mine).start()

    def recv_one(self, p):
        self.copy(p, p).wait_recv()

    def start(self):
        self.each(self.start_one)

    def recv(self):
        self.waited = True
        if self.apart:
            self.each(self.recv_one)
        else:
            self.bulk().wait_recv()

    def sent(self):
        self.bulk().wait_send()


def kernel(
    msa_h, stretch_h, shift_h, wlrt_h, offs_h, wf_h, fbias_h, adj_h,
    pd_h, ag_h, pg_h, wo_h,
    pd_out, ag_out, pg_out, wo_out,
    msa, stretch, shift, wlrt_v, offs, wf, fbias, adj,
    scaled, inv, nf, nb, np_, wl4t, wrt, rt,
    sb, rb, rbf, las, la, laf, lbf, lb, lbr, lbrf, lgf, rs, lmat, lt, rmat, amat, wff, w2, w2t,
    gmat, xmat, rgs, rgr, rgo, ryq, ryr, rz, rzr, lacc, lgs, lzr, bsf, bs, br, ng,
    wpart, wsend, wrecv, wzs, wzr, wfin, wall_v, pdb,
    psend, precv, pzs, pzr, pgs, pgr,
    in_sem, adj_sem, ssems, rsems, adj_r, zr_r, yf_r, ry_r,
):
    me = lax.axis_index("dap")
    core = lax.rem(me, 2)
    x = lax.rem(me // 2, NX)
    z = lax.rem(me // 8, NZ)
    y = me // 64
    m = y * 8 + x * 2 + core
    other = 1 - core

    def plane_dev(mm):
        return (mm // 8) * 64 + z * 8 + lax.rem(mm, 8)

    def z_dev(zz):
        return y * 64 + zz * 8 + x * 2 + core

    def x_dev(xx):
        return y * 64 + z * 8 + xx * 2 + core

    def core_dev(_):
        return y * 64 + z * 8 + x * 2 + other

    def y_dev(_):
        return (1 - y) * 64 + z * 8 + x * 2 + core

    def planes(body):
        loop(1, NM, lambda k: body(lax.rem(m + k, NM)))

    def zs(body):
        for k in (4, 3, 5, 2, 6, 1, 7):
            body(lax.rem(z + k, NZ))

    def zs_far(body):
        for k in FAR:
            body(lax.rem(z + k, NZ))

    def zs_near(body):
        for k in NEAR:
            body(lax.rem(z + k, NZ))

    def xs(body):
        for k in (1, 3, 2):
            body(lax.rem(x + k, NX))

    exchanges = []

    def exchange(each, device, mine, src, dst, whole, rsem=None):
        k = pl.ds(len(exchanges), 1)
        e = Exchange(
            each, device, mine, src, dst, whole, ssems.at[k], rsems.at[k] if rsem is None else rsem, rsem is not None
        )
        exchanges.append(e)
        return e

    def finish():
        for e in exchanges:
            if not e.waited:
                e.recv()
        for e in exchanges:
            e.sent()

    small = [
        pltpu.make_async_copy(src, dst, in_sem.at[k])
        for k, (src, dst) in enumerate(
            [
                (msa_h, msa), (stretch_h, stretch), (shift_h, shift), (wlrt_h, wlrt_v), (offs_h, offs),
                (wf_h, wf), (fbias_h, fbias), (adj_h, adj),
            ]
        )
    ]
    for c in small:
        c.start()

    def adj_part(xx):
        return adj.at[:, pl.ds(pl.multiple_of(xx * 128, 128), 128), :]

    def own_i(xx):
        return amat.at[pl.ds(xx * 4, 4)]


    barrier = pltpu.get_barrier_semaphore()
    planes(lambda mm: pl.semaphore_signal(barrier, inc=1, device_id={"dap": plane_dev(mm)}, device_id_type=MESH))
    zs(lambda zz: pl.semaphore_signal(barrier, inc=1, device_id={"dap": z_dev(zz)}, device_id_type=MESH))
    for c in small:
        c.wait()

    def norm_rows(k):
        rows = pl.ds(pl.multiple_of(k * 64, 64), 64)
        v = msa[0, rows, :].astype(f32)
        c = v - jnp.mean(v, axis=-1, keepdims=True)
        iv = lax.rsqrt(jnp.mean(c * c, axis=-1, keepdims=True) + EPSILON)
        sc = c * iv
        scaled[rows, :] = sc
        inv[rows, :] = jnp.broadcast_to(iv, (64, 128))
        n = (sc * stretch[...] + shift[...]).astype(bf16)
        nb[rows, :] = n
        n = n.astype(f32)
        nf[0, rows, :] = n[:, :128]
        nf[1, rows, :] = n[:, 128:]

    loop(0, 8, norm_rows)
    for r in range(4):
        for zz in range(NZ):
            v = [
                jnp.concatenate([nf[h, pl.ds(yy * 256 + zz * 32 + r, 8, stride=4), :] for h in range(2)], axis=1)
                for yy in range(2)
            ]
            np_[pl.ds(r * 128 + zz * 16, 16), :] = jnp.concatenate(v, axis=0).astype(bf16)

    wlrt = wlrt_v[...]
    w_rows = wlrt.astype(f32).T.astype(bf16)
    wrt[...] = wlrt[CH:, :]
    spread = lax.broadcasted_iota(jnp.int32, (64, 128), 0) == (lax.broadcasted_iota(jnp.int32, (64, 128), 1) & 31)
    wl4 = dot(w_rows, spread.astype(f32).astype(bf16))
    wl4t[...] = wl4.T.astype(bf16)
    diag = lax.broadcasted_iota(jnp.int32, (64, 64), 0) == lax.broadcasted_iota(jnp.int32, (64, 64), 1)
    offs_col = jnp.sum(jnp.where(diag, jnp.broadcast_to(offs[...], (64, 64)), 0.0), axis=1, keepdims=True)
    offs4 = jnp.sum(jnp.where(spread, jnp.broadcast_to(offs_col, (64, 128)), 0.0), axis=0, keepdims=True)
    lane_r = lax.broadcasted_iota(jnp.int32, (256, 128), 1) >> 5
    left = jnp.zeros((128, 128), f32)
    for r in range(4):
        left = left + dot(np_[pl.ds(r * 128, 128), :], jnp.where(lane_r == r, wl4, 0.0).astype(bf16))
    left = (left + offs4).astype(bf16).astype(f32) * (1.0 / ROWS)
    las[...] = left.astype(bf16).reshape(NZ, NM, 128)
    rt[...] = (dot_nt(wlrt[CH:, :], nb[...]) + offs_col[CH:, :]).astype(bf16)
    for mm in range(NM):
        xx, cc = (mm % 8) // 2, mm % 2
        sb[mm] = rt[pl.ds(cc * 16, 16), pl.ds(xx * 128, 128)]

    pl.semaphore_wait(barrier, NM - 1 + NZ - 1)

    first = exchange(planes, plane_dev, m, lambda mm: sb.at[mm], lambda mm: rb.at[mm], rb.at[pl.ds(0, NM - 1)])
    first.start()
    rb[m] = sb[m]
    zleft = exchange(zs, z_dev, z, lambda zz: las.at[zz], lambda zz: la.at[zz], la.at[pl.ds(0, NZ - 1)])
    zleft.start()
    la[z] = las[z]
    adjoint = exchange(xs, x_dev, x, adj_part, own_i, amat.at[pl.ds(0, 12)], adj_r)
    adjoint.start()
    own_adj = pltpu.make_async_copy(adj_part(x), own_i(x), adj_sem)
    own_adj.start()

    wff[...] = wf[...].astype(f32)
    for d in range(CH):
        w2[pl.ds(d * 32, 32), :] = wff[pl.ds(d, 32, stride=32), :].astype(bf16)
    for k in range(8):
        w2t[:, pl.ds(k * 128, 128)] = w2[pl.ds(k * 128, 128), :].astype(f32).T.astype(bf16)

    first.recv()

    rbf[...] = rb[...].reshape(256, 128).astype(f32)
    for d in range(16):
        rs[:, pl.ds(d * 128, 128)] = rbf[pl.ds(d, 16, stride=16), :].astype(bf16)

    def zrows(zz):
        return pl.ds(pl.multiple_of(zz * 16, 16), 16)

    def half(cc):
        return pl.ds(pl.multiple_of(cc * 2048, 2048), 2048)

    def quarter(cc, yy):
        return pl.ds(pl.multiple_of(cc * 2048 + yy * 1024, 1024), 1024)

    def r_piece(zz, yy):
        return rmat.at[zrows(zz), quarter(core, yy)]

    rs_own = rs.at[:, pl.ds(pl.multiple_of(y * 1024, 1024), 1024)]
    zfar = exchange(
        zs_far, z_dev, z, lambda zz: rs_own, lambda zz: r_piece(zz, y), rmat.at[pl.ds(0, 48), quarter(0, 0)], zr_r
    )
    znear = exchange(
        zs_near, z_dev, z, lambda zz: rs, lambda zz: rmat.at[zrows(zz), half(core)], rmat.at[pl.ds(0, 64), half(0)], zr_r
    )
    zfar.start()
    znear.start()
    rmat[zrows(z), half(core)] = rs[...]

    zleft.recv()
    laf[...] = la[...].reshape(128, 128).astype(f32)
    for mm in range(0, NM, 2):
        for cc in range(2):
            yc, xx = (mm // 8) * 2 + cc, (mm % 8) // 2
            lbf[pl.ds(yc * 32 + xx * 8, 8), :] = laf[pl.ds(mm + cc, 8, stride=16), :]
    lb[...] = lbf[...].astype(bf16).reshape(4, 32, 128)
    lplane = exchange(
        planes,
        plane_dev,
        m,
        lambda mm: lb.at[(mm // 8) * 2 + lax.rem(mm, 2)],
        lambda mm: lbr.at[mm],
        lbr.at[pl.ds(0, NM - 1)],
    )
    lplane.start()
    lbr[m] = lb[y * 2 + core]

    yswap = exchange(
        zs_far, y_dev, None, lambda zz: r_piece(zz, y), None, rmat.at[pl.ds(0, 48), quarter(0, 0)], yf_r
    )
    swap = exchange(None, core_dev, None, None, None, rmat.at[:, half(other)])

    def to_core(piece):
        pltpu.make_async_remote_copy(
            src_ref=piece,
            dst_ref=piece,
            send_sem=swap.ssem.at[0],
            recv_sem=swap.rsem.at[0],
            device_id={"dap": core_dev(0)},
            device_id_type=MESH,
        ).start()

    def y_copy(zz, yy):
        return pltpu.make_async_remote_copy(
            src_ref=r_piece(zz, yy),
            dst_ref=r_piece(zz, yy),
            send_sem=yswap.ssem.at[0],
            recv_sem=yf_r.at[zz],
            device_id={"dap": y_dev(0)},
            device_id_type=MESH,
        )

    yswap.recv_one = lambda zz: y_copy(zz, 1 - y).wait_recv()

    def forward(k):
        zz = lax.rem(z + k, NZ)
        if k in FAR:
            zfar.recv_one(zz)
            y_copy(zz, y).start()
            to_core(r_piece(zz, y))
        else:
            znear.recv_one(zz)
            to_core(rmat.at[zrows(zz), half(core)])

    def forward_y(k):
        zz = lax.rem(z + k, NZ)
        yswap.recv_one(zz)
        to_core(r_piece(zz, 1 - y))

    to_core(rmat.at[zrows(z), half(core)])
    zfar.waited = True
    znear.waited = True
    yswap.waited = True

    def grad_pair(t):
        a2 = amat[pl.ds(t * 2, 2)].reshape(256, 128)
        for q in range(4):
            g = dot_nt(w2[pl.ds(q * 256, 256), :], a2)
            for e in range(8):
                for u in range(2):
                    rows = pl.ds(pl.multiple_of((2 * t + u) * 32, 32), 32)
                    gmat[rows, pl.ds((q * 8 + e) * 128, 128)] = g[e * 32 : e * 32 + 32, u * 128 : u * 128 + 128].astype(
                        bf16
                    )

    own_adj.wait()
    loop(x * 2, x * 2 + 2, grad_pair)
    adjoint.waited = True
    for k in (1, 3, 2):
        xx = lax.rem(x + k, NX)
        adjoint.recv_one(xx)
        loop(xx * 2, xx * 2 + 2, grad_pair)

    def left_part(cc, yy):
        cols = quarter(cc, yy)
        lacc[...] += dot_nt(rmat[:, cols], gmat[:, cols])

    lplane.recv()
    lbrf[...] = lbr[...].reshape(512, 128).astype(f32)
    for zz in range(NZ):
        for xx in range(NX):
            lmat[pl.ds(zz * 16, 16), pl.ds(xx * 128, 128)] = lbrf[pl.ds(xx * 8 + zz, 16, stride=32), :].astype(bf16)
    for k in range(4):
        lt[pl.ds(k * 128, 128), :] = lmat[:, pl.ds(k * 128, 128)].astype(f32).T.astype(bf16)

    def columns(ref, yy):
        return ref.at[:, pl.ds(pl.multiple_of(yy * 1024, 1024), 1024)]

    def right_other(yy):
        def part(k):
            cols = pl.ds(pl.multiple_of(other * 2048 + yy * 1024 + k * 512, 512), 512)
            rgs[:, pl.ds(pl.multiple_of(yy * 1024 + k * 512, 512), 512)] = dot(lmat[...], gmat[:, cols]).astype(bf16)

        loop(0, 2, part)

    def right_own(yy):
        def part(k):
            cols = pl.ds(pl.multiple_of(core * 2048 + yy * 1024 + k * 512, 512), 512)
            rgo[:, pl.ds(pl.multiple_of(yy * 1024 + k * 512, 512), 512)] = dot(lmat[...], gmat[:, cols])

        loop(0, 2, part)

    add = [
        exchange(
            lambda body: body(0),
            core_dev,
            0,
            lambda _, yy=yy: columns(rgs, yy),
            lambda _, yy=yy: columns(rgr, yy),
            columns(rgr, yy),
        )
        for yy in (1 - y, y)
    ]
    right_other(1 - y)
    add[0].start()
    right_other(y)
    add[1].start()
    for k in FAR:
        forward(k)
    right_own(1 - y)
    right_own(y)
    add[0].recv()

    def right_add(k):
        cols = pl.ds(pl.multiple_of((1 - y) * 1024 + k * 512, 512), 512)
        ryq[:, pl.ds(pl.multiple_of(k * 512, 512), 512)] = (rgo[:, cols] + rgr[:, cols].astype(f32)).astype(bf16)

    loop(0, 2, right_add)

    def all_z(body):
        for k in (4, 3, 5, 2, 6, 1, 7, 0):
            body(lax.rem(z + k, NZ))

    ry = exchange(all_z, y_dev, None, lambda zz: ryq.at[zrows(zz), :], None, ryr, ry_r)
    ry.copy = lambda zz, _: pltpu.make_async_remote_copy(
        src_ref=ryq.at[zrows(zz), :],
        dst_ref=ryr.at[zrows(zz), :],
        send_sem=ry.ssem.at[0],
        recv_sem=ry_r.at[zz],
        device_id={"dap": y_dev(0)},
        device_id_type=MESH,
    )
    ry.start()
    add[1].recv()
    for k in NEAR:
        forward(k)
    for k in FAR:
        forward_y(k)
    lacc[...] = jnp.zeros((128, 512), f32)
    left_part(core, y)
    left_part(core, 1 - y)

    bright = exchange(
        zs, z_dev, z, lambda zz: rz.at[zrows(zz), :], lambda zz: rzr.at[zz], rzr.at[pl.ds(0, NZ - 1)]
    )
    mine = pl.ds(pl.multiple_of(y * 1024, 1024), 1024)
    ry.waited = True

    def right_rows(k):
        zz = lax.rem(z + k, NZ)
        ry.recv_one(zz)
        t = rgo[zrows(zz), mine] + rgr[zrows(zz), mine].astype(f32) + ryr[zrows(zz), :].astype(f32)
        if k == 0:
            rzr[z] = t.astype(bf16)
        else:
            rz[zrows(zz), :] = t.astype(bf16)
            bright.start_one(zz)

    for k in (4, 3, 5):
        right_rows(k)
    swap.recv()
    left_part(other, y)
    left_part(other, 1 - y)
    lgs[...] = (lacc[...] * (1.0 / ROWS)).astype(bf16)
    bleft = exchange(
        zs, z_dev, z, lambda zz: lgs.at[zrows(zz), :], lambda zz: lzr.at[zz], lzr.at[pl.ds(0, NZ - 1)]
    )
    bleft.start()
    lzr[z] = lgs[zrows(z), :]


    def outer_part(n):
        o = dot(lt[...], rmat[:, pl.ds(pl.multiple_of(n * 256, 256), 256)])
        for i in range(16):
            for e in range(2):
                rows = pl.ds(pl.multiple_of((2 * n + e) * 32, 32), 32)
                xmat[rows, pl.ds(i * 128, 128)] = o[i * 32 : i * 32 + 32, e * 128 : e * 128 + 128].astype(bf16)

    for n, ks in enumerate([(2, 6), (1, 7), (0,), ()]):
        for k in ks:
            right_rows(k)
        loop(n * 4, n * 4 + 4, outer_part)

    def w_part(n):
        rows = pl.ds(pl.multiple_of(n * 256, 256), 256)
        wpart[rows, :] = dot(xmat[rows, :], amat[...].reshape(2048, 128))

    loop(0, 4, w_part)
    for c in range(CH):
        wsend[c // 2, pl.ds((c % 2) * 32, 32), :] = wpart[pl.ds(c, 32, stride=32), :].astype(bf16)
    wplane = exchange(planes, plane_dev, m, lambda mm: wsend.at[mm], lambda mm: wrecv.at[mm], wrecv.at[pl.ds(0, NM - 1)])
    wplane.start()
    wrecv[m] = wsend[m]

    bright.recv()
    bleft.recv()
    bsf[...] = jnp.zeros((768, 128), f32)
    for d in range(8):
        t = rzr[0, :, pl.ds(d * 128, 128)].astype(f32)
        for zz in range(1, NZ):
            t = t + rzr[zz, :, pl.ds(d * 128, 128)].astype(f32)
        bsf[pl.ds(32 + d, 16, stride=48), :] = t
    for zz in range(NZ):
        for xx in range(NX):
            bsf[pl.ds(xx * 8 + zz, 16, stride=48), :] = lzr[zz, :, pl.ds(xx * 128, 128)].astype(f32)
    loop(0, NM, lambda k: bs.__setitem__(k, bsf[pl.ds(pl.multiple_of(k * 48, 48), 48), :].astype(bf16)))
    back = exchange(planes, plane_dev, m, lambda mm: bs.at[mm], lambda mm: br.at[mm], br.at[pl.ds(0, NM - 1)])
    back.start()
    br[m] = bs[m]

    def delta_pair(t):
        p = dot(w2t[...], xmat[:, pl.ds(pl.multiple_of(t * 256, 256), 256)])
        pdb[pl.ds(t * 2, 2)] = (p.T + fbias[...]).astype(bf16).reshape(2, 128, 128)

    loop(0, 8, delta_pair)

    def out_part(xx):
        return pd_out.at[:, pl.ds(pl.multiple_of(xx * 128, 128), 128), :]

    delta = exchange(xs, x_dev, x, lambda xx: pdb.at[pl.ds(xx * 4, 4)], out_part, pd_out.at[:, pl.ds(0, 384), :])
    delta.start()
    pd_out[:, pl.ds(pl.multiple_of(x * 128, 128), 128), :] = pdb[pl.ds(x * 4, 4)]

    back.recv()
    for yy in range(2):
        for cc in range(2):
            t = None
            for xx in range(NX):
                v = br[yy * 8 + xx * 2 + cc, pl.ds(0, 32), :].astype(f32)
                t = v if t is None else t + v
            for xx in range(NX):
                lgf[pl.ds(yy * 8 + xx * 2 + cc, 8, stride=16), :] = t[xx * 8 : xx * 8 + 8, :]
    lg = lgf[...]
    rparts = []
    for cc in range(2):
        for yy in range(2):
            row = [br[yy * 8 + xx * 2 + cc, pl.ds(32, 16), :].astype(f32)[:8] for xx in range(NX)]
            rparts.append(jnp.concatenate(row, axis=1))
    rg = jnp.concatenate(rparts, axis=0)
    lgb = lg.astype(bf16)
    lgt = lgb.astype(f32).T
    lcat = jnp.concatenate([lgt[r * 32 : r * 32 + 32, :] for r in range(4)], axis=1).astype(bf16)
    rgb = rg.astype(bf16)
    pleft = dot(lcat, np_[...])
    pright = dot(rgb, nb[...])
    for h in range(2):
        cols = slice(h * 128, h * 128 + 128)
        for k in range(4):
            psend[h * 8 + k] = pleft[k * 8 : k * 8 + 8, cols]
            psend[h * 8 + 4 + k] = pright[k * 8 : k * 8 + 8, cols]
    pplane = exchange(planes, plane_dev, m, lambda mm: psend.at[mm], lambda mm: precv.at[mm], precv.at[pl.ds(0, NM - 1)])
    pplane.start()
    precv[m] = psend[m]

    wplane.recv()
    t = wrecv[0].astype(f32)
    for mm in range(1, NM):
        t = t + wrecv[mm].astype(f32)
    wzs[...] = t.astype(bf16)
    wz = exchange(zs, z_dev, z, lambda zz: wzs, lambda zz: wzr.at[zz], wzr.at[pl.ds(0, NZ - 1)])
    wz.start()
    wzr[z] = wzs[...]

    row_r = lax.broadcasted_iota(jnp.int32, (128, 256), 0) >> 5
    for r in range(4):
        v = dot(lgb, jnp.where(row_r == r, wl4t[...].astype(f32), 0.0).astype(bf16))
        for g in range(16):
            for h in range(2):
                ng[h, pl.ds((g % 2) * 256 + (g // 2) * 32 + r, 8, stride=4), :] = v[
                    g * 8 : g * 8 + 8, h * 128 : h * 128 + 128
                ]
    nr = dot(rgb.astype(f32).T.astype(bf16), wrt[...])
    ng[0] = ng[0] + nr[:, :128]
    ng[1] = ng[1] + nr[:, 128:]

    pplane.recv()
    t = precv[0]
    for mm in range(1, NM):
        t = t + precv[mm]
    pzs[...] = t
    pz = exchange(zs, z_dev, z, lambda zz: pzs, lambda zz: pzr.at[zz], pzr.at[pl.ds(0, NZ - 1)])
    pz.start()
    pzr[z] = t
    def back_rows(k):
        rows = pl.ds(pl.multiple_of(k * 64, 64), 64)
        hid = jnp.concatenate([ng[0, rows, :], ng[1, rows, :]], axis=1) * stretch[...]
        sc = scaled[rows, :]
        iv = inv[rows, :][:, :1]
        g = iv * (
            hid - jnp.mean(hid, axis=-1, keepdims=True) - sc * jnp.mean(hid * sc, axis=-1, keepdims=True)
        )
        ag_out[0, rows, :] = g.astype(bf16)

    loop(0, 8, back_rows)
    ag_copy = pltpu.make_async_copy(ag_out, ag_h, in_sem.at[0])
    ag_copy.start()

    wz.recv()
    t = wzr[0].astype(f32)
    for zz in range(1, NZ):
        t = t + wzr[zz].astype(f32)
    wfin[...] = (t * (math.sqrt(ROWS) / RES)).astype(bf16)
    wall = exchange(
        planes, plane_dev, m, lambda mm: wfin, lambda mm: wall_v.at[mm], wall_v.at[pl.ds(0, NM - 1)]
    )
    wall.start()
    wall_v[m] = wfin[...]

    pz.recv()
    t = pzr[0]
    for zz in range(1, NZ):
        t = t + pzr[zz]
    t = t * (1.0 / RES)
    pgs[...] = t
    pall = exchange(planes, plane_dev, m, lambda mm: pgs, lambda mm: pgr.at[mm], pgr.at[pl.ds(0, NM - 1)])
    pall.start()
    pgr[m] = t

    delta.recv()
    pd_copy = pltpu.make_async_copy(pd_out, pd_h, in_sem.at[1])
    pd_copy.start()
    wall.recv()
    wo_out[...] = wall_v[...].reshape(1024, 128).astype(f32)
    wo_copy = pltpu.make_async_copy(wo_out, wo_h, in_sem.at[2])
    wo_copy.start()
    pall.recv()
    pt = pgr[...].reshape(2, 64, 128)
    pg_out[:, pl.ds(0, 128)] = pt[0]
    pg_out[:, pl.ds(128, 128)] = pt[1]
    pg_copy = pltpu.make_async_copy(pg_out, pg_h, in_sem.at[3])
    pg_copy.start()
    finish()
    for c in (ag_copy, pd_copy, wo_copy, pg_copy):
        c.wait()


def emit(pd, ag, pg, wo, pd_o, ag_o, pg_o, wo_o, pd_v, ag_v, pg_v, wo_v, sems):
    parts = [(pd.at[k], pd_v.at[k], pd_o.at[k]) for k in range(4)]
    parts += [(ag, ag_v, ag_o), (pg, pg_v, pg_o), (wo, wo_v, wo_o)]
    for k, (src, mid, _) in enumerate(parts):
        pltpu.make_async_copy(src, mid, sems.at[k]).start()
    for k, (src, mid, dst) in enumerate(parts):
        pltpu.make_async_copy(src, mid, sems.at[k]).wait()
        pltpu.make_async_copy(mid, dst, sems.at[k]).start()
    for k, (_, mid, dst) in enumerate(parts):
        pltpu.make_async_copy(mid, dst, sems.at[k]).wait()


def shards(msa, stretch, shift, wlr, offs, wf, fbias, adj):
    def vm(shape, dtype):
        return pltpu.VMEM(shape, dtype)

    def sem(*n):
        return pltpu.SemaphoreType.DMA(n)

    scratch = [
        vm((4, 512, 128), bf16), vm((1, 512, 256), bf16), vm((64, 256), f32), vm((1024, 128), f32),
        vm((1, 512, 256), bf16), vm((1, 256), f32), vm((1, 256), f32), vm((64, 256), bf16), vm((1, 64), f32),
        vm((1024, 128), bf16), vm((1, 128), f32), vm((4, 512, 128), bf16),
        vm((512, 256), f32), vm((512, 128), f32), vm((2, 512, 128), f32), vm((512, 256), bf16), vm((512, 256), bf16),
        vm((128, 256), bf16), vm((32, 256), bf16), vm((32, 512), bf16),
        vm((16, 16, 128), bf16), vm((16, 16, 128), bf16), vm((256, 128), f32), vm((8, 16, 128), bf16),
        vm((8, 16, 128), bf16), vm((128, 128), f32), vm((128, 128), f32), vm((4, 32, 128), bf16), vm((16, 32, 128), bf16),
        vm((512, 128), f32), vm((128, 128), f32),
        vm((16, 2048), bf16), vm((128, 512), bf16), vm((512, 128), bf16), vm((128, 4096), bf16),
        vm((16, 128, 128), bf16), vm((1024, 128), f32), vm((1024, 128), bf16), vm((128, 1024), bf16),
        vm((512, 4096), bf16), vm((1024, 2048), bf16), vm((128, 2048), bf16), vm((128, 2048), bf16),
        vm((128, 2048), f32), vm((128, 1024), bf16), vm((128, 1024), bf16), vm((128, 1024), bf16),
        vm((8, 16, 1024), bf16), vm((128, 512), f32),
        vm((128, 512), bf16), vm((8, 16, 512), bf16), vm((768, 128), f32), vm((16, 48, 128), bf16),
        vm((16, 48, 128), bf16), vm((2, 512, 128), f32),
        vm((1024, 128), f32), vm((16, 64, 128), bf16), vm((16, 64, 128), bf16), vm((64, 128), bf16),
        vm((8, 64, 128), bf16), vm((64, 128), bf16), vm((16, 64, 128), bf16), vm((16, 128, 128), bf16),
        vm((16, 8, 128), f32), vm((16, 8, 128), f32), vm((8, 128), f32), vm((8, 8, 128), f32), vm((8, 128), f32),
        vm((16, 8, 128), f32),
        sem(8), pltpu.SemaphoreType.DMA, sem(24), sem(24), sem(4), sem(8), sem(8), sem(8),
    ]
    pd, ag, pg, wo = pl.pallas_call(
        kernel,
        out_shape=(
            jax.ShapeDtypeStruct((4, 512, 128), bf16),
            jax.ShapeDtypeStruct((1, 512, 256), bf16),
            jax.ShapeDtypeStruct((64, 256), f32),
            jax.ShapeDtypeStruct((1024, 128), f32),
        ),
        in_specs=[pl.BlockSpec(memory_space=pltpu.HBM)] * 8,
        out_specs=(pl.BlockSpec(memory_space=pltpu.HBM),) * 4,
        scratch_shapes=scratch,
        compiler_params=pltpu.CompilerParams(
            collective_id=0, has_side_effects=True, vmem_limit_bytes=60 * 1024 * 1024
        ),
    )(
        msa,
        stretch.reshape(1, 256),
        shift.reshape(1, 256),
        wlr.T,
        offs.reshape(1, 64),
        wf,
        fbias.reshape(1, 128),
        adj,
    )
    pd, ag, pg, wo = pl.pallas_call(
        emit,
        out_shape=tuple(jax.ShapeDtypeStruct(v.shape, v.dtype) for v in (pd, ag, pg, wo)),
        in_specs=[pl.BlockSpec(memory_space=pltpu.HBM)] * 4,
        out_specs=(pl.BlockSpec(memory_space=pltpu.HBM),) * 4,
        scratch_shapes=[vm((4, 512, 128), bf16), vm((1, 512, 256), bf16), vm((64, 256), f32), vm((1024, 128), f32), sem(7)],
        compiler_params=pltpu.CompilerParams(vmem_limit_bytes=60 * 1024 * 1024),
    )(pd, ag, pg, wo)
    return pd, ag, pg.T, wo


def solution(mesh):
    placed = (P("dap", "crop", None), P(), P(), P(), P(), P(), P(), P("dap", "crop", None))
    return jax.shard_map(
        shards,
        mesh=mesh,
        in_specs=placed,
        out_specs=(
            P("dap", "crop", None),
            P("dap", "crop", None),
            P("crop", None),
            P("crop", None),
        ),
        check_vma=False,
    )
```

```python
import math

import jax
import jax.numpy as jnp
from jax import lax
from jax.experimental import pallas as pl
from jax.experimental.pallas import tpu as pltpu
from jax.sharding import PartitionSpec as P

EPSILON = 1e-05
MESH = pl.DeviceIdType.MESH
f32 = jnp.float32
bf16 = jnp.bfloat16

NX, NZ, NM = 4, 8, 16
CH = 32
ROWS = 128
RES = 512
FAR = (4, 3, 5)
NEAR = (2, 6, 1, 7)


def dot(a, b):
    return jnp.dot(a, b, preferred_element_type=f32)


def dot_nt(a, b):
    return lax.dot_general(a, b, (((1,), (1,)), ((), ())), preferred_element_type=f32)


def loop(low, high, body):
    def step(k, carry):
        body(k)
        return carry

    lax.fori_loop(low, high, step, 0)


class Exchange:
    def __init__(self, each, device, mine, src, dst, whole, ssem, rsem, apart=False):
        self.each, self.device, self.mine, self.src, self.dst, self.whole = each, device, mine, src, dst, whole
        self.ssem, self.rsem, self.apart = ssem, rsem, apart
        self.waited = False

    def copy(self, p, slot):
        return pltpu.make_async_remote_copy(
            src_ref=self.src(p),
            dst_ref=self.dst(slot),
            send_sem=self.ssem.at[0],
            recv_sem=self.rsem.at[slot if self.apart else 0],
            device_id={"dap": self.device(p)},
            device_id_type=MESH,
        )

    def bulk(self):
        return pltpu.make_async_remote_copy(
            src_ref=self.whole,
            dst_ref=self.whole,
            send_sem=self.ssem.at[0],
            recv_sem=self.rsem.at[0],
            device_id={"dap": self.device(0)},
            device_id_type=MESH,
        )

    def start_one(self, p):
        self.copy(p, self.mine).start()

    def recv_one(self, p):
        self.copy(p, p).wait_recv()

    def start(self):
        self.each(self.start_one)

    def recv(self):
        self.waited = True
        if self.apart:
            self.each(self.recv_one)
        else:
            self.bulk().wait_recv()

    def sent(self):
        self.bulk().wait_send()


def kernel(
    msa_h, stretch_h, shift_h, wlrt_h, offs_h, wf_h, fbias_h, adj_h,
    pd_h, ag_h, pg_h, wo_h,
    pd_out, ag_out, pg_out, wo_out,
    msa, stretch, shift, wlrt_v, offs, wf, fbias, adj,
    scaled, inv, nf, nb, np_, wl4t, wrt, rt,
    sb, rb, rbf, las, la, laf, lbf, lb, lbr, lbrf, rs, lmat, lt, rmat, amat, wff, w2, w2t,
    gmat, xmat, rgs, rgr, rgo, ryq, ryr, rz, rzf, rzn, rsum, lacc, lgp, lgs, lgr, lzf, lzs, lzr, bsf, bs, br, ng,
    wpart, wsend, wrecv, wzs, wzr, wfin, wall_v, pdb,
    psend, precv, pzs, pzr, pgs, pgr,
    in_sem, adj_sem, ssems, rsems, adj_r, zr_r, yf_r, ry_r,
):
    me = lax.axis_index("dap")
    core = lax.rem(me, 2)
    x = lax.rem(me // 2, NX)
    z = lax.rem(me // 8, NZ)
    y = me // 64
    m = y * 8 + x * 2 + core
    other = 1 - core

    def plane_dev(mm):
        return (mm // 8) * 64 + z * 8 + lax.rem(mm, 8)

    def z_dev(zz):
        return y * 64 + zz * 8 + x * 2 + core

    def x_dev(xx):
        return y * 64 + z * 8 + xx * 2 + core

    def core_dev(_):
        return y * 64 + z * 8 + x * 2 + other

    def y_dev(_):
        return (1 - y) * 64 + z * 8 + x * 2 + core

    def planes(body):
        loop(1, NM, lambda k: body(lax.rem(m + k, NM)))

    def zs(body):
        for k in (4, 3, 5, 2, 6, 1, 7):
            body(lax.rem(z + k, NZ))

    def zs_far(body):
        for k in FAR:
            body(lax.rem(z + k, NZ))

    def zs_near(body):
        for k in NEAR:
            body(lax.rem(z + k, NZ))

    def xs(body):
        for k in (1, 3, 2):
            body(lax.rem(x + k, NX))

    exchanges = []

    def exchange(each, device, mine, src, dst, whole, rsem=None):
        k = pl.ds(len(exchanges), 1)
        e = Exchange(
            each, device, mine, src, dst, whole, ssems.at[k], rsems.at[k] if rsem is None else rsem, rsem is not None
        )
        exchanges.append(e)
        return e

    def finish():
        for e in exchanges:
            if not e.waited:
                e.recv()
        for e in exchanges:
            e.sent()

    small = [
        pltpu.make_async_copy(src, dst, in_sem.at[k])
        for k, (src, dst) in enumerate(
            [
                (msa_h, msa), (stretch_h, stretch), (shift_h, shift), (wlrt_h, wlrt_v), (offs_h, offs),
                (wf_h, wf), (fbias_h, fbias), (adj_h, adj),
            ]
        )
    ]
    for c in small:
        c.start()

    def adj_part(xx):
        return adj.at[:, pl.ds(pl.multiple_of(xx * 128, 128), 128), :]

    def own_i(xx):
        return amat.at[pl.ds(xx * 4, 4)]


    barrier = pltpu.get_barrier_semaphore()
    planes(lambda mm: pl.semaphore_signal(barrier, inc=1, device_id={"dap": plane_dev(mm)}, device_id_type=MESH))
    zs(lambda zz: pl.semaphore_signal(barrier, inc=1, device_id={"dap": z_dev(zz)}, device_id_type=MESH))
    for c in small:
        c.wait()

    def norm_rows(k):
        rows = pl.ds(pl.multiple_of(k * 64, 64), 64)
        v = msa[0, rows, :].astype(f32)
        c = v - jnp.mean(v, axis=-1, keepdims=True)
        iv = lax.rsqrt(jnp.mean(c * c, axis=-1, keepdims=True) + EPSILON)
        sc = c * iv
        scaled[rows, :] = sc
        inv[rows, :] = jnp.broadcast_to(iv, (64, 128))
        n = (sc * stretch[...] + shift[...]).astype(bf16)
        nb[rows, :] = n
        n = n.astype(f32)
        nf[0, rows, :] = n[:, :128]
        nf[1, rows, :] = n[:, 128:]

    loop(0, 8, norm_rows)
    for r in range(4):
        for zz in range(NZ):
            v = [
                jnp.concatenate([nf[h, pl.ds(yy * 256 + zz * 32 + r, 8, stride=4), :] for h in range(2)], axis=1)
                for yy in range(2)
            ]
            np_[pl.ds(r * 128 + zz * 16, 16), :] = jnp.concatenate(v, axis=0).astype(bf16)

    wlrt = wlrt_v[...]
    w_rows = wlrt.astype(f32).T.astype(bf16)
    wrt[...] = wlrt[CH:, :]
    spread = lax.broadcasted_iota(jnp.int32, (64, 128), 0) == (lax.broadcasted_iota(jnp.int32, (64, 128), 1) & 31)
    wl4 = dot(w_rows, spread.astype(f32).astype(bf16))
    wl4t[...] = wl4.T.astype(bf16)
    diag = lax.broadcasted_iota(jnp.int32, (64, 64), 0) == lax.broadcasted_iota(jnp.int32, (64, 64), 1)
    offs_col = jnp.sum(jnp.where(diag, jnp.broadcast_to(offs[...], (64, 64)), 0.0), axis=1, keepdims=True)
    offs4 = jnp.sum(jnp.where(spread, jnp.broadcast_to(offs_col, (64, 128)), 0.0), axis=0, keepdims=True)
    lane_r = lax.broadcasted_iota(jnp.int32, (256, 128), 1) >> 5
    left = jnp.zeros((128, 128), f32)
    for r in range(4):
        left = left + dot(np_[pl.ds(r * 128, 128), :], jnp.where(lane_r == r, wl4, 0.0).astype(bf16))
    left = (left + offs4).astype(bf16).astype(f32) * (1.0 / ROWS)
    las[...] = left.astype(bf16).reshape(NZ, NM, 128)
    rt[...] = (dot_nt(wlrt[CH:, :], nb[...]) + offs_col[CH:, :]).astype(bf16)
    for mm in range(NM):
        xx, cc = (mm % 8) // 2, mm % 2
        sb[mm] = rt[pl.ds(cc * 16, 16), pl.ds(xx * 128, 128)]

    pl.semaphore_wait(barrier, NM - 1 + NZ - 1)

    first = exchange(planes, plane_dev, m, lambda mm: sb.at[mm], lambda mm: rb.at[mm], rb.at[pl.ds(0, NM - 1)])
    first.start()
    rb[m] = sb[m]
    zleft = exchange(zs, z_dev, z, lambda zz: las.at[zz], lambda zz: la.at[zz], la.at[pl.ds(0, NZ - 1)])
    zleft.start()
    la[z] = las[z]
    adjoint = exchange(xs, x_dev, x, adj_part, own_i, amat.at[pl.ds(0, 12)], adj_r)
    adjoint.start()
    own_adj = pltpu.make_async_copy(adj_part(x), own_i(x), adj_sem)
    own_adj.start()

    wff[...] = wf[...].astype(f32)
    for d in range(CH):
        w2[pl.ds(d * 32, 32), :] = wff[pl.ds(d, 32, stride=32), :].astype(bf16)
    for k in range(8):
        w2t[:, pl.ds(k * 128, 128)] = w2[pl.ds(k * 128, 128), :].astype(f32).T.astype(bf16)

    first.recv()

    rbf[...] = rb[...].reshape(256, 128).astype(f32)
    for d in range(16):
        rs[:, pl.ds(d * 128, 128)] = rbf[pl.ds(d, 16, stride=16), :].astype(bf16)

    def zrows(zz):
        return pl.ds(pl.multiple_of(zz * 16, 16), 16)

    def half(cc):
        return pl.ds(pl.multiple_of(cc * 2048, 2048), 2048)

    def quarter(cc, yy):
        return pl.ds(pl.multiple_of(cc * 2048 + yy * 1024, 1024), 1024)

    def r_piece(zz, yy):
        return rmat.at[zrows(zz), quarter(core, yy)]

    rs_own = rs.at[:, pl.ds(pl.multiple_of(y * 1024, 1024), 1024)]
    zfar = exchange(
        zs_far, z_dev, z, lambda zz: rs_own, lambda zz: r_piece(zz, y), rmat.at[pl.ds(0, 16 * len(FAR)), quarter(0, 0)], zr_r
    )
    znear = exchange(
        zs_near, z_dev, z, lambda zz: rs, lambda zz: rmat.at[zrows(zz), half(core)], rmat.at[pl.ds(0, 16 * len(NEAR)), half(0)], zr_r
    )
    zfar.start()
    znear.start()
    rmat[zrows(z), half(core)] = rs[...]

    zleft.recv()
    laf[...] = la[...].reshape(128, 128).astype(f32)
    for mm in range(0, NM, 2):
        for cc in range(2):
            yc, xx = (mm // 8) * 2 + cc, (mm % 8) // 2
            lbf[pl.ds(yc * 32 + xx * 8, 8), :] = laf[pl.ds(mm + cc, 8, stride=16), :]
    lb[...] = lbf[...].astype(bf16).reshape(4, 32, 128)
    lplane = exchange(
        planes,
        plane_dev,
        m,
        lambda mm: lb.at[(mm // 8) * 2 + lax.rem(mm, 2)],
        lambda mm: lbr.at[mm],
        lbr.at[pl.ds(0, NM - 1)],
    )
    lplane.start()
    lbr[m] = lb[y * 2 + core]

    yswap = exchange(
        zs_far, y_dev, None, lambda zz: r_piece(zz, y), None, rmat.at[pl.ds(0, 16 * len(FAR)), quarter(0, 0)], yf_r
    )
    swap = exchange(None, core_dev, None, None, None, rmat.at[:, half(other)])

    def to_core(piece):
        pltpu.make_async_remote_copy(
            src_ref=piece,
            dst_ref=piece,
            send_sem=swap.ssem.at[0],
            recv_sem=swap.rsem.at[0],
            device_id={"dap": core_dev(0)},
            device_id_type=MESH,
        ).start()

    def y_copy(zz, yy):
        return pltpu.make_async_remote_copy(
            src_ref=r_piece(zz, yy),
            dst_ref=r_piece(zz, yy),
            send_sem=yswap.ssem.at[0],
            recv_sem=yf_r.at[zz],
            device_id={"dap": y_dev(0)},
            device_id_type=MESH,
        )

    yswap.recv_one = lambda zz: y_copy(zz, 1 - y).wait_recv()

    def forward(k):
        zz = lax.rem(z + k, NZ)
        if k in FAR:
            zfar.recv_one(zz)
            y_copy(zz, y).start()
            to_core(r_piece(zz, y))
        else:
            znear.recv_one(zz)
            to_core(rmat.at[zrows(zz), half(core)])

    def forward_y(k):
        zz = lax.rem(z + k, NZ)
        yswap.recv_one(zz)
        to_core(r_piece(zz, 1 - y))

    to_core(rmat.at[zrows(z), half(core)])
    zfar.waited = True
    znear.waited = True
    yswap.waited = True

    def grad_pair(t):
        a2 = amat[pl.ds(t * 2, 2)].reshape(256, 128)
        for q in range(4):
            g = dot_nt(w2[pl.ds(q * 256, 256), :], a2)
            for e in range(8):
                for u in range(2):
                    rows = pl.ds(pl.multiple_of((2 * t + u) * 32, 32), 32)
                    gmat[rows, pl.ds((q * 8 + e) * 128, 128)] = g[e * 32 : e * 32 + 32, u * 128 : u * 128 + 128].astype(
                        bf16
                    )

    own_adj.wait()
    loop(x * 2, x * 2 + 2, grad_pair)
    adjoint.waited = True
    for k in (1, 3, 2):
        xx = lax.rem(x + k, NX)
        adjoint.recv_one(xx)
        loop(xx * 2, xx * 2 + 2, grad_pair)

    def left_part(cc, yy):
        cols = quarter(cc, yy)
        t = dot_nt(rmat[:, cols], gmat[:, cols])
        for xx in range(NX):
            lacc[xx] += t[:, xx * 128 : xx * 128 + 128]

    lplane.recv()
    lbrf[...] = lbr[...].reshape(512, 128).astype(f32)
    for zz in range(NZ):
        for xx in range(NX):
            lmat[pl.ds(zz * 16, 16), pl.ds(xx * 128, 128)] = lbrf[pl.ds(xx * 8 + zz, 16, stride=32), :].astype(bf16)
    for k in range(4):
        lt[pl.ds(k * 128, 128), :] = lmat[:, pl.ds(k * 128, 128)].astype(f32).T.astype(bf16)

    def columns(ref, yy):
        return ref.at[:, pl.ds(pl.multiple_of(yy * 1024, 1024), 1024)]

    def right_other(yy):
        def part(k):
            cols = pl.ds(pl.multiple_of(other * 2048 + yy * 1024 + k * 512, 512), 512)
            rgs[:, pl.ds(pl.multiple_of(yy * 1024 + k * 512, 512), 512)] = dot(lmat[...], gmat[:, cols]).astype(bf16)

        loop(0, 2, part)

    def right_own(yy):
        def part(k):
            cols = pl.ds(pl.multiple_of(core * 2048 + yy * 1024 + k * 512, 512), 512)
            rgo[:, pl.ds(pl.multiple_of(yy * 1024 + k * 512, 512), 512)] = dot(lmat[...], gmat[:, cols])

        loop(0, 2, part)

    add = [
        exchange(
            lambda body: body(0),
            core_dev,
            0,
            lambda _, yy=yy: columns(rgs, yy),
            lambda _, yy=yy: columns(rgr, yy),
            columns(rgr, yy),
        )
        for yy in (1 - y, y)
    ]
    right_other(1 - y)
    add[0].start()
    right_other(y)
    add[1].start()
    for k in FAR:
        forward(k)
    right_own(1 - y)
    right_own(y)
    add[0].recv()

    ry = exchange(
        zs_far, y_dev, None, lambda zz: ryq.at[zrows(zz), :], None, ryr.at[pl.ds(0, 16 * len(FAR)), :], ry_r
    )
    ry.copy = lambda zz, _: pltpu.make_async_remote_copy(
        src_ref=ryq.at[zrows(zz), :],
        dst_ref=ryr.at[zrows(zz), :],
        send_sem=ry.ssem.at[0],
        recv_sem=ry_r.at[zz],
        device_id={"dap": y_dev(0)},
        device_id_type=MESH,
    )
    theirs = pl.ds(pl.multiple_of((1 - y) * 1024, 1024), 1024)
    mine = pl.ds(pl.multiple_of(y * 1024, 1024), 1024)
    for k in FAR:
        rows = zrows(lax.rem(z + k, NZ))
        ryq[rows, :] = (rgo[rows, theirs] + rgr[rows, theirs].astype(f32)).astype(bf16)
        ry.start_one(lax.rem(z + k, NZ))
    bfar = exchange(
        zs_far, z_dev, z, lambda zz: rz.at[zrows(zz), mine], lambda zz: rzf.at[zz], rzf.at[pl.ds(0, len(FAR))]
    )
    bnear = exchange(
        zs_near, z_dev, z, lambda zz: rz.at[zrows(zz), :], lambda zz: rzn.at[zz], rzn.at[pl.ds(0, len(NEAR))]
    )
    add[1].recv()
    for k in NEAR:
        rows = zrows(lax.rem(z + k, NZ))
        rz[rows, :] = (rgo[rows, :] + rgr[rows, :].astype(f32)).astype(bf16)
        bnear.start_one(lax.rem(z + k, NZ))
    for k in NEAR:
        forward(k)
    for k in FAR:
        forward_y(k)
    lacc[...] = jnp.zeros((NX, 128, 128), f32)
    left_part(core, y)
    left_part(core, 1 - y)

    ry.waited = True

    def right_rows(k):
        zz = lax.rem(z + k, NZ)
        rows = zrows(zz)
        ry.recv_one(zz)
        rz[rows, mine] = (rgo[rows, mine] + rgr[rows, mine].astype(f32) + ryr[rows, :].astype(f32)).astype(bf16)
        bfar.start_one(zz)

    for k in FAR[:3]:
        right_rows(k)
    swap.recv()
    left_part(other, y)
    left_part(other, 1 - y)
    for xx in range(NX):
        for mm in range(NM):
            lgp[mm, pl.ds(xx * 8, 8), :] = lacc[xx, pl.ds(mm, 8, stride=16), :]
    lgs[...] = (lgp[...] * (1.0 / ROWS)).astype(bf16)
    bleft = exchange(planes, plane_dev, m, lambda mm: lgs.at[mm], lambda mm: lgr.at[mm], lgr.at[pl.ds(0, NM - 1)])
    bleft.start()
    lgr[m] = lgs[m]

    def outer_part(n):
        o = dot(lt[...], rmat[:, pl.ds(pl.multiple_of(n * 256, 256), 256)])
        for i in range(16):
            for e in range(2):
                rows = pl.ds(pl.multiple_of((2 * n + e) * 32, 32), 32)
                xmat[rows, pl.ds(i * 128, 128)] = o[i * 32 : i * 32 + 32, e * 128 : e * 128 + 128].astype(bf16)

    for n, ks in enumerate([FAR[3:4], FAR[4:], (), ()]):
        for k in ks:
            right_rows(k)
        loop(n * 4, n * 4 + 4, outer_part)

    bleft.recv()
    for yc in range(4):
        t = None
        for xx in range(NX):
            v = lgr[(yc // 2) * 8 + xx * 2 + yc % 2].astype(f32)
            t = v if t is None else t + v
        for xx in range(NX):
            lzf[pl.ds((yc // 2) * 8 + xx * 2 + yc % 2, 8, stride=16), :] = t[xx * 8 : xx * 8 + 8, :]
    lzs[...] = lzf[...].astype(bf16).reshape(NZ, NM, 128)
    bzl = exchange(zs, z_dev, z, lambda zz: lzs.at[zz], lambda zz: lzr.at[zz], lzr.at[pl.ds(0, NZ - 1)])
    bzl.start()
    lzr[z] = lzs[z]

    bnear.recv()
    bfar.recv()
    rows = zrows(z)
    t = rgo[rows, :] + rgr[rows, :].astype(f32)
    for k in NEAR:
        t = t + rzn[lax.rem(z + k, NZ)].astype(f32)
    rsum[...] = t
    t = rsum[:, mine]
    for k in FAR:
        t = t + rzf[lax.rem(z + k, NZ)].astype(f32)
    rsum[:, mine] = t
    for d in range(16):
        bsf[pl.ds(d, 16, stride=16), :] = rsum[:, pl.ds(d * 128, 128)]
    bs[...] = bsf[...].astype(bf16).reshape(NM, 16, 128)
    back = exchange(planes, plane_dev, m, lambda mm: bs.at[mm], lambda mm: br.at[mm], br.at[pl.ds(0, NM - 1)])
    back.start()
    br[m] = bs[m]

    def w_part(n):
        rows = pl.ds(pl.multiple_of(n * 256, 256), 256)
        wpart[rows, :] = dot(xmat[rows, :], amat[...].reshape(2048, 128))

    loop(0, 4, w_part)
    for c in range(CH):
        wsend[c // 2, pl.ds((c % 2) * 32, 32), :] = wpart[pl.ds(c, 32, stride=32), :].astype(bf16)
    wplane = exchange(planes, plane_dev, m, lambda mm: wsend.at[mm], lambda mm: wrecv.at[mm], wrecv.at[pl.ds(0, NM - 1)])
    wplane.start()
    wrecv[m] = wsend[m]


    def delta_pair(t):
        p = dot(w2t[...], xmat[:, pl.ds(pl.multiple_of(t * 256, 256), 256)])
        pdb[pl.ds(t * 2, 2)] = (p.T + fbias[...]).astype(bf16).reshape(2, 128, 128)

    loop(0, 4, delta_pair)

    back.recv()
    bzl.recv()
    lg = lzr[...].reshape(128, 128).astype(f32)
    rparts = []
    for cc in range(2):
        row = [br[xx * 2 + cc].astype(f32) + br[8 + xx * 2 + cc].astype(f32) for xx in range(NX)]
        rparts.append(jnp.concatenate(row, axis=1))
    rg = jnp.concatenate(rparts, axis=0)
    lgb = lg.astype(bf16)
    lgt = lgb.astype(f32).T
    lcat = jnp.concatenate([lgt[r * 32 : r * 32 + 32, :] for r in range(4)], axis=1).astype(bf16)
    rgb = rg.astype(bf16)
    pleft = dot(lcat, np_[...])
    pright = dot(rgb, nb[...])
    for h in range(2):
        cols = slice(h * 128, h * 128 + 128)
        for k in range(4):
            psend[h * 8 + k] = pleft[k * 8 : k * 8 + 8, cols]
            psend[h * 8 + 4 + k] = pright[k * 8 : k * 8 + 8, cols]
    pplane = exchange(planes, plane_dev, m, lambda mm: psend.at[mm], lambda mm: precv.at[mm], precv.at[pl.ds(0, NM - 1)])
    pplane.start()
    precv[m] = psend[m]

    loop(4, 8, delta_pair)
    wplane.recv()
    t = wrecv[0].astype(f32)
    for mm in range(1, NM):
        t = t + wrecv[mm].astype(f32)
    wzs[...] = t.astype(bf16)
    wz = exchange(zs, z_dev, z, lambda zz: wzs, lambda zz: wzr.at[zz], wzr.at[pl.ds(0, NZ - 1)])
    wz.start()
    wzr[z] = wzs[...]

    row_r = lax.broadcasted_iota(jnp.int32, (128, 256), 0) >> 5
    for r in range(4):
        v = dot(lgb, jnp.where(row_r == r, wl4t[...].astype(f32), 0.0).astype(bf16))
        for g in range(16):
            for h in range(2):
                ng[h, pl.ds((g % 2) * 256 + (g // 2) * 32 + r, 8, stride=4), :] = v[
                    g * 8 : g * 8 + 8, h * 128 : h * 128 + 128
                ]
    nr = dot(rgb.astype(f32).T.astype(bf16), wrt[...])
    ng[0] = ng[0] + nr[:, :128]
    ng[1] = ng[1] + nr[:, 128:]

    pplane.recv()
    t = precv[0]
    for mm in range(1, NM):
        t = t + precv[mm]
    pzs[...] = t
    pz = exchange(zs, z_dev, z, lambda zz: pzs, lambda zz: pzr.at[zz], pzr.at[pl.ds(0, NZ - 1)])
    pz.start()
    pzr[z] = t

    def out_part(xx):
        return pd_out.at[:, pl.ds(pl.multiple_of(xx * 128, 128), 128), :]

    delta = exchange(xs, x_dev, x, lambda xx: pdb.at[pl.ds(xx * 4, 4)], out_part, pd_out.at[:, pl.ds(0, 384), :])
    delta.start()
    pd_out[:, pl.ds(pl.multiple_of(x * 128, 128), 128), :] = pdb[pl.ds(x * 4, 4)]

    def back_rows(k):
        rows = pl.ds(pl.multiple_of(k * 64, 64), 64)
        hid = jnp.concatenate([ng[0, rows, :], ng[1, rows, :]], axis=1) * stretch[...]
        sc = scaled[rows, :]
        iv = inv[rows, :][:, :1]
        g = iv * (
            hid - jnp.mean(hid, axis=-1, keepdims=True) - sc * jnp.mean(hid * sc, axis=-1, keepdims=True)
        )
        ag_out[0, rows, :] = g.astype(bf16)

    loop(0, 8, back_rows)
    ag_copy = pltpu.make_async_copy(ag_out, ag_h, in_sem.at[0])
    ag_copy.start()

    wz.recv()
    t = wzr[0].astype(f32)
    for zz in range(1, NZ):
        t = t + wzr[zz].astype(f32)
    wfin[...] = (t * (math.sqrt(ROWS) / RES)).astype(bf16)
    wall = exchange(
        planes, plane_dev, m, lambda mm: wfin, lambda mm: wall_v.at[mm], wall_v.at[pl.ds(0, NM - 1)]
    )
    wall.start()
    wall_v[m] = wfin[...]

    pz.recv()
    t = pzr[0]
    for zz in range(1, NZ):
        t = t + pzr[zz]
    t = t * (1.0 / RES)
    pgs[...] = t
    pall = exchange(planes, plane_dev, m, lambda mm: pgs, lambda mm: pgr.at[mm], pgr.at[pl.ds(0, NM - 1)])
    pall.start()
    pgr[m] = t

    wall.recv()
    wo_out[...] = wall_v[...].reshape(1024, 128).astype(f32)
    wo_copy = pltpu.make_async_copy(wo_out, wo_h, in_sem.at[2])
    wo_copy.start()
    delta.recv()
    pd_copy = pltpu.make_async_copy(pd_out, pd_h, in_sem.at[1])
    pd_copy.start()
    pall.recv()
    pt = pgr[...].reshape(2, 64, 128)
    pg_out[:, pl.ds(0, 128)] = pt[0]
    pg_out[:, pl.ds(128, 128)] = pt[1]
    pg_copy = pltpu.make_async_copy(pg_out, pg_h, in_sem.at[3])
    pg_copy.start()
    finish()
    for c in (ag_copy, pd_copy, wo_copy, pg_copy):
        c.wait()


def emit(pd, ag, pg, wo, pd_o, ag_o, pg_o, wo_o, sems):
    copies = [(pd.at[k], pd_o.at[k]) for k in range(4)] + [(ag, ag_o), (pg, pg_o), (wo, wo_o)]
    copies = [pltpu.make_async_copy(src, dst, sems.at[k]) for k, (src, dst) in enumerate(copies)]
    for c in copies:
        c.start()
    for c in copies:
        c.wait()


def shards(msa, stretch, shift, wlr, offs, wf, fbias, adj):
    def vm(shape, dtype):
        return pltpu.VMEM(shape, dtype)

    def sem(*n):
        return pltpu.SemaphoreType.DMA(n)

    scratch = [
        vm((4, 512, 128), bf16), vm((1, 512, 256), bf16), vm((64, 256), f32), vm((1024, 128), f32),
        vm((1, 512, 256), bf16), vm((1, 256), f32), vm((1, 256), f32), vm((64, 256), bf16), vm((1, 64), f32),
        vm((1024, 128), bf16), vm((1, 128), f32), vm((4, 512, 128), bf16),
        vm((512, 256), f32), vm((512, 128), f32), vm((2, 512, 128), f32), vm((512, 256), bf16), vm((512, 256), bf16),
        vm((128, 256), bf16), vm((32, 256), bf16), vm((32, 512), bf16),
        vm((16, 16, 128), bf16), vm((16, 16, 128), bf16), vm((256, 128), f32), vm((8, 16, 128), bf16),
        vm((8, 16, 128), bf16), vm((128, 128), f32), vm((128, 128), f32), vm((4, 32, 128), bf16), vm((16, 32, 128), bf16),
        vm((512, 128), f32),
        vm((16, 2048), bf16), vm((128, 512), bf16), vm((512, 128), bf16), vm((128, 4096), bf16),
        vm((16, 128, 128), bf16), vm((1024, 128), f32), vm((1024, 128), bf16), vm((128, 1024), bf16),
        vm((512, 4096), bf16), vm((1024, 2048), bf16), vm((128, 2048), bf16), vm((128, 2048), bf16),
        vm((128, 2048), f32), vm((128, 1024), bf16), vm((128, 1024), bf16), vm((128, 2048), bf16),
        vm((8, 16, 1024), bf16), vm((8, 16, 2048), bf16), vm((16, 2048), f32),
        vm((4, 128, 128), f32), vm((16, 32, 128), f32), vm((16, 32, 128), bf16), vm((16, 32, 128), bf16),
        vm((128, 128), f32), vm((8, 16, 128), bf16), vm((8, 16, 128), bf16),
        vm((256, 128), f32), vm((16, 16, 128), bf16), vm((16, 16, 128), bf16), vm((2, 512, 128), f32),
        vm((1024, 128), f32), vm((16, 64, 128), bf16), vm((16, 64, 128), bf16), vm((64, 128), bf16),
        vm((8, 64, 128), bf16), vm((64, 128), bf16), vm((16, 64, 128), bf16), vm((16, 128, 128), bf16),
        vm((16, 8, 128), f32), vm((16, 8, 128), f32), vm((8, 128), f32), vm((8, 8, 128), f32), vm((8, 128), f32),
        vm((16, 8, 128), f32),
        sem(8), pltpu.SemaphoreType.DMA, sem(24), sem(24), sem(4), sem(8), sem(8), sem(8),
    ]
    pd, ag, pg, wo = pl.pallas_call(
        kernel,
        out_shape=(
            jax.ShapeDtypeStruct((4, 512, 128), bf16),
            jax.ShapeDtypeStruct((1, 512, 256), bf16),
            jax.ShapeDtypeStruct((64, 256), f32),
            jax.ShapeDtypeStruct((1024, 128), f32),
        ),
        in_specs=[pl.BlockSpec(memory_space=pltpu.HBM)] * 8,
        out_specs=(pl.BlockSpec(memory_space=pltpu.HBM),) * 4,
        scratch_shapes=scratch,
        compiler_params=pltpu.CompilerParams(
            collective_id=0, has_side_effects=True, vmem_limit_bytes=48 * 1024 * 1024
        ),
    )(
        *[
            pltpu.with_memory_space_constraint(v, pltpu.HBM)
            for v in (
                msa,
                stretch.reshape(1, 256),
                shift.reshape(1, 256),
                wlr.T,
                offs.reshape(1, 64),
                wf,
                fbias.reshape(1, 128),
                adj,
            )
        ]
    )
    pd, ag, pg, wo = pl.pallas_call(
        emit,
        out_shape=tuple(jax.ShapeDtypeStruct(v.shape, v.dtype) for v in (pd, ag, pg, wo)),
        in_specs=[pl.BlockSpec(memory_space=pl.ANY)] * 4,
        out_specs=(pl.BlockSpec(memory_space=pltpu.HBM),) * 4,
        scratch_shapes=[sem(7)],
        compiler_params=pltpu.CompilerParams(vmem_limit_bytes=16 * 1024 * 1024),
    )(pd, ag, pg, wo)
    return pd, ag, pg.T, wo


def solution(mesh):
    placed = (P("dap", "crop", None), P(), P(), P(), P(), P(), P(), P("dap", "crop", None))
    return jax.shard_map(
        shards,
        mesh=mesh,
        in_specs=placed,
        out_specs=(
            P("dap", "crop", None),
            P("dap", "crop", None),
            P("crop", None),
            P("crop", None),
        ),
        check_vma=False,
    )
```

```python
import math

import jax
import jax.numpy as jnp
from jax import lax
from jax.experimental import pallas as pl
from jax.experimental.pallas import tpu as pltpu
from jax.sharding import PartitionSpec as P

EPSILON = 1e-05
MESH = pl.DeviceIdType.MESH
f32 = jnp.float32
bf16 = jnp.bfloat16

NX, NZ, NM = 4, 8, 16
CH = 32
ROWS = 128
RES = 512
FAR = (4, 3, 5)
NEAR = (2, 6, 1, 7)


def dot(a, b):
    return jnp.dot(a, b, preferred_element_type=f32)


def dot_nt(a, b):
    return lax.dot_general(a, b, (((1,), (1,)), ((), ())), preferred_element_type=f32)


def loop(low, high, body):
    def step(k, carry):
        body(k)
        return carry

    lax.fori_loop(low, high, step, 0)


class Exchange:
    def __init__(self, each, device, mine, src, dst, whole, ssem, rsem, apart=False):
        self.each, self.device, self.mine, self.src, self.dst, self.whole = each, device, mine, src, dst, whole
        self.ssem, self.rsem, self.apart = ssem, rsem, apart
        self.waited = False

    def copy(self, p, slot):
        return pltpu.make_async_remote_copy(
            src_ref=self.src(p),
            dst_ref=self.dst(slot),
            send_sem=self.ssem.at[0],
            recv_sem=self.rsem.at[slot if self.apart else 0],
            device_id={"dap": self.device(p)},
            device_id_type=MESH,
        )

    def bulk(self):
        return pltpu.make_async_remote_copy(
            src_ref=self.whole,
            dst_ref=self.whole,
            send_sem=self.ssem.at[0],
            recv_sem=self.rsem.at[0],
            device_id={"dap": self.device(0)},
            device_id_type=MESH,
        )

    def start_one(self, p):
        self.copy(p, self.mine).start()

    def recv_one(self, p):
        self.copy(p, p).wait_recv()

    def start(self):
        self.each(self.start_one)

    def recv(self):
        self.waited = True
        if self.apart:
            self.each(self.recv_one)
        else:
            self.bulk().wait_recv()

    def sent(self):
        self.bulk().wait_send()


def kernel(
    msa_h, stretch_h, shift_h, wlrt_h, offs_h, wf_h, fbias_h, adj_h,
    pd_h, ag_h, pg_h, wo_h,
    pd_out, ag_out, pg_out, wo_out,
    msa, stretch, shift, wlrt_v, offs, wf, fbias, adj,
    scaled, inv, nf, nb, np_, wl4t, wrt, rt,
    sb, rb, rbf, las, la, laf, lbf, lb, lbr, lbrf, rs, lmat, lt, rmat, amat, wff, w2, w2t,
    gmat, xmat, rgs, rgr, rgo, ryq, ryr, rz, rzf, rzn, rsum, lacc, lgp, lgs, lgr, lzf, lzs, lzr, bsf, bs, br, ng,
    wpart, wsend, wrecv, wzs, wzr, wfin, wall_v, pdb,
    psend, precv, pzs, pzr, pgs, pgr,
    in_sem, adj_sem, ssems, rsems, adj_r, zr_r, yf_r, ry_r,
):
    me = lax.axis_index("dap")
    core = lax.rem(me, 2)
    x = lax.rem(me // 2, NX)
    z = lax.rem(me // 8, NZ)
    y = me // 64
    m = y * 8 + x * 2 + core
    other = 1 - core

    def plane_dev(mm):
        return (mm // 8) * 64 + z * 8 + lax.rem(mm, 8)

    def z_dev(zz):
        return y * 64 + zz * 8 + x * 2 + core

    def x_dev(xx):
        return y * 64 + z * 8 + xx * 2 + core

    def core_dev(_):
        return y * 64 + z * 8 + x * 2 + other

    def y_dev(_):
        return (1 - y) * 64 + z * 8 + x * 2 + core

    def planes(body):
        loop(1, NM, lambda k: body(lax.rem(m + k, NM)))

    def zs(body):
        for k in (4, 3, 5, 2, 6, 1, 7):
            body(lax.rem(z + k, NZ))

    def zs_far(body):
        for k in FAR:
            body(lax.rem(z + k, NZ))

    def zs_near(body):
        for k in NEAR:
            body(lax.rem(z + k, NZ))

    def xs(body):
        for k in (1, 3, 2):
            body(lax.rem(x + k, NX))

    exchanges = []

    def exchange(each, device, mine, src, dst, whole, rsem=None):
        k = pl.ds(len(exchanges), 1)
        e = Exchange(
            each, device, mine, src, dst, whole, ssems.at[k], rsems.at[k] if rsem is None else rsem, rsem is not None
        )
        exchanges.append(e)
        return e

    def finish():
        for e in exchanges:
            if not e.waited:
                e.recv()
        for e in exchanges:
            e.sent()

    small = [
        pltpu.make_async_copy(src, dst, in_sem.at[k])
        for k, (src, dst) in enumerate(
            [
                (msa_h, msa), (stretch_h, stretch), (shift_h, shift), (wlrt_h, wlrt_v), (offs_h, offs),
                (wf_h, wf), (fbias_h, fbias), (adj_h, adj),
            ]
        )
    ]
    for c in small:
        c.start()

    def adj_part(xx):
        return adj.at[:, pl.ds(pl.multiple_of(xx * 128, 128), 128), :]

    def own_i(xx):
        return amat.at[pl.ds(xx * 4, 4)]


    barrier = pltpu.get_barrier_semaphore()
    planes(lambda mm: pl.semaphore_signal(barrier, inc=1, device_id={"dap": plane_dev(mm)}, device_id_type=MESH))
    zs(lambda zz: pl.semaphore_signal(barrier, inc=1, device_id={"dap": z_dev(zz)}, device_id_type=MESH))
    for c in small:
        c.wait()

    def norm_rows(k):
        rows = pl.ds(pl.multiple_of(k * 64, 64), 64)
        v = msa[0, rows, :].astype(f32)
        c = v - jnp.mean(v, axis=-1, keepdims=True)
        iv = lax.rsqrt(jnp.mean(c * c, axis=-1, keepdims=True) + EPSILON)
        sc = c * iv
        scaled[rows, :] = sc
        inv[rows, :] = jnp.broadcast_to(iv, (64, 128))
        n = (sc * stretch[...] + shift[...]).astype(bf16)
        nb[rows, :] = n
        n = n.astype(f32)
        nf[0, rows, :] = n[:, :128]
        nf[1, rows, :] = n[:, 128:]

    loop(0, 8, norm_rows)
    for r in range(4):
        for zz in range(NZ):
            v = [
                jnp.concatenate([nf[h, pl.ds(yy * 256 + zz * 32 + r, 8, stride=4), :] for h in range(2)], axis=1)
                for yy in range(2)
            ]
            np_[pl.ds(r * 128 + zz * 16, 16), :] = jnp.concatenate(v, axis=0).astype(bf16)

    wlrt = wlrt_v[...]
    w_rows = wlrt.astype(f32).T.astype(bf16)
    wrt[...] = wlrt[CH:, :]
    spread = lax.broadcasted_iota(jnp.int32, (64, 128), 0) == (lax.broadcasted_iota(jnp.int32, (64, 128), 1) & 31)
    wl4 = dot(w_rows, spread.astype(f32).astype(bf16))
    wl4t[...] = wl4.T.astype(bf16)
    diag = lax.broadcasted_iota(jnp.int32, (64, 64), 0) == lax.broadcasted_iota(jnp.int32, (64, 64), 1)
    offs_col = jnp.sum(jnp.where(diag, jnp.broadcast_to(offs[...], (64, 64)), 0.0), axis=1, keepdims=True)
    offs4 = jnp.sum(jnp.where(spread, jnp.broadcast_to(offs_col, (64, 128)), 0.0), axis=0, keepdims=True)
    lane_r = lax.broadcasted_iota(jnp.int32, (256, 128), 1) >> 5
    left = jnp.zeros((128, 128), f32)
    for r in range(4):
        left = left + dot(np_[pl.ds(r * 128, 128), :], jnp.where(lane_r == r, wl4, 0.0).astype(bf16))
    left = (left + offs4).astype(bf16).astype(f32) * (1.0 / ROWS)
    las[...] = left.astype(bf16).reshape(NZ, NM, 128)
    rt[...] = (dot_nt(wlrt[CH:, :], nb[...]) + offs_col[CH:, :]).astype(bf16)
    for mm in range(NM):
        xx, cc = (mm % 8) // 2, mm % 2
        sb[mm] = rt[pl.ds(cc * 16, 16), pl.ds(xx * 128, 128)]

    pl.semaphore_wait(barrier, NM - 1 + NZ - 1)

    first = exchange(planes, plane_dev, m, lambda mm: sb.at[mm], lambda mm: rb.at[mm], rb.at[pl.ds(0, NM - 1)])
    first.start()
    rb[m] = sb[m]
    zleft = exchange(zs, z_dev, z, lambda zz: las.at[zz], lambda zz: la.at[zz], la.at[pl.ds(0, NZ - 1)])
    zleft.start()
    la[z] = las[z]
    adjoint = exchange(xs, x_dev, x, adj_part, own_i, amat.at[pl.ds(0, 12)], adj_r)
    adjoint.start()
    own_adj = pltpu.make_async_copy(adj_part(x), own_i(x), adj_sem)
    own_adj.start()

    wff[...] = wf[...].astype(f32)
    for d in range(CH):
        w2[pl.ds(d * 32, 32), :] = wff[pl.ds(d, 32, stride=32), :].astype(bf16)
    for k in range(8):
        w2t[:, pl.ds(k * 128, 128)] = w2[pl.ds(k * 128, 128), :].astype(f32).T.astype(bf16)

    first.recv()

    rbf[...] = rb[...].reshape(256, 128).astype(f32)
    for d in range(16):
        rs[:, pl.ds(d * 128, 128)] = rbf[pl.ds(d, 16, stride=16), :].astype(bf16)

    def zrows(zz):
        return pl.ds(pl.multiple_of(zz * 16, 16), 16)

    def half(cc):
        return pl.ds(pl.multiple_of(cc * 2048, 2048), 2048)

    def quarter(cc, yy):
        return pl.ds(pl.multiple_of(cc * 2048 + yy * 1024, 1024), 1024)

    def r_piece(zz, yy):
        return rmat.at[zrows(zz), quarter(core, yy)]

    rs_own = rs.at[:, pl.ds(pl.multiple_of(y * 1024, 1024), 1024)]
    zfar = exchange(
        zs_far, z_dev, z, lambda zz: rs_own, lambda zz: r_piece(zz, y), rmat.at[pl.ds(0, 16 * len(FAR)), quarter(0, 0)], zr_r
    )
    znear = exchange(
        zs_near, z_dev, z, lambda zz: rs, lambda zz: rmat.at[zrows(zz), half(core)], rmat.at[pl.ds(0, 16 * len(NEAR)), half(0)], zr_r
    )
    zfar.start()
    znear.start()
    rmat[zrows(z), half(core)] = rs[...]

    zleft.recv()
    laf[...] = la[...].reshape(128, 128).astype(f32)
    for mm in range(0, NM, 2):
        for cc in range(2):
            yc, xx = (mm // 8) * 2 + cc, (mm % 8) // 2
            lbf[pl.ds(yc * 32 + xx * 8, 8), :] = laf[pl.ds(mm + cc, 8, stride=16), :]
    lb[...] = lbf[...].astype(bf16).reshape(4, 32, 128)
    lplane = exchange(
        planes,
        plane_dev,
        m,
        lambda mm: lb.at[(mm // 8) * 2 + lax.rem(mm, 2)],
        lambda mm: lbr.at[mm],
        lbr.at[pl.ds(0, NM - 1)],
    )
    lplane.start()
    lbr[m] = lb[y * 2 + core]

    yswap = exchange(
        zs_far, y_dev, None, lambda zz: r_piece(zz, y), None, rmat.at[pl.ds(0, 16 * len(FAR)), quarter(0, 0)], yf_r
    )
    swap = exchange(None, core_dev, None, None, None, rmat.at[:, half(other)])

    def to_core(piece):
        pltpu.make_async_remote_copy(
            src_ref=piece,
            dst_ref=piece,
            send_sem=swap.ssem.at[0],
            recv_sem=swap.rsem.at[0],
            device_id={"dap": core_dev(0)},
            device_id_type=MESH,
        ).start()

    def y_copy(zz, yy):
        return pltpu.make_async_remote_copy(
            src_ref=r_piece(zz, yy),
            dst_ref=r_piece(zz, yy),
            send_sem=yswap.ssem.at[0],
            recv_sem=yf_r.at[zz],
            device_id={"dap": y_dev(0)},
            device_id_type=MESH,
        )

    yswap.recv_one = lambda zz: y_copy(zz, 1 - y).wait_recv()

    def forward(k):
        zz = lax.rem(z + k, NZ)
        if k in FAR:
            zfar.recv_one(zz)
            y_copy(zz, y).start()
            to_core(r_piece(zz, y))
        else:
            znear.recv_one(zz)
            to_core(rmat.at[zrows(zz), half(core)])

    def forward_y(k):
        zz = lax.rem(z + k, NZ)
        yswap.recv_one(zz)
        to_core(r_piece(zz, 1 - y))

    to_core(rmat.at[zrows(z), half(core)])
    zfar.waited = True
    znear.waited = True
    yswap.waited = True

    def grad_pair(t):
        a2 = amat[pl.ds(t * 2, 2)].reshape(256, 128)
        for q in range(4):
            g = dot_nt(w2[pl.ds(q * 256, 256), :], a2)
            for e in range(8):
                for u in range(2):
                    rows = pl.ds(pl.multiple_of((2 * t + u) * 32, 32), 32)
                    gmat[rows, pl.ds((q * 8 + e) * 128, 128)] = g[e * 32 : e * 32 + 32, u * 128 : u * 128 + 128].astype(
                        bf16
                    )

    own_adj.wait()
    loop(x * 2, x * 2 + 2, grad_pair)
    adjoint.waited = True
    for k in (1, 3, 2):
        xx = lax.rem(x + k, NX)
        adjoint.recv_one(xx)
        loop(xx * 2, xx * 2 + 2, grad_pair)

    def left_part(cc, yy):
        cols = quarter(cc, yy)
        t = dot_nt(rmat[:, cols], gmat[:, cols])
        for xx in range(NX):
            lacc[xx] += t[:, xx * 128 : xx * 128 + 128]

    lplane.recv()
    lbrf[...] = lbr[...].reshape(512, 128).astype(f32)
    for zz in range(NZ):
        for xx in range(NX):
            lmat[pl.ds(zz * 16, 16), pl.ds(xx * 128, 128)] = lbrf[pl.ds(xx * 8 + zz, 16, stride=32), :].astype(bf16)
    for k in range(4):
        lt[pl.ds(k * 128, 128), :] = lmat[:, pl.ds(k * 128, 128)].astype(f32).T.astype(bf16)

    def columns(ref, yy):
        return ref.at[:, pl.ds(pl.multiple_of(yy * 1024, 1024), 1024)]

    def right_other(yy):
        def part(k):
            cols = pl.ds(pl.multiple_of(other * 2048 + yy * 1024 + k * 512, 512), 512)
            rgs[:, pl.ds(pl.multiple_of(yy * 1024 + k * 512, 512), 512)] = dot(lmat[...], gmat[:, cols]).astype(bf16)

        loop(0, 2, part)

    def right_own(yy):
        def part(k):
            cols = pl.ds(pl.multiple_of(core * 2048 + yy * 1024 + k * 512, 512), 512)
            rgo[:, pl.ds(pl.multiple_of(yy * 1024 + k * 512, 512), 512)] = dot(lmat[...], gmat[:, cols])

        loop(0, 2, part)

    add = [
        exchange(
            lambda body: body(0),
            core_dev,
            0,
            lambda _, yy=yy: columns(rgs, yy),
            lambda _, yy=yy: columns(rgr, yy),
            columns(rgr, yy),
        )
        for yy in (1 - y, y)
    ]
    right_other(1 - y)
    add[0].start()
    right_other(y)
    add[1].start()
    for k in FAR:
        forward(k)
    right_own(1 - y)
    right_own(y)
    add[0].recv()

    ry = exchange(
        zs_far, y_dev, None, lambda zz: ryq.at[zrows(zz), :], None, ryr.at[pl.ds(0, 16 * len(FAR)), :], ry_r
    )
    ry.copy = lambda zz, _: pltpu.make_async_remote_copy(
        src_ref=ryq.at[zrows(zz), :],
        dst_ref=ryr.at[zrows(zz), :],
        send_sem=ry.ssem.at[0],
        recv_sem=ry_r.at[zz],
        device_id={"dap": y_dev(0)},
        device_id_type=MESH,
    )
    theirs = pl.ds(pl.multiple_of((1 - y) * 1024, 1024), 1024)
    mine = pl.ds(pl.multiple_of(y * 1024, 1024), 1024)
    for k in FAR:
        rows = zrows(lax.rem(z + k, NZ))
        ryq[rows, :] = (rgo[rows, theirs] + rgr[rows, theirs].astype(f32)).astype(bf16)
        ry.start_one(lax.rem(z + k, NZ))
    bfar = exchange(
        zs_far, z_dev, z, lambda zz: rz.at[zrows(zz), mine], lambda zz: rzf.at[zz], rzf.at[pl.ds(0, len(FAR))]
    )
    bnear = exchange(
        zs_near, z_dev, z, lambda zz: rz.at[zrows(zz), :], lambda zz: rzn.at[zz], rzn.at[pl.ds(0, len(NEAR))]
    )
    add[1].recv()
    for k in NEAR:
        rows = zrows(lax.rem(z + k, NZ))
        rz[rows, :] = (rgo[rows, :] + rgr[rows, :].astype(f32)).astype(bf16)
        bnear.start_one(lax.rem(z + k, NZ))
    for k in NEAR:
        forward(k)
    for k in FAR:
        forward_y(k)
    lacc[...] = jnp.zeros((NX, 128, 128), f32)
    left_part(core, y)
    left_part(core, 1 - y)

    ry.waited = True

    def right_rows(k):
        zz = lax.rem(z + k, NZ)
        rows = zrows(zz)
        ry.recv_one(zz)
        rz[rows, mine] = (rgo[rows, mine] + rgr[rows, mine].astype(f32) + ryr[rows, :].astype(f32)).astype(bf16)
        bfar.start_one(zz)

    for k in FAR[:3]:
        right_rows(k)
    swap.recv()
    left_part(other, y)
    left_part(other, 1 - y)
    for xx in range(NX):
        for mm in range(NM):
            lgp[mm, pl.ds(xx * 8, 8), :] = lacc[xx, pl.ds(mm, 8, stride=16), :]
    lgs[...] = (lgp[...] * (1.0 / ROWS)).astype(bf16)
    bleft = exchange(planes, plane_dev, m, lambda mm: lgs.at[mm], lambda mm: lgr.at[mm], lgr.at[pl.ds(0, NM - 1)])
    bleft.start()
    lgr[m] = lgs[m]

    def outer_part(n):
        o = dot(lt[...], rmat[:, pl.ds(pl.multiple_of(n * 256, 256), 256)])
        for i in range(16):
            for e in range(2):
                rows = pl.ds(pl.multiple_of((2 * n + e) * 32, 32), 32)
                xmat[rows, pl.ds(i * 128, 128)] = o[i * 32 : i * 32 + 32, e * 128 : e * 128 + 128].astype(bf16)

    for n, ks in enumerate([FAR[3:4], FAR[4:], (), ()]):
        for k in ks:
            right_rows(k)
        loop(n * 4, n * 4 + 4, outer_part)

    def w_part(n):
        rows = pl.ds(pl.multiple_of(n * 256, 256), 256)
        wpart[rows, :] = dot(xmat[rows, :], amat[...].reshape(2048, 128))

    loop(0, 2, w_part)

    bleft.recv()
    for yc in range(4):
        t = None
        for xx in range(NX):
            v = lgr[(yc // 2) * 8 + xx * 2 + yc % 2].astype(f32)
            t = v if t is None else t + v
        for xx in range(NX):
            lzf[pl.ds((yc // 2) * 8 + xx * 2 + yc % 2, 8, stride=16), :] = t[xx * 8 : xx * 8 + 8, :]
    lzs[...] = lzf[...].astype(bf16).reshape(NZ, NM, 128)
    bzl = exchange(zs, z_dev, z, lambda zz: lzs.at[zz], lambda zz: lzr.at[zz], lzr.at[pl.ds(0, NZ - 1)])
    bzl.start()
    lzr[z] = lzs[z]

    bnear.recv()
    bfar.recv()
    rows = zrows(z)
    t = rgo[rows, :] + rgr[rows, :].astype(f32)
    for k in NEAR:
        t = t + rzn[lax.rem(z + k, NZ)].astype(f32)
    rsum[...] = t
    t = rsum[:, mine]
    for k in FAR:
        t = t + rzf[lax.rem(z + k, NZ)].astype(f32)
    rsum[:, mine] = t
    for d in range(16):
        bsf[pl.ds(d, 16, stride=16), :] = rsum[:, pl.ds(d * 128, 128)]
    bs[...] = bsf[...].astype(bf16).reshape(NM, 16, 128)
    back = exchange(planes, plane_dev, m, lambda mm: bs.at[mm], lambda mm: br.at[mm], br.at[pl.ds(0, NM - 1)])
    back.start()
    br[m] = bs[m]

    loop(2, 4, w_part)
    for c in range(CH):
        wsend[c // 2, pl.ds((c % 2) * 32, 32), :] = wpart[pl.ds(c, 32, stride=32), :].astype(bf16)
    wplane = exchange(planes, plane_dev, m, lambda mm: wsend.at[mm], lambda mm: wrecv.at[mm], wrecv.at[pl.ds(0, NM - 1)])
    wplane.start()
    wrecv[m] = wsend[m]


    def delta_pair(t):
        p = dot(w2t[...], xmat[:, pl.ds(pl.multiple_of(t * 256, 256), 256)])
        pdb[pl.ds(t * 2, 2)] = (p.T + fbias[...]).astype(bf16).reshape(2, 128, 128)

    loop(0, 4, delta_pair)

    back.recv()
    bzl.recv()
    lg = lzr[...].reshape(128, 128).astype(f32)
    rparts = []
    for cc in range(2):
        row = [br[xx * 2 + cc].astype(f32) + br[8 + xx * 2 + cc].astype(f32) for xx in range(NX)]
        rparts.append(jnp.concatenate(row, axis=1))
    rg = jnp.concatenate(rparts, axis=0)
    lgb = lg.astype(bf16)
    lgt = lgb.astype(f32).T
    lcat = jnp.concatenate([lgt[r * 32 : r * 32 + 32, :] for r in range(4)], axis=1).astype(bf16)
    rgb = rg.astype(bf16)
    pleft = dot(lcat, np_[...])
    pright = dot(rgb, nb[...])
    for h in range(2):
        cols = slice(h * 128, h * 128 + 128)
        for k in range(4):
            psend[h * 8 + k] = pleft[k * 8 : k * 8 + 8, cols]
            psend[h * 8 + 4 + k] = pright[k * 8 : k * 8 + 8, cols]
    pplane = exchange(planes, plane_dev, m, lambda mm: psend.at[mm], lambda mm: precv.at[mm], precv.at[pl.ds(0, NM - 1)])
    pplane.start()
    precv[m] = psend[m]

    loop(4, 8, delta_pair)

    def out_part(xx):
        return pd_out.at[:, pl.ds(pl.multiple_of(xx * 128, 128), 128), :]

    delta = exchange(xs, x_dev, x, lambda xx: pdb.at[pl.ds(xx * 4, 4)], out_part, pd_out.at[:, pl.ds(0, 384), :])
    delta.start()
    pd_out[:, pl.ds(pl.multiple_of(x * 128, 128), 128), :] = pdb[pl.ds(x * 4, 4)]

    wplane.recv()
    t = wrecv[0].astype(f32)
    for mm in range(1, NM):
        t = t + wrecv[mm].astype(f32)
    wzs[...] = t.astype(bf16)
    wz = exchange(zs, z_dev, z, lambda zz: wzs, lambda zz: wzr.at[zz], wzr.at[pl.ds(0, NZ - 1)])
    wz.start()
    wzr[z] = wzs[...]

    row_r = lax.broadcasted_iota(jnp.int32, (128, 256), 0) >> 5
    for r in range(4):
        v = dot(lgb, jnp.where(row_r == r, wl4t[...].astype(f32), 0.0).astype(bf16))
        for g in range(16):
            for h in range(2):
                ng[h, pl.ds((g % 2) * 256 + (g // 2) * 32 + r, 8, stride=4), :] = v[
                    g * 8 : g * 8 + 8, h * 128 : h * 128 + 128
                ]
    nr = dot(rgb.astype(f32).T.astype(bf16), wrt[...])
    ng[0] = ng[0] + nr[:, :128]
    ng[1] = ng[1] + nr[:, 128:]

    pplane.recv()
    t = precv[0]
    for mm in range(1, NM):
        t = t + precv[mm]
    pzs[...] = t
    pz = exchange(zs, z_dev, z, lambda zz: pzs, lambda zz: pzr.at[zz], pzr.at[pl.ds(0, NZ - 1)])
    pz.start()
    pzr[z] = t


    def back_rows(k):
        rows = pl.ds(pl.multiple_of(k * 64, 64), 64)
        hid = jnp.concatenate([ng[0, rows, :], ng[1, rows, :]], axis=1) * stretch[...]
        sc = scaled[rows, :]
        iv = inv[rows, :][:, :1]
        g = iv * (
            hid - jnp.mean(hid, axis=-1, keepdims=True) - sc * jnp.mean(hid * sc, axis=-1, keepdims=True)
        )
        ag_out[0, rows, :] = g.astype(bf16)

    loop(0, 8, back_rows)
    ag_copy = pltpu.make_async_copy(ag_out, ag_h, in_sem.at[0])
    ag_copy.start()

    wz.recv()
    t = wzr[0].astype(f32)
    for zz in range(1, NZ):
        t = t + wzr[zz].astype(f32)
    wfin[...] = (t * (math.sqrt(ROWS) / RES)).astype(bf16)
    wall = exchange(
        planes, plane_dev, m, lambda mm: wfin, lambda mm: wall_v.at[mm], wall_v.at[pl.ds(0, NM - 1)]
    )
    wall.start()
    wall_v[m] = wfin[...]

    pz.recv()
    t = pzr[0]
    for zz in range(1, NZ):
        t = t + pzr[zz]
    t = t * (1.0 / RES)
    pgs[...] = t
    pall = exchange(planes, plane_dev, m, lambda mm: pgs, lambda mm: pgr.at[mm], pgr.at[pl.ds(0, NM - 1)])
    pall.start()
    pgr[m] = t

    wall.recv()
    wo_out[...] = wall_v[...].reshape(1024, 128).astype(f32)
    wo_copy = pltpu.make_async_copy(wo_out, wo_h, in_sem.at[2])
    wo_copy.start()
    delta.recv()
    pd_copy = pltpu.make_async_copy(pd_out, pd_h, in_sem.at[1])
    pd_copy.start()
    pall.recv()
    pt = pgr[...].reshape(2, 64, 128)
    pg_out[:, pl.ds(0, 128)] = pt[0]
    pg_out[:, pl.ds(128, 128)] = pt[1]
    pg_copy = pltpu.make_async_copy(pg_out, pg_h, in_sem.at[3])
    pg_copy.start()
    finish()
    for c in (ag_copy, pd_copy, wo_copy, pg_copy):
        c.wait()


def emit(pd, ag, pg, wo, pd_o, ag_o, pg_o, wo_o, sems):
    copies = [(pd.at[k], pd_o.at[k]) for k in range(4)] + [(ag, ag_o), (pg, pg_o), (wo, wo_o)]
    copies = [pltpu.make_async_copy(src, dst, sems.at[k]) for k, (src, dst) in enumerate(copies)]
    for c in copies:
        c.start()
    for c in copies:
        c.wait()


def shards(msa, stretch, shift, wlr, offs, wf, fbias, adj):
    def vm(shape, dtype):
        return pltpu.VMEM(shape, dtype)

    def sem(*n):
        return pltpu.SemaphoreType.DMA(n)

    scratch = [
        vm((4, 512, 128), bf16), vm((1, 512, 256), bf16), vm((64, 256), f32), vm((1024, 128), f32),
        vm((1, 512, 256), bf16), vm((1, 256), f32), vm((1, 256), f32), vm((64, 256), bf16), vm((1, 64), f32),
        vm((1024, 128), bf16), vm((1, 128), f32), vm((4, 512, 128), bf16),
        vm((512, 256), f32), vm((512, 128), f32), vm((2, 512, 128), f32), vm((512, 256), bf16), vm((512, 256), bf16),
        vm((128, 256), bf16), vm((32, 256), bf16), vm((32, 512), bf16),
        vm((16, 16, 128), bf16), vm((16, 16, 128), bf16), vm((256, 128), f32), vm((8, 16, 128), bf16),
        vm((8, 16, 128), bf16), vm((128, 128), f32), vm((128, 128), f32), vm((4, 32, 128), bf16), vm((16, 32, 128), bf16),
        vm((512, 128), f32),
        vm((16, 2048), bf16), vm((128, 512), bf16), vm((512, 128), bf16), vm((128, 4096), bf16),
        vm((16, 128, 128), bf16), vm((1024, 128), f32), vm((1024, 128), bf16), vm((128, 1024), bf16),
        vm((512, 4096), bf16), vm((1024, 2048), bf16), vm((128, 2048), bf16), vm((128, 2048), bf16),
        vm((128, 2048), f32), vm((128, 1024), bf16), vm((128, 1024), bf16), vm((128, 2048), bf16),
        vm((8, 16, 1024), bf16), vm((8, 16, 2048), bf16), vm((16, 2048), f32),
        vm((4, 128, 128), f32), vm((16, 32, 128), f32), vm((16, 32, 128), bf16), vm((16, 32, 128), bf16),
        vm((128, 128), f32), vm((8, 16, 128), bf16), vm((8, 16, 128), bf16),
        vm((256, 128), f32), vm((16, 16, 128), bf16), vm((16, 16, 128), bf16), vm((2, 512, 128), f32),
        vm((1024, 128), f32), vm((16, 64, 128), bf16), vm((16, 64, 128), bf16), vm((64, 128), bf16),
        vm((8, 64, 128), bf16), vm((64, 128), bf16), vm((16, 64, 128), bf16), vm((16, 128, 128), bf16),
        vm((16, 8, 128), f32), vm((16, 8, 128), f32), vm((8, 128), f32), vm((8, 8, 128), f32), vm((8, 128), f32),
        vm((16, 8, 128), f32),
        sem(8), pltpu.SemaphoreType.DMA, sem(24), sem(24), sem(4), sem(8), sem(8), sem(8),
    ]
    pd, ag, pg, wo = pl.pallas_call(
        kernel,
        out_shape=(
            jax.ShapeDtypeStruct((4, 512, 128), bf16),
            jax.ShapeDtypeStruct((1, 512, 256), bf16),
            jax.ShapeDtypeStruct((64, 256), f32),
            jax.ShapeDtypeStruct((1024, 128), f32),
        ),
        in_specs=[pl.BlockSpec(memory_space=pltpu.HBM)] * 8,
        out_specs=(pl.BlockSpec(memory_space=pltpu.HBM),) * 4,
        scratch_shapes=scratch,
        compiler_params=pltpu.CompilerParams(
            collective_id=0, has_side_effects=True, vmem_limit_bytes=48 * 1024 * 1024
        ),
    )(
        *[
            pltpu.with_memory_space_constraint(v, pltpu.HBM)
            for v in (
                msa,
                stretch.reshape(1, 256),
                shift.reshape(1, 256),
                wlr.T,
                offs.reshape(1, 64),
                wf,
                fbias.reshape(1, 128),
                adj,
            )
        ]
    )
    pd, ag, pg, wo = pl.pallas_call(
        emit,
        out_shape=tuple(jax.ShapeDtypeStruct(v.shape, v.dtype) for v in (pd, ag, pg, wo)),
        in_specs=[pl.BlockSpec(memory_space=pl.ANY)] * 4,
        out_specs=(pl.BlockSpec(memory_space=pltpu.HBM),) * 4,
        scratch_shapes=[sem(7)],
        compiler_params=pltpu.CompilerParams(vmem_limit_bytes=16 * 1024 * 1024),
    )(pd, ag, pg, wo)
    return pd, ag, pg.T, wo


def solution(mesh):
    placed = (P("dap", "crop", None), P(), P(), P(), P(), P(), P(), P("dap", "crop", None))
    return jax.shard_map(
        shards,
        mesh=mesh,
        in_specs=placed,
        out_specs=(
            P("dap", "crop", None),
            P("dap", "crop", None),
            P("crop", None),
            P("crop", None),
        ),
        check_vma=False,
    )
```

```python
import math

import jax
import jax.numpy as jnp
from jax import lax
from jax.experimental import pallas as pl
from jax.experimental.pallas import tpu as pltpu
from jax.sharding import PartitionSpec as P

EPSILON = 1e-05
MESH = pl.DeviceIdType.MESH
f32 = jnp.float32
bf16 = jnp.bfloat16

NX, NZ, NM = 4, 8, 16
CH = 32
ROWS = 128
RES = 512
PLANE_STEPS = [(dy, dx, dc) for dx in (2, 1, 3, 0) for dy in (1, 0) for dc in (1, 0) if dy or dx or dc]
FAR = (4, 3, 5)
NEAR = (2, 6, 1, 7)


def dot(a, b):
    return jnp.dot(a, b, preferred_element_type=f32)


def dot_nt(a, b):
    return lax.dot_general(a, b, (((1,), (1,)), ((), ())), preferred_element_type=f32)


def loop(low, high, body):
    def step(k, carry):
        body(k)
        return carry

    lax.fori_loop(low, high, step, 0)


class Exchange:
    def __init__(self, each, device, mine, src, dst, whole, ssem, rsem, apart=False):
        self.each, self.device, self.mine, self.src, self.dst, self.whole = each, device, mine, src, dst, whole
        self.ssem, self.rsem, self.apart = ssem, rsem, apart
        self.waited = False

    def copy(self, p, slot):
        return pltpu.make_async_remote_copy(
            src_ref=self.src(p),
            dst_ref=self.dst(slot),
            send_sem=self.ssem.at[0],
            recv_sem=self.rsem.at[slot if self.apart else 0],
            device_id={"dap": self.device(p)},
            device_id_type=MESH,
        )

    def bulk(self):
        return pltpu.make_async_remote_copy(
            src_ref=self.whole,
            dst_ref=self.whole,
            send_sem=self.ssem.at[0],
            recv_sem=self.rsem.at[0],
            device_id={"dap": self.device(0)},
            device_id_type=MESH,
        )

    def start_one(self, p):
        self.copy(p, self.mine).start()

    def recv_one(self, p):
        self.copy(p, p).wait_recv()

    def start(self):
        self.each(self.start_one)

    def recv(self):
        self.waited = True
        if self.apart:
            self.each(self.recv_one)
        else:
            self.bulk().wait_recv()

    def sent(self):
        self.bulk().wait_send()


def kernel(
    msa_h, stretch_h, shift_h, wlrt_h, offs_h, wf_h, fbias_h, adj_h,
    pd_h, ag_h, pg_h, wo_h,
    pd_out, ag_out, pg_out, wo_out,
    msa, stretch, shift, wlrt_v, offs, wf, fbias, adj,
    scaled, inv, nf, nb, np_, wl4t, wrt, rt,
    sb, rb, rbf, las, la, laf, lbf, lb, lbr, lbrf, rs, lmat, lt, rmat, amat, wff, w2, w2t,
    gmat, xmat, rgs, rgr, rgo, ryq, ryr, rz, rzf, rzn, rsum, lacc, lgp, lgs, lgr, lzf, lzs, lzr, bsf, bs, br, ng,
    wpart, wsend, wrecv, wzs, wzr, wfin, wall_v, pdb,
    psend, precv, pzs, pzr, pgs, pgr,
    in_sem, adj_sem, ssems, rsems, adj_r, zr_r, yf_r, ry_r,
):
    me = lax.axis_index("dap")
    core = lax.rem(me, 2)
    x = lax.rem(me // 2, NX)
    z = lax.rem(me // 8, NZ)
    y = me // 64
    m = y * 8 + x * 2 + core
    other = 1 - core

    def plane_dev(mm):
        return (mm // 8) * 64 + z * 8 + lax.rem(mm, 8)

    def z_dev(zz):
        return y * 64 + zz * 8 + x * 2 + core

    def x_dev(xx):
        return y * 64 + z * 8 + xx * 2 + core

    def core_dev(_):
        return y * 64 + z * 8 + x * 2 + other

    def y_dev(_):
        return (1 - y) * 64 + z * 8 + x * 2 + core

    def planes(body):
        for dy, dx, dc in PLANE_STEPS:
            body((1 - y if dy else y) * 8 + lax.rem(x + dx, NX) * 2 + (other if dc else core))

    def zs(body):
        for k in (4, 3, 5, 2, 6, 1, 7):
            body(lax.rem(z + k, NZ))

    def zs_far(body):
        for k in FAR:
            body(lax.rem(z + k, NZ))

    def zs_near(body):
        for k in NEAR:
            body(lax.rem(z + k, NZ))

    def xs(body):
        for k in (1, 3, 2):
            body(lax.rem(x + k, NX))

    exchanges = []

    def exchange(each, device, mine, src, dst, whole, rsem=None):
        k = pl.ds(len(exchanges), 1)
        e = Exchange(
            each, device, mine, src, dst, whole, ssems.at[k], rsems.at[k] if rsem is None else rsem, rsem is not None
        )
        exchanges.append(e)
        return e

    def finish():
        for e in exchanges:
            if not e.waited:
                e.recv()
        for e in exchanges:
            e.sent()

    small = [
        pltpu.make_async_copy(src, dst, in_sem.at[k])
        for k, (src, dst) in enumerate(
            [
                (msa_h, msa), (stretch_h, stretch), (shift_h, shift), (wlrt_h, wlrt_v), (offs_h, offs),
                (wf_h, wf), (fbias_h, fbias), (adj_h, adj),
            ]
        )
    ]
    for c in small:
        c.start()

    def adj_part(xx):
        return adj.at[:, pl.ds(pl.multiple_of(xx * 128, 128), 128), :]

    def own_i(xx):
        return amat.at[pl.ds(xx * 4, 4)]


    barrier = pltpu.get_barrier_semaphore()
    planes(lambda mm: pl.semaphore_signal(barrier, inc=1, device_id={"dap": plane_dev(mm)}, device_id_type=MESH))
    zs(lambda zz: pl.semaphore_signal(barrier, inc=1, device_id={"dap": z_dev(zz)}, device_id_type=MESH))
    for c in small:
        c.wait()

    def norm_rows(k):
        rows = pl.ds(pl.multiple_of(k * 64, 64), 64)
        v = msa[0, rows, :].astype(f32)
        c = v - jnp.mean(v, axis=-1, keepdims=True)
        iv = lax.rsqrt(jnp.mean(c * c, axis=-1, keepdims=True) + EPSILON)
        sc = c * iv
        scaled[rows, :] = sc
        inv[rows, :] = jnp.broadcast_to(iv, (64, 128))
        n = (sc * stretch[...] + shift[...]).astype(bf16)
        nb[rows, :] = n
        n = n.astype(f32)
        nf[0, rows, :] = n[:, :128]
        nf[1, rows, :] = n[:, 128:]

    loop(0, 8, norm_rows)
    for r in range(4):
        for zz in range(NZ):
            v = [
                jnp.concatenate([nf[h, pl.ds(yy * 256 + zz * 32 + r, 8, stride=4), :] for h in range(2)], axis=1)
                for yy in range(2)
            ]
            np_[pl.ds(r * 128 + zz * 16, 16), :] = jnp.concatenate(v, axis=0).astype(bf16)

    wlrt = wlrt_v[...]
    w_rows = wlrt.astype(f32).T.astype(bf16)
    wrt[...] = wlrt[CH:, :]
    spread = lax.broadcasted_iota(jnp.int32, (64, 128), 0) == (lax.broadcasted_iota(jnp.int32, (64, 128), 1) & 31)
    wl4 = dot(w_rows, spread.astype(f32).astype(bf16))
    wl4t[...] = wl4.T.astype(bf16)
    diag = lax.broadcasted_iota(jnp.int32, (64, 64), 0) == lax.broadcasted_iota(jnp.int32, (64, 64), 1)
    offs_col = jnp.sum(jnp.where(diag, jnp.broadcast_to(offs[...], (64, 64)), 0.0), axis=1, keepdims=True)
    offs4 = jnp.sum(jnp.where(spread, jnp.broadcast_to(offs_col, (64, 128)), 0.0), axis=0, keepdims=True)
    lane_r = lax.broadcasted_iota(jnp.int32, (256, 128), 1) >> 5
    left = jnp.zeros((128, 128), f32)
    for r in range(4):
        left = left + dot(np_[pl.ds(r * 128, 128), :], jnp.where(lane_r == r, wl4, 0.0).astype(bf16))
    left = (left + offs4).astype(bf16).astype(f32) * (1.0 / ROWS)
    las[...] = left.astype(bf16).reshape(NZ, NM, 128)
    rt[...] = (dot_nt(wlrt[CH:, :], nb[...]) + offs_col[CH:, :]).astype(bf16)
    for mm in range(NM):
        xx, cc = (mm % 8) // 2, mm % 2
        sb[mm] = rt[pl.ds(cc * 16, 16), pl.ds(xx * 128, 128)]

    pl.semaphore_wait(barrier, NM - 1 + NZ - 1)

    first = exchange(planes, plane_dev, m, lambda mm: sb.at[mm], lambda mm: rb.at[mm], rb.at[pl.ds(0, NM - 1)])
    first.start()
    rb[m] = sb[m]
    zleft = exchange(zs, z_dev, z, lambda zz: las.at[zz], lambda zz: la.at[zz], la.at[pl.ds(0, NZ - 1)])
    zleft.start()
    la[z] = las[z]
    adjoint = exchange(xs, x_dev, x, adj_part, own_i, amat.at[pl.ds(0, 12)], adj_r)
    adjoint.start()
    own_adj = pltpu.make_async_copy(adj_part(x), own_i(x), adj_sem)
    own_adj.start()

    wff[...] = wf[...].astype(f32)
    for d in range(CH):
        w2[pl.ds(d * 32, 32), :] = wff[pl.ds(d, 32, stride=32), :].astype(bf16)
    for k in range(8):
        w2t[:, pl.ds(k * 128, 128)] = w2[pl.ds(k * 128, 128), :].astype(f32).T.astype(bf16)

    first.recv()

    rbf[...] = rb[...].reshape(256, 128).astype(f32)
    for d in range(16):
        rs[:, pl.ds(d * 128, 128)] = rbf[pl.ds(d, 16, stride=16), :].astype(bf16)

    def zrows(zz):
        return pl.ds(pl.multiple_of(zz * 16, 16), 16)

    def half(cc):
        return pl.ds(pl.multiple_of(cc * 2048, 2048), 2048)

    def quarter(cc, yy):
        return pl.ds(pl.multiple_of(cc * 2048 + yy * 1024, 1024), 1024)

    def r_piece(zz, yy):
        return rmat.at[zrows(zz), quarter(core, yy)]

    rs_own = rs.at[:, pl.ds(pl.multiple_of(y * 1024, 1024), 1024)]
    zfar = exchange(
        zs_far, z_dev, z, lambda zz: rs_own, lambda zz: r_piece(zz, y), rmat.at[pl.ds(0, 16 * len(FAR)), quarter(0, 0)], zr_r
    )
    znear = exchange(
        zs_near, z_dev, z, lambda zz: rs, lambda zz: rmat.at[zrows(zz), half(core)], rmat.at[pl.ds(0, 16 * len(NEAR)), half(0)], zr_r
    )
    zfar.start()
    znear.start()
    rmat[zrows(z), half(core)] = rs[...]

    zleft.recv()
    laf[...] = la[...].reshape(128, 128).astype(f32)
    for mm in range(0, NM, 2):
        for cc in range(2):
            yc, xx = (mm // 8) * 2 + cc, (mm % 8) // 2
            lbf[pl.ds(yc * 32 + xx * 8, 8), :] = laf[pl.ds(mm + cc, 8, stride=16), :]
    lb[...] = lbf[...].astype(bf16).reshape(4, 32, 128)
    lplane = exchange(
        planes,
        plane_dev,
        m,
        lambda mm: lb.at[(mm // 8) * 2 + lax.rem(mm, 2)],
        lambda mm: lbr.at[mm],
        lbr.at[pl.ds(0, NM - 1)],
    )
    lplane.start()
    lbr[m] = lb[y * 2 + core]

    yswap = exchange(
        zs_far, y_dev, None, lambda zz: r_piece(zz, y), None, rmat.at[pl.ds(0, 16 * len(FAR)), quarter(0, 0)], yf_r
    )
    swap = exchange(None, core_dev, None, None, None, rmat.at[:, half(other)])

    def to_core(piece):
        pltpu.make_async_remote_copy(
            src_ref=piece,
            dst_ref=piece,
            send_sem=swap.ssem.at[0],
            recv_sem=swap.rsem.at[0],
            device_id={"dap": core_dev(0)},
            device_id_type=MESH,
        ).start()

    def y_copy(zz, yy):
        return pltpu.make_async_remote_copy(
            src_ref=r_piece(zz, yy),
            dst_ref=r_piece(zz, yy),
            send_sem=yswap.ssem.at[0],
            recv_sem=yf_r.at[zz],
            device_id={"dap": y_dev(0)},
            device_id_type=MESH,
        )

    yswap.recv_one = lambda zz: y_copy(zz, 1 - y).wait_recv()

    def forward(k):
        zz = lax.rem(z + k, NZ)
        if k in FAR:
            zfar.recv_one(zz)
            y_copy(zz, y).start()
            to_core(r_piece(zz, y))
        else:
            znear.recv_one(zz)
            to_core(rmat.at[zrows(zz), half(core)])

    def forward_y(k):
        zz = lax.rem(z + k, NZ)
        yswap.recv_one(zz)
        to_core(r_piece(zz, 1 - y))

    to_core(rmat.at[zrows(z), half(core)])
    zfar.waited = True
    znear.waited = True
    yswap.waited = True

    def grad_pair(t):
        a2 = amat[pl.ds(t * 2, 2)].reshape(256, 128)
        for q in range(4):
            g = dot_nt(w2[pl.ds(q * 256, 256), :], a2)
            for e in range(8):
                for u in range(2):
                    rows = pl.ds(pl.multiple_of((2 * t + u) * 32, 32), 32)
                    gmat[rows, pl.ds((q * 8 + e) * 128, 128)] = g[e * 32 : e * 32 + 32, u * 128 : u * 128 + 128].astype(
                        bf16
                    )

    own_adj.wait()
    loop(x * 2, x * 2 + 2, grad_pair)
    adjoint.waited = True
    for k in (1, 3, 2):
        xx = lax.rem(x + k, NX)
        adjoint.recv_one(xx)
        loop(xx * 2, xx * 2 + 2, grad_pair)

    def left_part(cc, yy):
        cols = quarter(cc, yy)
        t = dot_nt(rmat[:, cols], gmat[:, cols])
        for xx in range(NX):
            lacc[xx] += t[:, xx * 128 : xx * 128 + 128]

    lplane.recv()
    lbrf[...] = lbr[...].reshape(512, 128).astype(f32)
    for zz in range(NZ):
        for xx in range(NX):
            lmat[pl.ds(zz * 16, 16), pl.ds(xx * 128, 128)] = lbrf[pl.ds(xx * 8 + zz, 16, stride=32), :].astype(bf16)
    for k in range(4):
        lt[pl.ds(k * 128, 128), :] = lmat[:, pl.ds(k * 128, 128)].astype(f32).T.astype(bf16)

    def columns(ref, yy):
        return ref.at[:, pl.ds(pl.multiple_of(yy * 1024, 1024), 1024)]

    def right_other(yy):
        def part(k):
            cols = pl.ds(pl.multiple_of(other * 2048 + yy * 1024 + k * 512, 512), 512)
            rgs[:, pl.ds(pl.multiple_of(yy * 1024 + k * 512, 512), 512)] = dot(lmat[...], gmat[:, cols]).astype(bf16)

        loop(0, 2, part)

    def right_own(yy):
        def part(k):
            cols = pl.ds(pl.multiple_of(core * 2048 + yy * 1024 + k * 512, 512), 512)
            rgo[:, pl.ds(pl.multiple_of(yy * 1024 + k * 512, 512), 512)] = dot(lmat[...], gmat[:, cols])

        loop(0, 2, part)

    add = [
        exchange(
            lambda body: body(0),
            core_dev,
            0,
            lambda _, yy=yy: columns(rgs, yy),
            lambda _, yy=yy: columns(rgr, yy),
            columns(rgr, yy),
        )
        for yy in (1 - y, y)
    ]
    right_other(1 - y)
    add[0].start()
    right_other(y)
    add[1].start()
    for k in FAR:
        forward(k)
    right_own(1 - y)
    right_own(y)
    add[0].recv()

    ry = exchange(
        zs_far, y_dev, None, lambda zz: ryq.at[zrows(zz), :], None, ryr.at[pl.ds(0, 16 * len(FAR)), :], ry_r
    )
    ry.copy = lambda zz, _: pltpu.make_async_remote_copy(
        src_ref=ryq.at[zrows(zz), :],
        dst_ref=ryr.at[zrows(zz), :],
        send_sem=ry.ssem.at[0],
        recv_sem=ry_r.at[zz],
        device_id={"dap": y_dev(0)},
        device_id_type=MESH,
    )
    theirs = pl.ds(pl.multiple_of((1 - y) * 1024, 1024), 1024)
    mine = pl.ds(pl.multiple_of(y * 1024, 1024), 1024)
    for k in FAR:
        rows = zrows(lax.rem(z + k, NZ))
        ryq[rows, :] = (rgo[rows, theirs] + rgr[rows, theirs].astype(f32)).astype(bf16)
        ry.start_one(lax.rem(z + k, NZ))
    bfar = exchange(
        zs_far, z_dev, z, lambda zz: rz.at[zrows(zz), mine], lambda zz: rzf.at[zz], rzf.at[pl.ds(0, len(FAR))]
    )
    bnear = exchange(
        zs_near, z_dev, z, lambda zz: rz.at[zrows(zz), :], lambda zz: rzn.at[zz], rzn.at[pl.ds(0, len(NEAR))]
    )
    add[1].recv()
    for k in NEAR:
        rows = zrows(lax.rem(z + k, NZ))
        rz[rows, :] = (rgo[rows, :] + rgr[rows, :].astype(f32)).astype(bf16)
        bnear.start_one(lax.rem(z + k, NZ))
    for k in NEAR:
        forward(k)
    for k in FAR:
        forward_y(k)
    lacc[...] = jnp.zeros((NX, 128, 128), f32)
    left_part(core, y)
    left_part(core, 1 - y)

    ry.waited = True

    def right_rows(k):
        zz = lax.rem(z + k, NZ)
        rows = zrows(zz)
        ry.recv_one(zz)
        rz[rows, mine] = (rgo[rows, mine] + rgr[rows, mine].astype(f32) + ryr[rows, :].astype(f32)).astype(bf16)
        bfar.start_one(zz)

    for k in FAR[:3]:
        right_rows(k)
    swap.recv()
    left_part(other, y)
    left_part(other, 1 - y)
    for xx in range(NX):
        for mm in range(NM):
            lgp[mm, pl.ds(xx * 8, 8), :] = lacc[xx, pl.ds(mm, 8, stride=16), :]
    lgs[...] = (lgp[...] * (1.0 / ROWS)).astype(bf16)
    bleft = exchange(planes, plane_dev, m, lambda mm: lgs.at[mm], lambda mm: lgr.at[mm], lgr.at[pl.ds(0, NM - 1)])
    bleft.start()
    lgr[m] = lgs[m]

    def outer_part(n):
        o = dot(lt[...], rmat[:, pl.ds(pl.multiple_of(n * 256, 256), 256)])
        for i in range(16):
            for e in range(2):
                rows = pl.ds(pl.multiple_of((2 * n + e) * 32, 32), 32)
                xmat[rows, pl.ds(i * 128, 128)] = o[i * 32 : i * 32 + 32, e * 128 : e * 128 + 128].astype(bf16)

    for n, ks in enumerate([FAR[3:4], FAR[4:], (), ()]):
        for k in ks:
            right_rows(k)
        loop(n * 4, n * 4 + 4, outer_part)

    def w_part(n):
        rows = pl.ds(pl.multiple_of(n * 256, 256), 256)
        wpart[rows, :] = dot(xmat[rows, :], amat[...].reshape(2048, 128))

    loop(0, 2, w_part)

    bleft.recv()
    for yc in range(4):
        t = None
        for xx in range(NX):
            v = lgr[(yc // 2) * 8 + xx * 2 + yc % 2].astype(f32)
            t = v if t is None else t + v
        for xx in range(NX):
            lzf[pl.ds((yc // 2) * 8 + xx * 2 + yc % 2, 8, stride=16), :] = t[xx * 8 : xx * 8 + 8, :]
    lzs[...] = lzf[...].astype(bf16).reshape(NZ, NM, 128)
    bzl = exchange(zs, z_dev, z, lambda zz: lzs.at[zz], lambda zz: lzr.at[zz], lzr.at[pl.ds(0, NZ - 1)])
    bzl.start()
    lzr[z] = lzs[z]

    bnear.recv()
    bfar.recv()
    rows = zrows(z)
    t = rgo[rows, :] + rgr[rows, :].astype(f32)
    for k in NEAR:
        t = t + rzn[lax.rem(z + k, NZ)].astype(f32)
    rsum[...] = t
    t = rsum[:, mine]
    for k in FAR:
        t = t + rzf[lax.rem(z + k, NZ)].astype(f32)
    rsum[:, mine] = t
    for d in range(16):
        bsf[pl.ds(d, 16, stride=16), :] = rsum[:, pl.ds(d * 128, 128)]
    bs[...] = bsf[...].astype(bf16).reshape(NM, 16, 128)
    back = exchange(planes, plane_dev, m, lambda mm: bs.at[mm], lambda mm: br.at[mm], br.at[pl.ds(0, NM - 1)])
    back.start()
    br[m] = bs[m]

    loop(2, 4, w_part)
    for c in range(CH):
        wsend[c // 2, pl.ds((c % 2) * 32, 32), :] = wpart[pl.ds(c, 32, stride=32), :].astype(bf16)
    wplane = exchange(planes, plane_dev, m, lambda mm: wsend.at[mm], lambda mm: wrecv.at[mm], wrecv.at[pl.ds(0, NM - 1)])
    wplane.start()
    wrecv[m] = wsend[m]


    def delta_pair(t):
        p = dot(w2t[...], xmat[:, pl.ds(pl.multiple_of(t * 256, 256), 256)])
        pdb[pl.ds(t * 2, 2)] = (p.T + fbias[...]).astype(bf16).reshape(2, 128, 128)

    loop(0, 4, delta_pair)

    back.recv()
    bzl.recv()
    lg = lzr[...].reshape(128, 128).astype(f32)
    rparts = []
    for cc in range(2):
        row = [br[xx * 2 + cc].astype(f32) + br[8 + xx * 2 + cc].astype(f32) for xx in range(NX)]
        rparts.append(jnp.concatenate(row, axis=1))
    rg = jnp.concatenate(rparts, axis=0)
    lgb = lg.astype(bf16)
    lgt = lgb.astype(f32).T
    lcat = jnp.concatenate([lgt[r * 32 : r * 32 + 32, :] for r in range(4)], axis=1).astype(bf16)
    rgb = rg.astype(bf16)
    pleft = dot(lcat, np_[...])
    pright = dot(rgb, nb[...])
    for h in range(2):
        cols = slice(h * 128, h * 128 + 128)
        for k in range(4):
            psend[h * 8 + k] = pleft[k * 8 : k * 8 + 8, cols]
            psend[h * 8 + 4 + k] = pright[k * 8 : k * 8 + 8, cols]
    pplane = exchange(planes, plane_dev, m, lambda mm: psend.at[mm], lambda mm: precv.at[mm], precv.at[pl.ds(0, NM - 1)])
    pplane.start()
    precv[m] = psend[m]

    loop(4, 8, delta_pair)

    def out_part(xx):
        return pd_out.at[:, pl.ds(pl.multiple_of(xx * 128, 128), 128), :]

    delta = exchange(xs, x_dev, x, lambda xx: pdb.at[pl.ds(xx * 4, 4)], out_part, pd_out.at[:, pl.ds(0, 384), :])
    delta.start()
    pd_out[:, pl.ds(pl.multiple_of(x * 128, 128), 128), :] = pdb[pl.ds(x * 4, 4)]

    wplane.recv()
    t = wrecv[0].astype(f32)
    for mm in range(1, NM):
        t = t + wrecv[mm].astype(f32)
    wzs[...] = t.astype(bf16)
    wz = exchange(zs, z_dev, z, lambda zz: wzs, lambda zz: wzr.at[zz], wzr.at[pl.ds(0, NZ - 1)])
    wz.start()
    wzr[z] = wzs[...]

    row_r = lax.broadcasted_iota(jnp.int32, (128, 256), 0) >> 5
    for r in range(4):
        v = dot(lgb, jnp.where(row_r == r, wl4t[...].astype(f32), 0.0).astype(bf16))
        for g in range(16):
            for h in range(2):
                ng[h, pl.ds((g % 2) * 256 + (g // 2) * 32 + r, 8, stride=4), :] = v[
                    g * 8 : g * 8 + 8, h * 128 : h * 128 + 128
                ]
    nr = dot(rgb.astype(f32).T.astype(bf16), wrt[...])
    ng[0] = ng[0] + nr[:, :128]
    ng[1] = ng[1] + nr[:, 128:]

    pplane.recv()
    t = precv[0]
    for mm in range(1, NM):
        t = t + precv[mm]
    pzs[...] = t
    pz = exchange(zs, z_dev, z, lambda zz: pzs, lambda zz: pzr.at[zz], pzr.at[pl.ds(0, NZ - 1)])
    pz.start()
    pzr[z] = t


    def back_rows(k):
        rows = pl.ds(pl.multiple_of(k * 64, 64), 64)
        hid = jnp.concatenate([ng[0, rows, :], ng[1, rows, :]], axis=1) * stretch[...]
        sc = scaled[rows, :]
        iv = inv[rows, :][:, :1]
        g = iv * (
            hid - jnp.mean(hid, axis=-1, keepdims=True) - sc * jnp.mean(hid * sc, axis=-1, keepdims=True)
        )
        ag_out[0, rows, :] = g.astype(bf16)

    loop(0, 8, back_rows)
    ag_copy = pltpu.make_async_copy(ag_out, ag_h, in_sem.at[0])
    ag_copy.start()

    wz.recv()
    t = wzr[0].astype(f32)
    for zz in range(1, NZ):
        t = t + wzr[zz].astype(f32)
    wfin[...] = (t * (math.sqrt(ROWS) / RES)).astype(bf16)
    wall = exchange(
        planes, plane_dev, m, lambda mm: wfin, lambda mm: wall_v.at[mm], wall_v.at[pl.ds(0, NM - 1)]
    )
    wall.start()
    wall_v[m] = wfin[...]

    pz.recv()
    t = pzr[0]
    for zz in range(1, NZ):
        t = t + pzr[zz]
    t = t * (1.0 / RES)
    pgs[...] = t
    pall = exchange(planes, plane_dev, m, lambda mm: pgs, lambda mm: pgr.at[mm], pgr.at[pl.ds(0, NM - 1)])
    pall.start()
    pgr[m] = t

    wall.recv()
    wo_out[...] = wall_v[...].reshape(1024, 128).astype(f32)
    wo_copy = pltpu.make_async_copy(wo_out, wo_h, in_sem.at[2])
    wo_copy.start()
    delta.recv()
    pd_copy = pltpu.make_async_copy(pd_out, pd_h, in_sem.at[1])
    pd_copy.start()
    pall.recv()
    pt = pgr[...].reshape(2, 64, 128)
    pg_out[:, pl.ds(0, 128)] = pt[0]
    pg_out[:, pl.ds(128, 128)] = pt[1]
    pg_copy = pltpu.make_async_copy(pg_out, pg_h, in_sem.at[3])
    pg_copy.start()
    finish()
    for c in (ag_copy, pd_copy, wo_copy, pg_copy):
        c.wait()


def emit(pd, ag, pg, wo, pd_o, ag_o, pg_o, wo_o, sems):
    copies = [(pd.at[k], pd_o.at[k]) for k in range(4)] + [(ag, ag_o), (pg, pg_o), (wo, wo_o)]
    copies = [pltpu.make_async_copy(src, dst, sems.at[k]) for k, (src, dst) in enumerate(copies)]
    for c in copies:
        c.start()
    for c in copies:
        c.wait()


def shards(msa, stretch, shift, wlr, offs, wf, fbias, adj):
    def vm(shape, dtype):
        return pltpu.VMEM(shape, dtype)

    def sem(*n):
        return pltpu.SemaphoreType.DMA(n)

    scratch = [
        vm((4, 512, 128), bf16), vm((1, 512, 256), bf16), vm((64, 256), f32), vm((1024, 128), f32),
        vm((1, 512, 256), bf16), vm((1, 256), f32), vm((1, 256), f32), vm((64, 256), bf16), vm((1, 64), f32),
        vm((1024, 128), bf16), vm((1, 128), f32), vm((4, 512, 128), bf16),
        vm((512, 256), f32), vm((512, 128), f32), vm((2, 512, 128), f32), vm((512, 256), bf16), vm((512, 256), bf16),
        vm((128, 256), bf16), vm((32, 256), bf16), vm((32, 512), bf16),
        vm((16, 16, 128), bf16), vm((16, 16, 128), bf16), vm((256, 128), f32), vm((8, 16, 128), bf16),
        vm((8, 16, 128), bf16), vm((128, 128), f32), vm((128, 128), f32), vm((4, 32, 128), bf16), vm((16, 32, 128), bf16),
        vm((512, 128), f32),
        vm((16, 2048), bf16), vm((128, 512), bf16), vm((512, 128), bf16), vm((128, 4096), bf16),
        vm((16, 128, 128), bf16), vm((1024, 128), f32), vm((1024, 128), bf16), vm((128, 1024), bf16),
        vm((512, 4096), bf16), vm((1024, 2048), bf16), vm((128, 2048), bf16), vm((128, 2048), bf16),
        vm((128, 2048), f32), vm((128, 1024), bf16), vm((128, 1024), bf16), vm((128, 2048), bf16),
        vm((8, 16, 1024), bf16), vm((8, 16, 2048), bf16), vm((16, 2048), f32),
        vm((4, 128, 128), f32), vm((16, 32, 128), f32), vm((16, 32, 128), bf16), vm((16, 32, 128), bf16),
        vm((128, 128), f32), vm((8, 16, 128), bf16), vm((8, 16, 128), bf16),
        vm((256, 128), f32), vm((16, 16, 128), bf16), vm((16, 16, 128), bf16), vm((2, 512, 128), f32),
        vm((1024, 128), f32), vm((16, 64, 128), bf16), vm((16, 64, 128), bf16), vm((64, 128), bf16),
        vm((8, 64, 128), bf16), vm((64, 128), bf16), vm((16, 64, 128), bf16), vm((16, 128, 128), bf16),
        vm((16, 8, 128), f32), vm((16, 8, 128), f32), vm((8, 128), f32), vm((8, 8, 128), f32), vm((8, 128), f32),
        vm((16, 8, 128), f32),
        sem(8), pltpu.SemaphoreType.DMA, sem(24), sem(24), sem(4), sem(8), sem(8), sem(8),
    ]
    pd, ag, pg, wo = pl.pallas_call(
        kernel,
        out_shape=(
            jax.ShapeDtypeStruct((4, 512, 128), bf16),
            jax.ShapeDtypeStruct((1, 512, 256), bf16),
            jax.ShapeDtypeStruct((64, 256), f32),
            jax.ShapeDtypeStruct((1024, 128), f32),
        ),
        in_specs=[pl.BlockSpec(memory_space=pltpu.HBM)] * 8,
        out_specs=(pl.BlockSpec(memory_space=pltpu.HBM),) * 4,
        scratch_shapes=scratch,
        compiler_params=pltpu.CompilerParams(
            collective_id=0, has_side_effects=True, vmem_limit_bytes=48 * 1024 * 1024
        ),
    )(
        *[
            pltpu.with_memory_space_constraint(v, pltpu.HBM)
            for v in (
                msa,
                stretch.reshape(1, 256),
                shift.reshape(1, 256),
                wlr.T,
                offs.reshape(1, 64),
                wf,
                fbias.reshape(1, 128),
                adj,
            )
        ]
    )
    pd, ag, pg, wo = pl.pallas_call(
        emit,
        out_shape=tuple(jax.ShapeDtypeStruct(v.shape, v.dtype) for v in (pd, ag, pg, wo)),
        in_specs=[pl.BlockSpec(memory_space=pl.ANY)] * 4,
        out_specs=(pl.BlockSpec(memory_space=pltpu.HBM),) * 4,
        scratch_shapes=[sem(7)],
        compiler_params=pltpu.CompilerParams(vmem_limit_bytes=16 * 1024 * 1024),
    )(pd, ag, pg, wo)
    return pd, ag, pg.T, wo


def solution(mesh):
    placed = (P("dap", "crop", None), P(), P(), P(), P(), P(), P(), P("dap", "crop", None))
    return jax.shard_map(
        shards,
        mesh=mesh,
        in_specs=placed,
        out_specs=(
            P("dap", "crop", None),
            P("dap", "crop", None),
            P("crop", None),
            P("crop", None),
        ),
        check_vma=False,
    )
```

```python
import math

import jax
import jax.numpy as jnp
from jax import lax
from jax.experimental import pallas as pl
from jax.experimental.pallas import tpu as pltpu
from jax.sharding import PartitionSpec as P

EPSILON = 1e-05
MESH = pl.DeviceIdType.MESH
f32 = jnp.float32
bf16 = jnp.bfloat16

NX, NZ, NM = 4, 8, 16
CH = 32
ROWS = 128
RES = 512
PLANE_STEPS = [(dy, dx, dc) for dx in (2, 1, 3, 0) for dy in (1, 0) for dc in (1, 0) if dy or dx or dc]
FAR = (4, 3, 5)
NEAR = (2, 6, 1, 7)


def dot(a, b):
    return jnp.dot(a, b, preferred_element_type=f32)


def dot_nt(a, b):
    return lax.dot_general(a, b, (((1,), (1,)), ((), ())), preferred_element_type=f32)


def loop(low, high, body):
    def step(k, carry):
        body(k)
        return carry

    lax.fori_loop(low, high, step, 0)


class Exchange:
    def __init__(self, each, device, mine, src, dst, whole, ssem, rsem, apart=False):
        self.each, self.device, self.mine, self.src, self.dst, self.whole = each, device, mine, src, dst, whole
        self.ssem, self.rsem, self.apart = ssem, rsem, apart
        self.waited = False

    def copy(self, p, slot):
        return pltpu.make_async_remote_copy(
            src_ref=self.src(p),
            dst_ref=self.dst(slot),
            send_sem=self.ssem.at[0],
            recv_sem=self.rsem.at[slot if self.apart else 0],
            device_id={"dap": self.device(p)},
            device_id_type=MESH,
        )

    def bulk(self):
        return pltpu.make_async_remote_copy(
            src_ref=self.whole,
            dst_ref=self.whole,
            send_sem=self.ssem.at[0],
            recv_sem=self.rsem.at[0],
            device_id={"dap": self.device(0)},
            device_id_type=MESH,
        )

    def start_one(self, p):
        self.copy(p, self.mine).start()

    def recv_one(self, p):
        self.copy(p, p).wait_recv()

    def start(self):
        self.each(self.start_one)

    def recv(self):
        self.waited = True
        if self.apart:
            self.each(self.recv_one)
        else:
            self.bulk().wait_recv()

    def sent(self):
        self.bulk().wait_send()


def kernel(
    msa_h, stretch_h, shift_h, wlrt_h, offs_h, wf_h, fbias_h, adj_h,
    pd_h, ag_h, pg_h, wo_h,
    pd_out, ag_out, pg_out, wo_out,
    msa, stretch, shift, wlrt_v, offs, wf, fbias, adj,
    scaled, inv, nf, nb, np_, wl4t, wrt, rt,
    sb, rb, rbf, las, la, laf, lbf, lb, lbr, lbrf, rs, lmat, lt, rmat, amat, wff, w2, w2t,
    gmat, xmat, rgs, rgr, rgo, ryq, ryr, rz, rzf, rzn, rsum, lacc, lgp, lgs, lgr, lzf, lzs, lzr, bsf, bs, br, ng,
    wpart, wsend, wrecv, wzs, wzr, wfin, wall_v, pdb,
    psend, precv, pzs, pzr, pgs, pgr,
    in_sem, adj_sem, ssems, rsems, adj_r, zr_r, yf_r, ry_r,
):
    me = lax.axis_index("dap")
    core = lax.rem(me, 2)
    x = lax.rem(me // 2, NX)
    z = lax.rem(me // 8, NZ)
    y = me // 64
    m = y * 8 + x * 2 + core
    other = 1 - core

    def plane_dev(mm):
        return (mm // 8) * 64 + z * 8 + lax.rem(mm, 8)

    def z_dev(zz):
        return y * 64 + zz * 8 + x * 2 + core

    def x_dev(xx):
        return y * 64 + z * 8 + xx * 2 + core

    def core_dev(_):
        return y * 64 + z * 8 + x * 2 + other

    def y_dev(_):
        return (1 - y) * 64 + z * 8 + x * 2 + core

    def planes(body):
        for dy, dx, dc in PLANE_STEPS:
            body((1 - y if dy else y) * 8 + lax.rem(x + dx, NX) * 2 + (other if dc else core))

    def zs(body):
        for k in (4, 3, 5, 2, 6, 1, 7):
            body(lax.rem(z + k, NZ))

    def zs_far(body):
        for k in FAR:
            body(lax.rem(z + k, NZ))

    def far_step(zz):
        return lax.rem(zz - z + NZ, NZ) - min(FAR)

    def zs_near(body):
        for k in NEAR:
            body(lax.rem(z + k, NZ))

    def xs(body):
        for k in (2, 1, 3):
            body(lax.rem(x + k, NX))

    exchanges = []

    def exchange(each, device, mine, src, dst, whole, rsem=None):
        k = pl.ds(len(exchanges), 1)
        e = Exchange(
            each, device, mine, src, dst, whole, ssems.at[k], rsems.at[k] if rsem is None else rsem, rsem is not None
        )
        exchanges.append(e)
        return e

    def finish():
        for e in exchanges:
            if not e.waited:
                e.recv()
        for e in exchanges:
            e.sent()

    small = [
        pltpu.make_async_copy(src, dst, in_sem.at[k])
        for k, (src, dst) in enumerate(
            [
                (msa_h, msa), (stretch_h, stretch), (shift_h, shift), (wlrt_h, wlrt_v), (offs_h, offs),
                (wf_h, wf), (fbias_h, fbias), (adj_h, adj),
            ]
        )
    ]
    for c in small:
        c.start()

    def adj_part(xx):
        return adj.at[:, pl.ds(pl.multiple_of(xx * 128, 128), 128), :]

    def own_i(xx):
        return amat.at[pl.ds(xx * 4, 4)]


    barrier = pltpu.get_barrier_semaphore()
    planes(lambda mm: pl.semaphore_signal(barrier, inc=1, device_id={"dap": plane_dev(mm)}, device_id_type=MESH))
    zs(lambda zz: pl.semaphore_signal(barrier, inc=1, device_id={"dap": z_dev(zz)}, device_id_type=MESH))
    for c in small:
        c.wait()

    def norm_rows(k):
        rows = pl.ds(pl.multiple_of(k * 64, 64), 64)
        v = msa[0, rows, :].astype(f32)
        c = v - jnp.mean(v, axis=-1, keepdims=True)
        iv = lax.rsqrt(jnp.mean(c * c, axis=-1, keepdims=True) + EPSILON)
        sc = c * iv
        scaled[rows, :] = sc
        inv[rows, :] = jnp.broadcast_to(iv, (64, 128))
        n = (sc * stretch[...] + shift[...]).astype(bf16)
        nb[rows, :] = n
        n = n.astype(f32)
        nf[0, rows, :] = n[:, :128]
        nf[1, rows, :] = n[:, 128:]

    loop(0, 8, norm_rows)
    for r in range(4):
        for zz in range(NZ):
            v = [
                jnp.concatenate([nf[h, pl.ds(yy * 256 + zz * 32 + r, 8, stride=4), :] for h in range(2)], axis=1)
                for yy in range(2)
            ]
            np_[pl.ds(r * 128 + zz * 16, 16), :] = jnp.concatenate(v, axis=0).astype(bf16)

    wlrt = wlrt_v[...]
    w_rows = wlrt.astype(f32).T.astype(bf16)
    wrt[...] = wlrt[CH:, :]
    spread = lax.broadcasted_iota(jnp.int32, (64, 128), 0) == (lax.broadcasted_iota(jnp.int32, (64, 128), 1) & 31)
    wl4 = dot(w_rows, spread.astype(f32).astype(bf16))
    wl4t[...] = wl4.T.astype(bf16)
    diag = lax.broadcasted_iota(jnp.int32, (64, 64), 0) == lax.broadcasted_iota(jnp.int32, (64, 64), 1)
    offs_col = jnp.sum(jnp.where(diag, jnp.broadcast_to(offs[...], (64, 64)), 0.0), axis=1, keepdims=True)
    offs4 = jnp.sum(jnp.where(spread, jnp.broadcast_to(offs_col, (64, 128)), 0.0), axis=0, keepdims=True)
    lane_r = lax.broadcasted_iota(jnp.int32, (256, 128), 1) >> 5
    left = jnp.zeros((128, 128), f32)
    for r in range(4):
        left = left + dot(np_[pl.ds(r * 128, 128), :], jnp.where(lane_r == r, wl4, 0.0).astype(bf16))
    left = (left + offs4).astype(bf16).astype(f32) * (1.0 / ROWS)
    las[...] = left.astype(bf16).reshape(NZ, NM, 128)
    rt[...] = (dot_nt(wlrt[CH:, :], nb[...]) + offs_col[CH:, :]).astype(bf16)
    for mm in range(NM):
        xx, cc = (mm % 8) // 2, mm % 2
        sb[mm] = rt[pl.ds(cc * 16, 16), pl.ds(xx * 128, 128)]

    pl.semaphore_wait(barrier, NM - 1 + NZ - 1)

    first = exchange(planes, plane_dev, m, lambda mm: sb.at[mm], lambda mm: rb.at[mm], rb.at[pl.ds(0, NM - 1)])
    first.start()
    rb[m] = sb[m]
    zleft = exchange(zs, z_dev, z, lambda zz: las.at[zz], lambda zz: la.at[zz], la.at[pl.ds(0, NZ - 1)])
    zleft.start()
    la[z] = las[z]
    adjoint = exchange(xs, x_dev, x, adj_part, own_i, amat.at[pl.ds(0, 12)], adj_r)
    adjoint.start()
    own_adj = pltpu.make_async_copy(adj_part(x), own_i(x), adj_sem)
    own_adj.start()

    wff[...] = wf[...].astype(f32)
    for d in range(CH):
        w2[pl.ds(d * 32, 32), :] = wff[pl.ds(d, 32, stride=32), :].astype(bf16)
    for k in range(8):
        w2t[:, pl.ds(k * 128, 128)] = w2[pl.ds(k * 128, 128), :].astype(f32).T.astype(bf16)

    first.recv()

    rbf[...] = rb[...].reshape(256, 128).astype(f32)
    for d in range(16):
        rs[:, pl.ds(d * 128, 128)] = rbf[pl.ds(d, 16, stride=16), :].astype(bf16)

    def zrows(zz):
        return pl.ds(pl.multiple_of(zz * 16, 16), 16)

    def half(cc):
        return pl.ds(pl.multiple_of(cc * 2048, 2048), 2048)

    def quarter(cc, yy):
        return pl.ds(pl.multiple_of(cc * 2048 + yy * 1024, 1024), 1024)

    def r_piece(zz, yy):
        return rmat.at[zrows(zz), quarter(core, yy)]

    rs_own = rs.at[:, pl.ds(pl.multiple_of(y * 1024, 1024), 1024)]
    zfar = exchange(
        zs_far, z_dev, z, lambda zz: rs_own, lambda zz: r_piece(zz, y), rmat.at[pl.ds(0, 16 * len(FAR)), quarter(0, 0)], zr_r
    )
    znear = exchange(
        zs_near, z_dev, z, lambda zz: rs, lambda zz: rmat.at[zrows(zz), half(core)], rmat.at[pl.ds(0, 16 * len(NEAR)), half(0)], zr_r
    )
    zfar.start()
    znear.start()
    rmat[zrows(z), half(core)] = rs[...]

    zleft.recv()
    laf[...] = la[...].reshape(128, 128).astype(f32)
    for mm in range(0, NM, 2):
        for cc in range(2):
            yc, xx = (mm // 8) * 2 + cc, (mm % 8) // 2
            lbf[pl.ds(yc * 32 + xx * 8, 8), :] = laf[pl.ds(mm + cc, 8, stride=16), :]
    lb[...] = lbf[...].astype(bf16).reshape(4, 32, 128)
    lplane = exchange(
        planes,
        plane_dev,
        m,
        lambda mm: lb.at[(mm // 8) * 2 + lax.rem(mm, 2)],
        lambda mm: lbr.at[mm],
        lbr.at[pl.ds(0, NM - 1)],
    )
    lplane.start()
    lbr[m] = lb[y * 2 + core]

    yswap = exchange(
        zs_far, y_dev, None, lambda zz: r_piece(zz, y), None, rmat.at[pl.ds(0, 16 * len(FAR)), quarter(0, 0)], yf_r
    )
    swap = exchange(None, core_dev, None, None, None, rmat.at[:, half(other)])

    def to_core(piece):
        pltpu.make_async_remote_copy(
            src_ref=piece,
            dst_ref=piece,
            send_sem=swap.ssem.at[0],
            recv_sem=swap.rsem.at[0],
            device_id={"dap": core_dev(0)},
            device_id_type=MESH,
        ).start()

    def y_copy(zz, yy):
        return pltpu.make_async_remote_copy(
            src_ref=r_piece(zz, yy),
            dst_ref=r_piece(zz, yy),
            send_sem=yswap.ssem.at[0],
            recv_sem=yf_r.at[far_step(zz)],
            device_id={"dap": y_dev(0)},
            device_id_type=MESH,
        )

    yswap.recv_one = lambda zz: y_copy(zz, 1 - y).wait_recv()

    def forward(k):
        zz = lax.rem(z + k, NZ)
        if k in FAR:
            zfar.recv_one(zz)
            y_copy(zz, y).start()
            to_core(r_piece(zz, y))
        else:
            znear.recv_one(zz)
            to_core(rmat.at[zrows(zz), half(core)])

    def forward_y(k):
        zz = lax.rem(z + k, NZ)
        yswap.recv_one(zz)
        to_core(r_piece(zz, 1 - y))

    to_core(rmat.at[zrows(z), half(core)])
    zfar.waited = True
    znear.waited = True
    yswap.waited = True

    def grad_pair(t):
        a2 = amat[pl.ds(t * 2, 2)].reshape(256, 128)
        for q in range(4):
            g = dot_nt(w2[pl.ds(q * 256, 256), :], a2)
            for e in range(8):
                for u in range(2):
                    rows = pl.ds(pl.multiple_of((2 * t + u) * 32, 32), 32)
                    gmat[rows, pl.ds((q * 8 + e) * 128, 128)] = g[e * 32 : e * 32 + 32, u * 128 : u * 128 + 128].astype(
                        bf16
                    )

    own_adj.wait()
    loop(x * 2, x * 2 + 2, grad_pair)
    adjoint.waited = True
    for k in (1, 3, 2):
        xx = lax.rem(x + k, NX)
        adjoint.recv_one(xx)
        loop(xx * 2, xx * 2 + 2, grad_pair)

    def left_part(cc, yy):
        cols = quarter(cc, yy)
        t = dot_nt(rmat[:, cols], gmat[:, cols])
        for xx in range(NX):
            lacc[xx] += t[:, xx * 128 : xx * 128 + 128]

    lplane.recv()
    lbrf[...] = lbr[...].reshape(512, 128).astype(f32)
    for zz in range(NZ):
        for xx in range(NX):
            lmat[pl.ds(zz * 16, 16), pl.ds(xx * 128, 128)] = lbrf[pl.ds(xx * 8 + zz, 16, stride=32), :].astype(bf16)
    for k in range(4):
        lt[pl.ds(k * 128, 128), :] = lmat[:, pl.ds(k * 128, 128)].astype(f32).T.astype(bf16)

    def columns(ref, yy):
        return ref.at[:, pl.ds(pl.multiple_of(yy * 1024, 1024), 1024)]

    def right_other(yy):
        def part(k):
            cols = pl.ds(pl.multiple_of(other * 2048 + yy * 1024 + k * 512, 512), 512)
            rgs[:, pl.ds(pl.multiple_of(yy * 1024 + k * 512, 512), 512)] = dot(lmat[...], gmat[:, cols]).astype(bf16)

        loop(0, 2, part)

    def right_own(yy):
        def part(k):
            cols = pl.ds(pl.multiple_of(core * 2048 + yy * 1024 + k * 512, 512), 512)
            rgo[:, pl.ds(pl.multiple_of(yy * 1024 + k * 512, 512), 512)] = dot(lmat[...], gmat[:, cols])

        loop(0, 2, part)

    add = [
        exchange(
            lambda body: body(0),
            core_dev,
            0,
            lambda _, yy=yy: columns(rgs, yy),
            lambda _, yy=yy: columns(rgr, yy),
            columns(rgr, yy),
        )
        for yy in (1 - y, y)
    ]
    right_other(1 - y)
    add[0].start()
    right_other(y)
    add[1].start()
    for k in FAR:
        forward(k)
    right_own(1 - y)
    right_own(y)
    add[0].recv()

    ry = exchange(
        zs_far, y_dev, None, lambda zz: ryq.at[zrows(zz), :], None, ryr.at[pl.ds(0, 16 * len(FAR)), :], ry_r
    )
    ry.copy = lambda zz, _: pltpu.make_async_remote_copy(
        src_ref=ryq.at[zrows(zz), :],
        dst_ref=ryr.at[zrows(zz), :],
        send_sem=ry.ssem.at[0],
        recv_sem=ry_r.at[far_step(zz)],
        device_id={"dap": y_dev(0)},
        device_id_type=MESH,
    )
    theirs = pl.ds(pl.multiple_of((1 - y) * 1024, 1024), 1024)
    mine = pl.ds(pl.multiple_of(y * 1024, 1024), 1024)
    for k in FAR:
        rows = zrows(lax.rem(z + k, NZ))
        ryq[rows, :] = (rgo[rows, theirs] + rgr[rows, theirs].astype(f32)).astype(bf16)
        ry.start_one(lax.rem(z + k, NZ))
    bfar = exchange(
        zs_far, z_dev, z, lambda zz: rz.at[zrows(zz), mine], lambda zz: rzf.at[zz], rzf.at[pl.ds(0, len(FAR))]
    )
    bnear = exchange(
        zs_near, z_dev, z, lambda zz: rz.at[zrows(zz), :], lambda zz: rzn.at[zz], rzn.at[pl.ds(0, len(NEAR))]
    )
    add[1].recv()
    for k in NEAR:
        rows = zrows(lax.rem(z + k, NZ))
        rz[rows, :] = (rgo[rows, :] + rgr[rows, :].astype(f32)).astype(bf16)
        bnear.start_one(lax.rem(z + k, NZ))
    for k in NEAR:
        forward(k)
    for k in FAR:
        forward_y(k)
    lacc[...] = jnp.zeros((NX, 128, 128), f32)
    left_part(core, y)
    left_part(core, 1 - y)

    ry.waited = True

    def right_rows(k):
        zz = lax.rem(z + k, NZ)
        rows = zrows(zz)
        ry.recv_one(zz)
        rz[rows, mine] = (rgo[rows, mine] + rgr[rows, mine].astype(f32) + ryr[rows, :].astype(f32)).astype(bf16)
        bfar.start_one(zz)

    for k in FAR[:3]:
        right_rows(k)
    swap.recv()
    left_part(other, y)
    left_part(other, 1 - y)
    for xx in range(NX):
        for mm in range(NM):
            lgp[mm, pl.ds(xx * 8, 8), :] = lacc[xx, pl.ds(mm, 8, stride=16), :]
    lgs[...] = (lgp[...] * (1.0 / ROWS)).astype(bf16)
    bleft = exchange(planes, plane_dev, m, lambda mm: lgs.at[mm], lambda mm: lgr.at[mm], lgr.at[pl.ds(0, NM - 1)])
    bleft.start()
    lgr[m] = lgs[m]

    def outer_part(n):
        o = dot(lt[...], rmat[:, pl.ds(pl.multiple_of(n * 256, 256), 256)])
        for i in range(16):
            for e in range(2):
                rows = pl.ds(pl.multiple_of((2 * n + e) * 32, 32), 32)
                xmat[rows, pl.ds(i * 128, 128)] = o[i * 32 : i * 32 + 32, e * 128 : e * 128 + 128].astype(bf16)

    for n, ks in enumerate([FAR[3:4], FAR[4:], (), ()]):
        for k in ks:
            right_rows(k)
        loop(n * 4, n * 4 + 4, outer_part)

    def w_part(n):
        rows = pl.ds(pl.multiple_of(n * 256, 256), 256)
        wpart[rows, :] = dot(xmat[rows, :], amat[...].reshape(2048, 128))

    loop(0, 2, w_part)

    bleft.recv()
    for yc in range(4):
        t = None
        for xx in range(NX):
            v = lgr[(yc // 2) * 8 + xx * 2 + yc % 2].astype(f32)
            t = v if t is None else t + v
        for xx in range(NX):
            lzf[pl.ds((yc // 2) * 8 + xx * 2 + yc % 2, 8, stride=16), :] = t[xx * 8 : xx * 8 + 8, :]
    lzs[...] = lzf[...].astype(bf16).reshape(NZ, NM, 128)
    bzl = exchange(zs, z_dev, z, lambda zz: lzs.at[zz], lambda zz: lzr.at[zz], lzr.at[pl.ds(0, NZ - 1)])
    bzl.start()
    lzr[z] = lzs[z]

    bnear.recv()
    bfar.recv()
    rows = zrows(z)
    t = rgo[rows, :] + rgr[rows, :].astype(f32)
    for k in NEAR:
        t = t + rzn[lax.rem(z + k, NZ)].astype(f32)
    rsum[...] = t
    t = rsum[:, mine]
    for k in FAR:
        t = t + rzf[lax.rem(z + k, NZ)].astype(f32)
    rsum[:, mine] = t
    for d in range(16):
        bsf[pl.ds(d, 16, stride=16), :] = rsum[:, pl.ds(d * 128, 128)]
    bs[...] = bsf[...].astype(bf16).reshape(NM, 16, 128)
    back = exchange(planes, plane_dev, m, lambda mm: bs.at[mm], lambda mm: br.at[mm], br.at[pl.ds(0, NM - 1)])
    back.start()
    br[m] = bs[m]

    loop(2, 4, w_part)
    for c in range(CH):
        wsend[c // 2, pl.ds((c % 2) * 32, 32), :] = wpart[pl.ds(c, 32, stride=32), :].astype(bf16)
    wplane = exchange(planes, plane_dev, m, lambda mm: wsend.at[mm], lambda mm: wrecv.at[mm], wrecv.at[pl.ds(0, NM - 1)])
    wplane.start()
    wrecv[m] = wsend[m]


    def delta_pair(t):
        p = dot(w2t[...], xmat[:, pl.ds(pl.multiple_of(t * 256, 256), 256)])
        pdb[pl.ds(t * 2, 2)] = (p.T + fbias[...]).astype(bf16).reshape(2, 128, 128)

    loop(0, 4, delta_pair)

    back.recv()
    bzl.recv()
    lg = lzr[...].reshape(128, 128).astype(f32)
    rparts = []
    for cc in range(2):
        row = [br[xx * 2 + cc].astype(f32) + br[8 + xx * 2 + cc].astype(f32) for xx in range(NX)]
        rparts.append(jnp.concatenate(row, axis=1))
    rg = jnp.concatenate(rparts, axis=0)
    lgb = lg.astype(bf16)
    lgt = lgb.astype(f32).T
    lcat = jnp.concatenate([lgt[r * 32 : r * 32 + 32, :] for r in range(4)], axis=1).astype(bf16)
    rgb = rg.astype(bf16)
    pleft = dot(lcat, np_[...])
    pright = dot(rgb, nb[...])
    for h in range(2):
        cols = slice(h * 128, h * 128 + 128)
        for k in range(4):
            psend[h * 8 + k] = pleft[k * 8 : k * 8 + 8, cols]
            psend[h * 8 + 4 + k] = pright[k * 8 : k * 8 + 8, cols]
    pplane = exchange(planes, plane_dev, m, lambda mm: psend.at[mm], lambda mm: precv.at[mm], precv.at[pl.ds(0, NM - 1)])
    pplane.start()
    precv[m] = psend[m]

    loop(4, 8, delta_pair)

    def out_part(xx):
        return pd_out.at[:, pl.ds(pl.multiple_of(xx * 128, 128), 128), :]

    delta = exchange(xs, x_dev, x, lambda xx: pdb.at[pl.ds(xx * 4, 4)], out_part, pd_out.at[:, pl.ds(0, 384), :])
    delta.start()
    pd_out[:, pl.ds(pl.multiple_of(x * 128, 128), 128), :] = pdb[pl.ds(x * 4, 4)]

    wplane.recv()
    t = wrecv[0].astype(f32)
    for mm in range(1, NM):
        t = t + wrecv[mm].astype(f32)
    wzs[...] = t.astype(bf16)
    wz = exchange(zs, z_dev, z, lambda zz: wzs, lambda zz: wzr.at[zz], wzr.at[pl.ds(0, NZ - 1)])
    wz.start()
    wzr[z] = wzs[...]

    row_r = lax.broadcasted_iota(jnp.int32, (128, 256), 0) >> 5
    for r in range(4):
        v = dot(lgb, jnp.where(row_r == r, wl4t[...].astype(f32), 0.0).astype(bf16))
        for g in range(16):
            for h in range(2):
                ng[h, pl.ds((g % 2) * 256 + (g // 2) * 32 + r, 8, stride=4), :] = v[
                    g * 8 : g * 8 + 8, h * 128 : h * 128 + 128
                ]
    nr = dot(rgb.astype(f32).T.astype(bf16), wrt[...])
    ng[0] = ng[0] + nr[:, :128]
    ng[1] = ng[1] + nr[:, 128:]

    pplane.recv()
    t = precv[0]
    for mm in range(1, NM):
        t = t + precv[mm]
    pzs[...] = t
    pz = exchange(zs, z_dev, z, lambda zz: pzs, lambda zz: pzr.at[zz], pzr.at[pl.ds(0, NZ - 1)])
    pz.start()
    pzr[z] = t


    def back_rows(k):
        rows = pl.ds(pl.multiple_of(k * 64, 64), 64)
        hid = jnp.concatenate([ng[0, rows, :], ng[1, rows, :]], axis=1) * stretch[...]
        sc = scaled[rows, :]
        iv = inv[rows, :][:, :1]
        g = iv * (
            hid - jnp.mean(hid, axis=-1, keepdims=True) - sc * jnp.mean(hid * sc, axis=-1, keepdims=True)
        )
        ag_out[0, rows, :] = g.astype(bf16)

    loop(0, 8, back_rows)
    ag_copy = pltpu.make_async_copy(ag_out, ag_h, in_sem.at[0])
    ag_copy.start()

    wz.recv()
    t = wzr[0].astype(f32)
    for zz in range(1, NZ):
        t = t + wzr[zz].astype(f32)
    wfin[...] = (t * (math.sqrt(ROWS) / RES)).astype(bf16)
    wall = exchange(
        planes, plane_dev, m, lambda mm: wfin, lambda mm: wall_v.at[mm], wall_v.at[pl.ds(0, NM - 1)]
    )
    wall.start()
    wall_v[m] = wfin[...]

    pz.recv()
    t = pzr[0]
    for zz in range(1, NZ):
        t = t + pzr[zz]
    t = t * (1.0 / RES)
    pgs[...] = t
    pall = exchange(planes, plane_dev, m, lambda mm: pgs, lambda mm: pgr.at[mm], pgr.at[pl.ds(0, NM - 1)])
    pall.start()
    pgr[m] = t

    wall.recv()
    wo_out[...] = wall_v[...].reshape(1024, 128).astype(f32)
    wo_copy = pltpu.make_async_copy(wo_out, wo_h, in_sem.at[2])
    wo_copy.start()
    delta.recv()
    pd_copy = pltpu.make_async_copy(pd_out, pd_h, in_sem.at[1])
    pd_copy.start()
    pall.recv()
    pt = pgr[...].reshape(2, 64, 128)
    pg_out[:, pl.ds(0, 128)] = pt[0]
    pg_out[:, pl.ds(128, 128)] = pt[1]
    pg_copy = pltpu.make_async_copy(pg_out, pg_h, in_sem.at[3])
    pg_copy.start()
    finish()
    for c in (ag_copy, pd_copy, wo_copy, pg_copy):
        c.wait()


def emit(pd, ag, pg, wo, pd_o, ag_o, pg_o, wo_o, sems):
    copies = [(pd.at[k], pd_o.at[k]) for k in range(4)] + [(ag, ag_o), (pg, pg_o), (wo, wo_o)]
    copies = [pltpu.make_async_copy(src, dst, sems.at[k]) for k, (src, dst) in enumerate(copies)]
    for c in copies:
        c.start()
    for c in copies:
        c.wait()


def shards(msa, stretch, shift, wlr, offs, wf, fbias, adj):
    def vm(shape, dtype):
        return pltpu.VMEM(shape, dtype)

    def sem(*n):
        return pltpu.SemaphoreType.DMA(n)

    scratch = [
        vm((4, 512, 128), bf16), vm((1, 512, 256), bf16), vm((64, 256), f32), vm((1024, 128), f32),
        vm((1, 512, 256), bf16), vm((1, 256), f32), vm((1, 256), f32), vm((64, 256), bf16), vm((1, 64), f32),
        vm((1024, 128), bf16), vm((1, 128), f32), vm((4, 512, 128), bf16),
        vm((512, 256), f32), vm((512, 128), f32), vm((2, 512, 128), f32), vm((512, 256), bf16), vm((512, 256), bf16),
        vm((128, 256), bf16), vm((32, 256), bf16), vm((32, 512), bf16),
        vm((16, 16, 128), bf16), vm((16, 16, 128), bf16), vm((256, 128), f32), vm((8, 16, 128), bf16),
        vm((8, 16, 128), bf16), vm((128, 128), f32), vm((128, 128), f32), vm((4, 32, 128), bf16), vm((16, 32, 128), bf16),
        vm((512, 128), f32),
        vm((16, 2048), bf16), vm((128, 512), bf16), vm((512, 128), bf16), vm((128, 4096), bf16),
        vm((16, 128, 128), bf16), vm((1024, 128), f32), vm((1024, 128), bf16), vm((128, 1024), bf16),
        vm((512, 4096), bf16), vm((1024, 2048), bf16), vm((128, 2048), bf16), vm((128, 2048), bf16),
        vm((128, 2048), f32), vm((128, 1024), bf16), vm((128, 1024), bf16), vm((128, 2048), bf16),
        vm((8, 16, 1024), bf16), vm((8, 16, 2048), bf16), vm((16, 2048), f32),
        vm((4, 128, 128), f32), vm((16, 32, 128), f32), vm((16, 32, 128), bf16), vm((16, 32, 128), bf16),
        vm((128, 128), f32), vm((8, 16, 128), bf16), vm((8, 16, 128), bf16),
        vm((256, 128), f32), vm((16, 16, 128), bf16), vm((16, 16, 128), bf16), vm((2, 512, 128), f32),
        vm((1024, 128), f32), vm((16, 64, 128), bf16), vm((16, 64, 128), bf16), vm((64, 128), bf16),
        vm((8, 64, 128), bf16), vm((64, 128), bf16), vm((16, 64, 128), bf16), vm((16, 128, 128), bf16),
        vm((16, 8, 128), f32), vm((16, 8, 128), f32), vm((8, 128), f32), vm((8, 8, 128), f32), vm((8, 128), f32),
        vm((16, 8, 128), f32),
        sem(8), pltpu.SemaphoreType.DMA, sem(23), sem(23), sem(4), sem(8), sem(3), sem(3),
    ]
    pd, ag, pg, wo = pl.pallas_call(
        kernel,
        out_shape=(
            jax.ShapeDtypeStruct((4, 512, 128), bf16),
            jax.ShapeDtypeStruct((1, 512, 256), bf16),
            jax.ShapeDtypeStruct((64, 256), f32),
            jax.ShapeDtypeStruct((1024, 128), f32),
        ),
        in_specs=[pl.BlockSpec(memory_space=pltpu.HBM)] * 8,
        out_specs=(pl.BlockSpec(memory_space=pltpu.HBM),) * 4,
        scratch_shapes=scratch,
        compiler_params=pltpu.CompilerParams(
            collective_id=0, has_side_effects=True, vmem_limit_bytes=48 * 1024 * 1024
        ),
    )(
        *[
            pltpu.with_memory_space_constraint(v, pltpu.HBM)
            for v in (
                msa,
                stretch.reshape(1, 256),
                shift.reshape(1, 256),
                wlr.T,
                offs.reshape(1, 64),
                wf,
                fbias.reshape(1, 128),
                adj,
            )
        ]
    )
    pd, ag, pg, wo = pl.pallas_call(
        emit,
        out_shape=tuple(jax.ShapeDtypeStruct(v.shape, v.dtype) for v in (pd, ag, pg, wo)),
        in_specs=[pl.BlockSpec(memory_space=pl.ANY)] * 4,
        out_specs=(pl.BlockSpec(memory_space=pltpu.HBM),) * 4,
        scratch_shapes=[sem(7)],
        compiler_params=pltpu.CompilerParams(vmem_limit_bytes=16 * 1024 * 1024),
    )(pd, ag, pg, wo)
    return pd, ag, pg.T, wo


def solution(mesh):
    placed = (P("dap", "crop", None), P(), P(), P(), P(), P(), P(), P("dap", "crop", None))
    return jax.shard_map(
        shards,
        mesh=mesh,
        in_specs=placed,
        out_specs=(
            P("dap", "crop", None),
            P("dap", "crop", None),
            P("crop", None),
            P("crop", None),
        ),
        check_vma=False,
    )
```
